32 devices in a mesh: dp: 8 (over z, x), tensor: 4 (over y, core).
Axes of the slice: x: 2, y: 2, z: 4, core: 2. Of those that a mesh axis runs over, the one named last changes fastest.
Arguments:
- tokens: bfloat16 [16384, 1024], P(('dp', 'tensor')), may hold values from -6 to 6
- mix_gain: bfloat16 [1024], P('dp'), may hold values from 0.5 to 1.5
- rnn_weight: bfloat16 [1024, 1536], P('dp', 'tensor'), may hold values from -0.1875 to 0.1875
- gelu_weight: bfloat16 [1024, 1536], P('dp', 'tensor'), may hold values from -0.1875 to 0.1875
- conv_weight: bfloat16 [4, 1536], P(None, ('tensor', 'dp')), may hold values from -3 to 3
- conv_bias: bfloat16 [1536], P(('tensor', 'dp')), may hold values from -1.5 to 1.5
- recur_weight: bfloat16 [12, 128, 128], P('tensor', 'dp'), may hold values from -0.5 to 0.5
- input_weight: bfloat16 [12, 128, 128], P('tensor', 'dp'), may hold values from -0.5 to 0.5
- recur_bias: bfloat16 [1536], P(('tensor', 'dp')), may hold values from -2.5 to 2.5
- input_bias: bfloat16 [1536], P(('tensor', 'dp')), may hold values from -2.5 to 2.5
- decay_param: bfloat16 [1536], P(('tensor', 'dp')), may hold values from -9 to 0
- out_weight: bfloat16 [1536, 1024], P('tensor', 'dp'), may hold values from -0.15625 to 0.15625
- mlp_gain: bfloat16 [1024], P('dp'), may hold values from 0.5 to 1.5
- gate_weight: bfloat16 [1024, 3072], P('dp', 'tensor'), may hold values from -0.1875 to 0.1875
- up_weight: bfloat16 [1024, 3072], P('dp', 'tensor'), may hold values from -0.1875 to 0.1875
- down_weight: bfloat16 [3072, 1024], P('tensor', 'dp'), may hold values from -0.109375 to 0.109375
- cotangent: bfloat16 [16384, 1024], P(('dp', 'tensor')), may hold values from -6 to 6
Outputs:
- block_out: bfloat16 [16384, 1024], P(('dp', 'tensor'))
- grad_tokens: float32 [16384, 1024], P(('dp', 'tensor'))
- grad_mix_gain: float32 [1024], P('dp')
- grad_rnn_weight: float32 [1024, 1536], P('dp', 'tensor')
- grad_gelu_weight: float32 [1024, 1536], P('dp', 'tensor')
- grad_conv_weight: float32 [4, 1536], P(None, ('tensor', 'dp'))
- grad_conv_bias: float32 [1536], P(('tensor', 'dp'))
- grad_recur_weight: float32 [12, 128, 128], P('tensor', 'dp')
- grad_input_weight: float32 [12, 128, 128], P('tensor', 'dp')
- grad_recur_bias: float32 [1536], P(('tensor', 'dp'))
- grad_input_bias: float32 [1536], P(('tensor', 'dp'))
- grad_decay_param: float32 [1536], P(('tensor', 'dp'))
- grad_out_weight: float32 [1536, 1024], P('tensor', 'dp')
- grad_mlp_gain: float32 [1024], P('dp')
- grad_gate_weight: float32 [1024, 3072], P('dp', 'tensor')
- grad_up_weight: float32 [1024, 3072], P('dp', 'tensor')
- grad_down_weight: float32 [3072, 1024], P('tensor', 'dp')
The draws below stay inside these ranges and needn't reach their ends.
All inputs are finite; a program needn't handle non-finite values.
Results may differ from the reference program's by a relative error of at most 0.012.
Values may be sent and summed in bfloat16 or wider, within the bound.
A program may use at most 192 MiB of HBM per device.

```python
import jax
import jax.numpy as jnp
from jax import lax

D = 1024
R = 1536
FF = 3072
CONV_W = 4
HB = 128
SEQ_LEN = 1024
SEQ_DEV = 2
HEADS = 12
TOKENS = 16384
N_DP = 8


def level_of(key, shape, cuts, low, largest):
    loudness = 1.0
    for dim, blocks in cuts:
        heights = jax.random.uniform(jax.random.fold_in(jax.random.fold_in(key, 6), dim), (blocks,), jnp.float32, low / len(cuts), largest / len(cuts))
        loudness = loudness * jnp.repeat(jnp.exp(heights), shape[dim] // blocks).reshape((-1,) + (1,) * (len(shape) - 1 - dim))
    return loudness


def scatter_about(rng, extent, deviation, limit, shards=(), dtype=jnp.bfloat16):
    array = deviation * jax.random.normal(rng, extent, jnp.float32)
    if shards:
        array = array * level_of(rng, extent, shards, -0.22, 0.18)
    return jnp.clip(array, -limit, limit).astype(dtype)


def setup_inputs(seed: int = 0) -> dict:
    streams_of = jax.random.split(jax.random.key(seed), 18)
    return {
        "tokens": scatter_about(streams_of[0], (TOKENS, D), 1.0, 6.0, ((0, 32),)),
        "mix_gain": jnp.clip(1.0 + 0.1 * jax.random.normal(streams_of[1], (D,), jnp.float32), 0.5, 1.5).astype(jnp.bfloat16),
        "rnn_weight": scatter_about(streams_of[2], (D, R), D ** -0.5, 0.1875, ((0, 8), (1, 4))),
        "gelu_weight": scatter_about(streams_of[3], (D, R), D ** -0.5, 0.1875, ((0, 8), (1, 4))),
        "conv_weight": scatter_about(streams_of[4], (CONV_W, R), CONV_W ** -0.5, 3.0, ((1, 32),)),
        "conv_bias": scatter_about(streams_of[5], (R,), 0.3, 1.5, ((0, 32),)),
        "recur_weight": scatter_about(streams_of[6], (HEADS, HB, HB), HB ** -0.5, 0.5, ((0, 4), (1, 8))),
        "input_weight": scatter_about(streams_of[7], (HEADS, HB, HB), HB ** -0.5, 0.5, ((0, 4), (1, 8))),
        "recur_bias": scatter_about(streams_of[8], (R,), 0.5, 2.5, ((0, 32),)),
        "input_bias": scatter_about(streams_of[9], (R,), 0.5, 2.5, ((0, 32),)),
        "decay_param": jnp.clip(-9.0 + 9.0 * jax.random.uniform(streams_of[10], (R,), jnp.float32) ** level_of(streams_of[10], (R,), ((0, 32),), -0.2, 0.2), -9.0, 0.0).astype(jnp.bfloat16),
        "out_weight": scatter_about(streams_of[11], (R, D), R ** -0.5, 0.15625, ((0, 4), (1, 8))),
        "mlp_gain": jnp.clip(1.0 + 0.1 * jax.random.normal(streams_of[12], (D,), jnp.float32), 0.5, 1.5).astype(jnp.bfloat16),
        "gate_weight": scatter_about(streams_of[13], (D, FF), D ** -0.5, 0.1875, ((0, 8), (1, 4))),
        "up_weight": scatter_about(streams_of[14], (D, FF), D ** -0.5, 0.1875, ((0, 8), (1, 4))),
        "down_weight": scatter_about(streams_of[15], (FF, D), FF ** -0.5, 0.109375, ((0, 4), (1, 8))),
        "cotangent": scatter_about(streams_of[16], (TOKENS, D), 1.0, 6.0, ((0, 32),)),
    }


@jax.custom_vjp
def low(v):
    return lax.optimization_barrier(v.astype(jnp.bfloat16)).astype(jnp.float32)

@jax.custom_vjp
def low_back(v):
    return v

def low_keep(v):
    return (low(v), None)

def low_pass(kept, grad):
    return (grad,)

def back_keep(v):
    return (v, None)

def back_low(kept, grad):
    return (low(grad),)
low.defvjp(low_keep, low_pass)
low_back.defvjp(back_keep, back_low)
EPS = 1e-06
GUARD = 0.01
DECAY_SCALE = 8.0

def rms_scale(values, gain):
    return values * lax.rsqrt(lax.optimization_barrier(jnp.mean(values * values, axis=-1, keepdims=True)) + EPS) * gain

def causal_conv(signal, weight, bias):
    width = weight.shape[0]
    length = signal.shape[1]
    padded = jnp.pad(signal, ((0, 0), (width - 1, 0), (0, 0)))
    total = jnp.zeros_like(signal) + bias
    for offset in range(width):
        total = total + weight[offset] * padded[:, width - 1 - offset:width - 1 - offset + length]
    return total

def combine(earlier, later):
    return (earlier[0] * later[0], later[0] * earlier[1] + later[1])

def lru_mix(recur_lin, input_lin, conv_out, branch_lin, decay_param, recur_bias, input_bias):
    recur = jax.nn.sigmoid(recur_lin + recur_bias)
    inward = jax.nn.sigmoid(input_lin + input_bias)
    decay = jnp.exp(-DECAY_SCALE * jax.nn.softplus(decay_param) * recur)
    driven = jnp.sqrt(1.0 - decay * decay + GUARD) * inward * conv_out
    decays_out, state = lax.associative_scan(combine, (decay, driven), axis=1)
    return state * jax.nn.gelu(branch_lin, approximate=True)

def hdot(left, right):
    return jnp.dot(left, right, precision=lax.Precision.HIGHEST)

def forward(rows, mix_gain, rnn_weight, gelu_weight, conv_weight, conv_bias, recur_weight, input_weight, recur_bias, input_bias, decay_param, out_weight, mlp_gain, gate_weight, up_weight, down_weight):
    seqs = rows.shape[0] // SEQ_LEN
    normed = low(rms_scale(rows, mix_gain))
    rnn_in = low_back(hdot(normed, rnn_weight))
    branch_in = low_back(hdot(normed, gelu_weight))
    conv_out = low(causal_conv(rnn_in.reshape(seqs, SEQ_LEN, R), conv_weight, conv_bias))
    conv_heads = conv_out.reshape(seqs * SEQ_LEN, HEADS, HB)
    recur_in = low_back(jnp.einsum('gkc,kcd->gkd', conv_heads, recur_weight, precision=lax.Precision.HIGHEST))
    input_in = low_back(jnp.einsum('gkc,kcd->gkd', conv_heads, input_weight, precision=lax.Precision.HIGHEST))
    lru_out = low(lru_mix(recur_in.reshape(seqs, SEQ_LEN, R), input_in.reshape(seqs, SEQ_LEN, R), conv_out, branch_in.reshape(seqs, SEQ_LEN, R), decay_param, recur_bias, input_bias))
    branch = low_back(hdot(lru_out.reshape(seqs * SEQ_LEN, R), out_weight))
    mixed = rows + branch
    normed_mlp = low(rms_scale(mixed, mlp_gain))
    gate_in = low_back(hdot(normed_mlp, gate_weight))
    up_in = low_back(hdot(normed_mlp, up_weight))
    hidden = low(jax.nn.gelu(gate_in, approximate=True) * up_in)
    return mixed + hdot(hidden, down_weight)

def reference(tokens, mix_gain, rnn_weight, gelu_weight, conv_weight, conv_bias, recur_weight, input_weight, recur_bias, input_bias, decay_param, out_weight, mlp_gain, gate_weight, up_weight, down_weight, cotangent):
    params = tuple((p.astype(jnp.float32) for p in (mix_gain, rnn_weight, gelu_weight, conv_weight, conv_bias, recur_weight, input_weight, recur_bias, input_bias, decay_param, out_weight, mlp_gain, gate_weight, up_weight, down_weight)))
    group = SEQ_DEV * SEQ_LEN
    blocks = tokens.astype(jnp.float32).reshape(N_DP, group, D)
    cot_blocks = cotangent.astype(jnp.float32).reshape(N_DP, group, D)

    def one_block(carry, inputs):
        rows, cot_rows = inputs
        result, back = jax.vjp(forward, rows, *params)
        grads = back(cot_rows)
        summed = tuple((total + grad for total, grad in zip(carry, grads[1:])))
        return (summed, (result, grads[0]))
    start = tuple((jnp.zeros_like(p) for p in params))
    totals, (results, grad_rows) = lax.scan(one_block, start, (blocks, cot_blocks))
    block_out = results.reshape(TOKENS, D).astype(jnp.bfloat16)
    grad_tokens = grad_rows.reshape(TOKENS, D)
    return (block_out, grad_tokens, totals[0], totals[1], totals[2], totals[3], totals[4], totals[5], totals[6], totals[7], totals[8], totals[9], totals[10], totals[11], totals[12], totals[13], totals[14])
```

```python
import functools

import jax
import jax.numpy as jnp
from jax import lax
from jax.experimental import pallas as pl
from jax.experimental.pallas import tpu as pltpu
from jax.sharding import PartitionSpec as P

SEQ = 1024
EPS = 1e-06
GUARD = 0.01
DECAY_SCALE = 8.0
GELU_K = 0.7978845608028654
GELU_C = 0.044715
BF = jnp.bfloat16
F32 = jnp.float32
MESH = pl.DeviceIdType.MESH
VMEM_LIMIT = 63 * 1024 * 1024

RNN, GEL, OUT, GA0, UP0, GA1, UP1, DN0, DN1 = range(9)
UNITS = 9
GATE, UP, DOWN = (GA0, GA1), (UP0, UP1), (DN0, DN1)
FLOW = {RNN: "zxy", GEL: "zyx", OUT: "yxz", GA0: "zxy", UP0: "zyx", GA1: "zxy", UP1: "zyx", DN0: "zxy", DN1: "zyx"}
SMALL = 48


def nn(a, b):
    return jnp.dot(a, b, preferred_element_type=F32)


def nt(a, b):
    return lax.dot_general(a, b, (((1,), (1,)), ((), ())), preferred_element_type=F32)


def gelu_parts(v):
    v2 = v * v
    th = jnp.tanh(GELU_K * v * (1.0 + GELU_C * v2))
    half = 0.5 * (1.0 + th)
    return v * half, half + (0.5 * GELU_K) * v * (1.0 - th * th) * (1.0 + (3.0 * GELU_C) * v2)


class Net:
    def __init__(self, z_size, x_size, y_size):
        self.size = {"z": z_size, "x": x_size, "y": y_size, "c": 2}
        dp, t = lax.axis_index("dp"), lax.axis_index("tensor")
        self.at = {"z": dp // x_size, "x": lax.rem(dp, x_size), "y": t // 2, "c": lax.rem(t, 2)}
        self.off = {"z": 0, "x": z_size - 1, "y": z_size + x_size - 2}

    def shifted(self, d, j):
        n = self.size[d]
        return lax.rem(self.at[d] + (j % n), n)

    def device(self, d, j):
        at = dict(self.at)
        at[d] = self.shifted(d, j)
        return (at["z"] * self.size["x"] + at["x"], at["y"] * 2 + at["c"])

    def barrier(self):
        sem = pltpu.get_barrier_semaphore()
        count = 0
        for d in "zxyc":
            for j in range(1, self.size[d]):
                pl.semaphore_signal(sem, inc=1, device_id=self.device(d, j), device_id_type=MESH)
                count += 1
        pl.semaphore_wait(sem, count)


class Gather:
    def __init__(self, net, ref, flows, ss, rs):
        self.net, self.ref, self.flows, self.ss, self.rs = net, ref, flows, ss, rs

    def region(self, u, s, at):
        order = self.flows[u]
        idx = [slice(None) if d in order[:s] else at[d] for d in "yzx"]
        return self.ref.at[(u, *idx)]

    def copy(self, u, s, j, sender):
        d = self.flows[u][s]
        at = dict(self.net.at)
        if sender:
            at[d] = self.net.shifted(d, -j)
        region = self.region(u, s, at)
        k = self.net.off[d] + j - 1
        return pltpu.make_async_remote_copy(
            src_ref=region, dst_ref=region, send_sem=self.ss.at[u, k], recv_sem=self.rs.at[u, k],
            device_id=self.net.device(d, j), device_id_type=MESH)

    def hops(self, u, s):
        return range(1, self.net.size[self.flows[u][s]])

    def start(self, u, s):
        for j in self.hops(u, s):
            self.copy(u, s, j, False).start()

    def wait(self, u, s):
        for j in self.hops(u, s):
            self.copy(u, s, j, True).wait_recv()

    def step(self, u, s):
        self.wait(u, s)
        if s < 2:
            self.start(u, s + 1)

    def drain(self, u):
        for s in range(3):
            for j in self.hops(u, s):
                self.copy(u, s, j, False).wait_send()


def pair_copy(net, src, dst, ss, rs, k):
    return pltpu.make_async_remote_copy(
        src_ref=src, dst_ref=dst, send_sem=ss.at[k], recv_sem=rs.at[k],
        device_id=net.device("c", 1), device_id_type=MESH)


def scan_forward(a, b, carry):
    rows, cols = a.shape
    a = a.reshape(rows // 8, 8, cols)
    b = b.reshape(rows // 8, 8, cols)
    place = lax.broadcasted_iota(jnp.int32, (rows // 8, 8, cols), 1)
    for k in (1, 2, 4):
        keep = place >= k
        b = b + a * jnp.where(keep, pltpu.roll(b, k, 1), 0.0)
        a = a * jnp.where(keep, pltpu.roll(a, k, 1), 1.0)
    out = []
    for g in range(rows // 8):
        s = b[g] + a[g] * carry
        out.append(s)
        carry = s[7:8]
    return jnp.concatenate(out, axis=0), carry


def scan_backward(a, b, carry):
    rows, cols = a.shape
    a = a.reshape(rows // 8, 8, cols)
    b = b.reshape(rows // 8, 8, cols)
    place = lax.broadcasted_iota(jnp.int32, (rows // 8, 8, cols), 1)
    for k in (1, 2, 4):
        keep = place < 8 - k
        b = b + a * jnp.where(keep, pltpu.roll(b, 8 - k, 1), 0.0)
        a = a * jnp.where(keep, pltpu.roll(a, 8 - k, 1), 1.0)
    out = []
    for g in reversed(range(rows // 8)):
        s = b[g] + a[g] * carry
        out.append(s)
        carry = s[0:1]
    return jnp.concatenate(out[::-1], axis=0), carry


def rows_of(i, n):
    return pl.ds(pl.multiple_of(i * n, n), n)


def join_params(gs, prm, gains, sizes):
    y_size = sizes[2]
    for yy in range(y_size):
        prm[yy] = jnp.sum(gs[0, yy, :, :, 32:48, :].astype(F32), axis=(0, 1))
    d = gains.shape[1]
    for n in range(2):
        row = jnp.concatenate([prm[0, 8 + 3 * n + k : 9 + 3 * n + k, :] for k in range(3)], axis=1)
        gains[n : n + 1, :] = row[:, :d]


def head_weight(gs, yy, first, group):
    blocks = gs[0, yy, :, :, first : first + 16, :]
    z, x, r, c = blocks.shape
    if group > 1:
        blocks = jnp.sum(blocks.astype(F32).reshape(z * x // group, group, r, c), axis=1).astype(BF)
    return blocks.reshape(-1, c)


def transpose_into(dst, src, n, step=256):
    @pl.loop(0, n // step)
    def _(i):
        dst[:, rows_of(i, step)] = src[rows_of(i, step), :].T


def forward_kernel(sizes, group,
                   tok, cot, wp, sp,
                   o_w, o_cot, o_cott, o_n1t, o_n2t, o_c6, o_cf, o_a, o_ri, o_lru, o_cv, o_mix, prm, gains, hw,
                   W, gs, T1, SA, SB, N1, RI, A, CV, C6, LRU, PS, PR, MIX,
                   ss, rs, sss, srs, ps, pr, ls, outs):
    net = Net(*sizes)
    y_size = sizes[2]
    c = net.at["c"]
    half = SEQ // 2
    ch = W.shape[-1]
    depth = T1.shape[1]
    own, other = pl.ds(pl.multiple_of(c * half, half), half), pl.ds(pl.multiple_of((1 - c) * half, half), half)
    mine = (net.at["y"], net.at["z"], net.at["x"])

    place = [
        pltpu.make_async_copy(sp, gs.at[(0, *mine)], ls.at[0]),
        pltpu.make_async_copy(wp, W.at[(slice(None), *mine)], ls.at[1]),
        pltpu.make_async_copy(tok, T1.at[own], ls.at[2]),
        pltpu.make_async_copy(cot, SA.at[own], ls.at[3]),
    ]
    for cp in place:
        cp.start()
    net.barrier()

    big = Gather(net, W, FLOW, ss, rs)
    small = Gather(net, gs, {0: "zxy"}, sss, srs)
    tok_copy = pair_copy(net, tok, T1.at[own], ps, pr, 0)
    cot_copy = pair_copy(net, cot, SA.at[own], ps, pr, 1)
    tok_in = pair_copy(net, tok, T1.at[other], ps, pr, 0)
    cot_in = pair_copy(net, cot, SA.at[other], ps, pr, 1)

    place[0].wait()
    small.start(0, 0)
    tok_copy.start()
    cot_copy.start()
    place[1].wait()
    big.start(RNN, 0)
    big.start(GEL, 0)
    big.start(OUT, 0)
    place[2].wait()
    place[3].wait()
    small.step(0, 0)
    small.step(0, 1)
    tok_in.wait_recv()
    cot_in.wait_recv()
    out_copies = []

    def send_out(src, dst):
        cp = pltpu.make_async_copy(src, dst, outs.at[len(out_copies)])
        cp.start()
        out_copies.append([cp, True])
        return len(out_copies) - 1

    def sent(k):
        if out_copies[k][1]:
            out_copies[k][0].wait()
            out_copies[k][1] = False

    k_cot = send_out(SA, o_cot)
    transpose_into(SB, SA, SEQ)
    k_cott = send_out(SB, o_cott)
    big.step(RNN, 0)
    small.wait(0, 2)
    join_params(gs, prm, gains, sizes)
    for yy in range(y_size):
        for n in range(2):
            hw[n, :, yy * ch : (yy + 1) * ch] = head_weight(gs, yy, 16 * n, group)
    big.start(GA0, 0)
    big.step(GEL, 0)

    @pl.loop(0, SEQ // 128)
    def _(i):
        v = T1[rows_of(i, 128), :].astype(F32)
        s = lax.rsqrt(jnp.mean(v * v, axis=1, keepdims=True) + EPS)
        N1[rows_of(i, 128), :] = (v * s * gains[0:1, :]).astype(BF)

    sent(k_cott)
    transpose_into(SB, N1, SEQ)
    k_n1t = send_out(SB, o_n1t)
    RI[0:8, :] = jnp.zeros((8, y_size * ch), F32)
    big.start(UP0, 0)
    big.step(RNN, 1)
    big.step(GEL, 1)
    big.step(OUT, 0)
    big.step(GA0, 0)
    big.wait(RNN, 2)

    def full(u):
        return jnp.concatenate([W[u, yy].reshape(depth, ch) for yy in range(y_size)], axis=1)

    w_out = {}

    def unit_out(u):
        w_out[u] = send_out(W.at[u], o_w.at[u])

    unit_out(RNN)

    @pl.loop(0, SEQ // 512)
    def _(i):
        RI[pl.ds(pl.multiple_of(i * 512 + 8, 8), 512), :] = nn(N1[rows_of(i, 512), :], full(RNN))

    send_out(RI, o_ri)
    big.start(GA1, 0)
    big.step(OUT, 1)
    big.step(UP0, 0)
    big.wait(GEL, 2)
    unit_out(GEL)

    T = 128

    def branch_tile(i, carries):
        hooks = {
            1: [lambda: big.step(GA0, 1)],
            2: [lambda: big.start(UP1, 0)],
            3: [lambda: big.step(UP0, 1), lambda: big.step(GA1, 0)],
            5: [lambda: big.wait(OUT, 2), lambda: big.start(DN0, 0)],
            6: [lambda: big.step(UP1, 0)],
        }
        for tile, fns in hooks.items():
            @pl.when(i == tile)
            def _():
                for fn in fns:
                    fn()
        rows = rows_of(i, T)
        br = nn(N1[rows, :], full(GEL))
        new = []
        for yy in range(y_size):
            cols = slice(yy * ch, (yy + 1) * ch)
            p = prm[yy]
            x = RI[pl.ds(pl.multiple_of(i * T, T), T + 8), cols]
            cv = p[4:5] + p[0:1] * x[8:]
            for k in range(1, 4):
                cv = cv + p[k : k + 1] * pltpu.roll(x, k, 0)[8:]
            cv_low = cv.astype(BF)
            CV[rows, cols] = cv_low
            cv = cv_low.astype(F32)
            rec, inp = [], []
            for h in range(ch // 128):
                hc = slice(yy * ch + h * 128, yy * ch + (h + 1) * 128)
                both = nn(cv_low[:, h * 128 : (h + 1) * 128], jnp.concatenate([hw[0, :, hc], hw[1, :, hc]], axis=1))
                rec.append(both[:, :128])
                inp.append(both[:, 128:])
            r = jax.nn.sigmoid(jnp.concatenate(rec, axis=1) + p[5:6])
            w = jax.nn.sigmoid(jnp.concatenate(inp, axis=1) + p[6:7])
            soft = jnp.log1p(jnp.exp(-jnp.abs(p[7:8]))) + jnp.maximum(p[7:8], 0.0)
            a = jnp.exp((-DECAY_SCALE * soft) * r)
            u = 1.0 - a * a + GUARD
            inv = lax.rsqrt(u)
            root = u * inv
            wc = w * cv
            state, last = scan_forward(a, root * wc, carries[yy])
            first = lax.broadcasted_iota(jnp.int32, (T, ch), 0) == 0
            prev = jnp.where(first, carries[yy], pltpu.roll(state, 1, 0))
            new.append(last)
            g, gp = gelu_parts(br[:, cols])
            LRU[rows, cols] = (state * g).astype(BF)
            cp = (prev - a * wc * inv) * a * r * (-DECAY_SCALE)
            A[rows, cols] = a
            C6[0, rows, cols] = g.astype(BF)
            C6[1, rows, cols] = (state * gp).astype(BF)
            C6[2, rows, cols] = cp.astype(BF)
            C6[3, rows, cols] = (cp * soft * (1.0 - r)).astype(BF)
            C6[4, rows, cols] = (root * wc * (1.0 - w)).astype(BF)
            C6[5, rows, cols] = (root * w).astype(BF)
        return tuple(new)

    lax.fori_loop(0, SEQ // T, branch_tile, tuple(jnp.zeros((1, ch), F32) for _ in range(y_size)))
    unit_out(OUT)
    k_cf = send_out(C6, o_cf)
    send_out(A, o_a)
    send_out(LRU, o_lru)
    send_out(CV, o_cv)

    def out_rows(rows):
        return nt(LRU[rows, :], full(OUT))

    PS[...] = out_rows(other)
    sent(k_cot)
    sent(k_n1t)
    mix_copy = pair_copy(net, PS, PR, ps, pr, 2)
    mix_copy.start()
    MIX[...] = out_rows(own)
    big.wait(GA0, 2)
    unit_out(GA0)
    big.start(DN1, 0)
    big.step(GA1, 1)
    mix_copy.wait_recv()

    @pl.loop(0, half // 128)
    def _(i):
        rows = rows_of(i, 128)
        v = tok[rows, :].astype(F32) + MIX[rows, :] + PR[rows, :]
        MIX[rows, :] = v
        s = lax.rsqrt(jnp.mean(v * v, axis=1, keepdims=True) + EPS)
        SA[pl.ds(pl.multiple_of(c * half + i * 128, 128), 128), :] = (v * s * gains[1:2, :]).astype(BF)

    n2_copy = pair_copy(net, SA.at[own], SA.at[own], ps, pr, 3)
    n2_in = pair_copy(net, SA.at[other], SA.at[other], ps, pr, 3)
    n2_copy.start()
    send_out(MIX, o_mix)
    big.step(DN0, 0)
    big.wait(UP0, 2)
    unit_out(UP0)
    n2_in.wait_recv()
    transpose_into(SB, SA, SEQ)
    send_out(SB, o_n2t)
    sent(k_cf)
    F = 256

    def ff(j):
        @pl.loop(0, SEQ // F)
        def _(i):
            rows = rows_of(i, F)
            up = nn(SA[rows, :], full(UP[j]))
            g, gp = gelu_parts(nn(SA[rows, :], full(GATE[j])))
            C6[j, rows, :] = (g * up).astype(BF)
            C6[2 + j, rows, :] = (gp * up).astype(BF)
            C6[4 + j, rows, :] = g.astype(BF)

    ff(0)
    big.step(UP1, 1)
    big.step(DN1, 0)
    big.wait(GA1, 2)
    unit_out(GA1)
    big.step(DN0, 1)
    big.wait(UP1, 2)
    unit_out(UP1)
    big.step(DN1, 1)
    ff(1)
    send_out(C6, o_c6)
    big.wait(DN0, 2)
    unit_out(DN0)
    big.wait(DN1, 2)
    unit_out(DN1)
    for u in range(UNITS):
        big.drain(u)
    small.drain(0)
    for cp in (tok_copy, cot_copy, mix_copy, n2_copy):
        cp.wait_send()
    for k in range(len(out_copies)):
        sent(k)


class Scatter:
    def __init__(self, net, ref, slots, flows, bufs, index, ss, rs, credit):
        self.net, self.ref, self.slots, self.flows = net, ref, slots, flows
        self.bufs, self.index, self.ss, self.rs, self.credit = bufs, index, ss, rs, credit

    def lands(self, u, s, j):
        buf = self.bufs[self.flows[u], s]
        return buf.at[self.index[u] % buf.shape[0], j - 1]

    def copy(self, u, s, j):
        order = self.flows[u]
        d = order[s]
        at = dict(self.net.at)
        at[d] = self.net.shifted(d, j)
        idx = [at[e] if e in order[: s + 1] else slice(None) for e in "yzx"]
        k = self.net.off[d] + j - 1
        return pltpu.make_async_remote_copy(
            src_ref=self.ref.at[(self.slots[u], *idx)], dst_ref=self.lands(u, s, j),
            send_sem=self.ss.at[u, k], recv_sem=self.rs.at[u, k],
            device_id=self.net.device(d, j), device_id_type=MESH)

    def hops(self, u, s):
        return range(1, self.net.size[self.flows[u][s]])

    def start(self, u, s):
        ring = self.bufs[self.flows[u], s].shape[0]
        if self.index[u] >= ring:
            pl.semaphore_wait(self.credit[self.flows[u]].at[self.index[u] - ring, s], self.net.size[self.flows[u][s]] - 1)
        for j in self.hops(u, s):
            self.copy(u, s, j).start()

    def add(self, u, s, out=None):
        order = self.flows[u]
        d = order[s]
        for j in self.hops(u, s):
            self.copy(u, s, j).wait_recv()
        rest = [e for e in "yzx" if e not in order[: s + 1]]
        buf = self.bufs[order, s]
        b = self.index[u] % buf.shape[0]

        def block(place):
            idx = [place[e] if e in place else self.net.at[e] for e in "yzx"]
            total = self.ref[(self.slots[u], *idx)].astype(F32)
            for j in self.hops(u, s):
                total = total + buf[(b, j - 1, *[place[e] for e in rest])].astype(F32)
            if out is None:
                self.ref[(self.slots[u], *idx)] = total.astype(BF)
            else:
                out[u] = total

        def over(names, place):
            if not names:
                block(place)
            elif names[0] == "z":
                @pl.loop(0, self.net.size["z"])
                def _(z):
                    over(names[1:], {**place, "z": z})
            else:
                for n in range(self.net.size[names[0]]):
                    over(names[1:], {**place, names[0]: n})

        over(rest, {})
        ring = buf.shape[0]
        if (self.flows[u], self.index[u] + ring) in [(self.flows[v], self.index[v]) for v in self.flows]:
            for j in self.hops(u, s):
                pl.semaphore_signal(self.credit[order].at[self.index[u], s], inc=1,
                                    device_id=self.net.device(d, -j), device_id_type=MESH)

    def step(self, u, s, out=None):
        self.add(u, s, out if s == 2 else None)
        if s < 2:
            self.start(u, s + 1)

    def drain(self, u):
        for s in range(3):
            for j in self.hops(u, s):
                self.copy(u, s, j).wait_send()


BACK = {DN0: "yxz", GA0: "yxz", UP0: "yxz", RNN: "yxz", DN1: "xyz", GA1: "xyz", UP1: "xyz", GEL: "xyz", OUT: "zxy"}
SLOT = {DN0: 9, DN1: 10, GA0: DN0, GA1: DN1, UP0: GA0, UP1: GA1, OUT: UP0, GEL: UP1, RNN: OUT}
INDEX = {DN0: 0, DN1: 0, GA0: 1, GA1: 1, UP0: 2, UP1: 2, RNN: 3, GEL: 3, OUT: 0}


def backward_kernel(sizes, group,
                    w_h, cot_h, cott_h, n1t_h, n2t_h, c6_h, cf_h, a_h, ri_h, lru_h, cv_h, mix_h, tok_h, prm, gains, hw,
                    o_block, o_gtok, o_gw, o_gs,
                    W, C6, COT, TT, NT, GM, PS, PR, LRU, AS, RS, acc, GS, pgain,
                    a0, a1, a2, b0, b1, b2, e0, e1, e2, s0, s1, s2,
                    ss, rs, sss, srs, ca, cb, ps, pr, ls, ast, rst):
    net = Net(*sizes)
    z_size, x_size, y_size = sizes
    c = net.at["c"]
    half = SEQ // 2
    ch = W.shape[-1]
    depth = COT.shape[1]
    own, other = pl.ds(pl.multiple_of(c * half, half), half), pl.ds(pl.multiple_of((1 - c) * half, half), half)
    loads = {}

    def load(name, src, dst):
        loads[name] = pltpu.make_async_copy(src, dst, ls.at[len(loads)])
        loads[name].start()

    def loaded(*names):
        for name in names:
            loads[name].wait()

    load("cott", cott_h, TT)
    load("h", c6_h.at[0:2], C6.at[0:2])
    load("cot", cot_h, COT)
    load("w_dn", w_h.at[DN0:], W.at[DN0:9])
    load("ab", c6_h.at[2:6], C6.at[2:6])
    load("w_ff", w_h.at[GA0:DN0], W.at[GA0:DN0])
    load("n2t", n2t_h, NT)
    load("mix", mix_h, GM)
    load("w_rnn", w_h.at[0:GA0], W.at[0:GA0])
    load("lru", lru_h, LRU)
    load("tok", tok_h, PS.at[1])
    net.barrier()
    bufs = {("yxz", 0): a0, ("yxz", 1): a1, ("yxz", 2): a2, ("xyz", 0): b0, ("xyz", 1): b1, ("xyz", 2): b2,
            ("zxy", 0): e0, ("zxy", 1): e1, ("zxy", 2): e2}
    big = Scatter(net, W, SLOT, BACK, bufs, INDEX, ss, rs, {"yxz": ca, "xyz": cb, "zxy": None})
    small = Scatter(net, GS, {0: 0}, {0: "yxz"}, {("yxz", 0): s0, ("yxz", 1): s1, ("yxz", 2): s2}, {0: 0}, sss, srs, None)

    def step(u, s):
        big.step(u, s, o_gw)

    def full(u):
        return jnp.concatenate([W[u, yy].reshape(depth, ch) for yy in range(y_size)], axis=1)

    zh = z_size // 2

    def weight_grad(u, left, right):
        @pl.loop(0, 2)
        def _(i):
            val = nn(left[rows_of(i, depth // 2), :], right[...]).astype(BF)
            for yy in range(y_size):
                W[SLOT[u], yy, pl.ds(i * zh, zh)] = val[:, yy * ch : (yy + 1) * ch].reshape(
                    zh, x_size, depth // (z_size * x_size), ch)

    loaded("cott", "h")
    weight_grad(DN0, TT, C6.at[0])
    big.start(DN0, 0)
    weight_grad(DN1, TT, C6.at[1])
    big.start(DN1, 0)
    loaded("cot", "w_dn", "ab")
    F = 256
    for j in range(2):
        @pl.loop(0, SEQ // F)
        def _(i):
            rows = rows_of(i, F)
            gh = nn(COT[rows, :], full(DOWN[j]))
            C6[2 + j, rows, :] = (gh * C6[2 + j, rows, :].astype(F32)).astype(BF)
            C6[4 + j, rows, :] = (gh * C6[4 + j, rows, :].astype(F32)).astype(BF)

    loaded("w_ff")

    def mlp_back(base, i):
        rows = pl.ds(pl.multiple_of(base + i * F, F), F)
        return (nt(C6[2, rows, :], full(GA0)) + nt(C6[3, rows, :], full(GA1))
                + nt(C6[4, rows, :], full(UP0)) + nt(C6[5, rows, :], full(UP1)))

    def mlp_out(base, i):
        rows = pl.ds(pl.multiple_of(base + i * F, F), F)
        return nt(C6[0, rows, :], full(DN0)) + nt(C6[1, rows, :], full(DN1))

    def partial_rows(fn, base, dst):
        @pl.loop(0, half // F)
        def _(i):
            dst[rows_of(i, F), :] = fn(base, i).astype(dst.dtype)

    base_own, base_other = c * half, (1 - c) * half
    partial_rows(mlp_back, base_other, PS.at[0])
    back_copy = pair_copy(net, PS.at[0], PR.at[0], ps, pr, 0)
    back_copy.start()
    partial_rows(mlp_back, base_own, o_gtok)
    loaded("mix", "n2t", "tok")
    acc[...] = jnp.zeros_like(acc)
    pgain[...] = jnp.zeros_like(pgain)
    step(DN0, 0)
    step(DN1, 0)
    back_copy.wait_recv()
    T = 128

    @pl.loop(0, half // T)
    def _(i):
        rows = rows_of(i, T)
        at = pl.ds(pl.multiple_of(base_own + i * T, T), T)
        v = GM[rows, :]
        gn = o_gtok[rows, :] + PR[0, rows, :].astype(F32)
        s = lax.rsqrt(jnp.mean(v * v, axis=1, keepdims=True) + EPS)
        q = gn * gains[1:2, :]
        pgain[1:2, :] += jnp.sum(gn * v * s, axis=0, keepdims=True)
        gm = COT[at, :].astype(F32) + s * q - (s * s * s) * v * jnp.mean(q * v, axis=1, keepdims=True)
        o_gtok[rows, :] = gm
        COT[at, :] = gm.astype(BF)

    row_copy = pair_copy(net, COT.at[own], COT.at[own], ps, pr, 1)
    row_in = pair_copy(net, COT.at[other], COT.at[other], ps, pr, 1)
    row_copy.start()
    back_copy.wait_send()
    partial_rows(mlp_out, base_other, PS.at[0])
    out_copy = pair_copy(net, PS.at[0], PR.at[1], ps, pr, 2)
    out_copy.start()
    @pl.loop(0, half // F)
    def _(i):
        GM[rows_of(i, F), :] += mlp_out(base_own, i)

    weight_grad(GA0, NT, C6.at[2])
    big.start(GA0, 0)
    weight_grad(GA1, NT, C6.at[3])
    big.start(GA1, 0)
    step(DN0, 1)
    step(DN1, 1)
    row_in.wait_recv()
    loaded("w_rnn", "lru")
    weight_grad(UP0, NT, C6.at[4])
    weight_grad(UP1, NT, C6.at[5])
    load("n1t", n1t_h, NT)
    load("cf", cf_h, C6)
    transpose_into(TT, COT, SEQ)
    weight_grad(OUT, TT, LRU)
    big.start(OUT, 0)
    load("cv", cv_h, LRU)
    out_copy.wait_recv()

    @pl.loop(0, half // F)
    def _(i):
        rows = rows_of(i, F)
        PR[1, rows, :] = (GM[rows, :] + PR[1, rows, :].astype(F32)).astype(BF)

    block_copy = pltpu.make_async_copy(PR.at[1], o_block, ls.at[15])
    block_copy.start()
    tiles = SEQ // T

    def fetch(n, slot):
        at = (tiles - 1 - n) * T
        return (
            pltpu.make_async_copy(a_h.at[pl.ds(pl.multiple_of(at, T), T)], AS.at[slot], ast.at[slot]),
            pltpu.make_async_copy(ri_h.at[pl.ds(pl.multiple_of(at, T), T + 8)], RS.at[slot], rst.at[slot]),
        )

    for cp in fetch(0, 0):
        cp.start()
    loaded("cf")

    def back_tile(n, carries):
        hooks = {
            0: [lambda: step(DN0, 2), lambda: step(DN1, 2)],
            1: [lambda: step(GA0, 0), lambda: big.start(UP0, 0)],
            2: [lambda: step(GA1, 0), lambda: big.start(UP1, 0)],
            4: [lambda: step(GA0, 1)],
            5: [lambda: step(GA1, 1)],
            6: [lambda: step(OUT, 0)],
            7: [lambda: step(GA0, 2), lambda: step(GA1, 2), lambda: step(OUT, 1)],
        }
        for tile, fns in hooks.items():
            @pl.when(n == tile)
            def _():
                for fn in fns:
                    fn()
        slot = lax.rem(n, 2)
        for cp in fetch(n, slot):
            cp.wait()

        @pl.when(n + 1 < tiles)
        def _():
            for cp in fetch(n + 1, 1 - slot):
                cp.start()

        i = tiles - 1 - n
        rows = rows_of(i, T)
        gl_all = nn(COT[rows, :], full(OUT))
        new = []
        for yy in range(y_size):
            adj_next, a_next, gco_next = carries[yy]
            cols = slice(yy * ch, (yy + 1) * ch)
            p = prm[yy]
            gl = gl_all[:, cols]
            at = AS[slot, :, cols]
            last = lax.broadcasted_iota(jnp.int32, (T, ch), 0) == T - 1
            shifted = jnp.where(last, a_next, pltpu.roll(at, T - 1, 0))
            adj, adj_first = scan_backward(shifted, gl * C6[0, rows, cols].astype(F32), adj_next)
            C6[1, rows, cols] = (gl * C6[1, rows, cols].astype(F32)).astype(BF)
            grp = adj * C6[3, rows, cols].astype(F32)
            gip = adj * C6[4, rows, cols].astype(F32)
            gr_low, gi_low = grp.astype(BF), gip.astype(BF)
            gcd = adj * C6[5, rows, cols].astype(F32)
            acc[yy, 5:6] += jnp.sum(grp, axis=0, keepdims=True)
            acc[yy, 6:7] += jnp.sum(gip, axis=0, keepdims=True)
            acc[yy, 7:8] += jnp.sum(adj * C6[2, rows, cols].astype(F32), axis=0, keepdims=True)
            C6[3, rows, cols] = gr_low
            C6[4, rows, cols] = gi_low
            parts = []
            for h in range(ch // 128):
                hs = slice(h * 128, (h + 1) * 128)
                hc = slice(yy * ch + h * 128, yy * ch + (h + 1) * 128)
                parts.append(nt(jnp.concatenate([gr_low[:, hs], gi_low[:, hs]], axis=1),
                                jnp.concatenate([hw[0, :, hc], hw[1, :, hc]], axis=1)))
            gco = gcd + jnp.concatenate(parts, axis=1)
            ext = jnp.concatenate([gco, gco_next], axis=0)
            x = RS[slot, :, cols]
            grn = p[0:1] * gco
            acc[yy, 0:1] += jnp.sum(gco * x[8:], axis=0, keepdims=True)
            acc[yy, 4:5] += jnp.sum(gco, axis=0, keepdims=True)
            for k in range(1, 4):
                grn = grn + p[k : k + 1] * pltpu.roll(ext, T + 8 - k, 0)[:T]
                acc[yy, k : k + 1] += jnp.sum(gco * pltpu.roll(x, k, 0)[8:], axis=0, keepdims=True)
            C6[5, rows, cols] = grn.astype(BF)
            new.append((adj_first, at[0:1], gco[0:8]))
        return tuple(new)

    zero = (jnp.zeros((1, ch), F32), jnp.zeros((1, ch), F32), jnp.zeros((8, ch), F32))
    lax.fori_loop(0, tiles, back_tile, (zero,) * y_size)
    loaded("n1t")
    step(UP0, 0)
    weight_grad(RNN, NT, C6.at[5])
    big.start(RNN, 0)
    step(UP1, 0)
    weight_grad(GEL, NT, C6.at[1])
    big.start(GEL, 0)

    def rnn_back(base, i):
        rows = pl.ds(pl.multiple_of(base + i * F, F), F)
        return nt(C6[5, rows, :], full(RNN)) + nt(C6[1, rows, :], full(GEL))

    out_copy.wait_send()
    partial_rows(rnn_back, base_other, PS.at[0])
    rnn_copy = pair_copy(net, PS.at[0], PR.at[0], ps, pr, 3)
    rnn_copy.start()
    partial_rows(rnn_back, base_own, GM)
    step(UP0, 1)
    step(UP1, 1)
    loaded("cv")
    for yy in range(y_size):
        acc[yy, 7:8] = acc[yy, 7:8] * jax.nn.sigmoid(prm[yy, 7:8])
        for h in range(ch // 128):
            hs = slice(h * 128, (h + 1) * 128)
            hc = slice(yy * ch + h * 128, yy * ch + (h + 1) * 128)
            both = lax.dot_general(LRU[:, hc], jnp.concatenate([C6[3, :, hc], C6[4, :, hc]], axis=1),
                                   (((0,), (0,)), ((), ())), preferred_element_type=F32)
            for n in range(2):
                val = both[:, n * 128 : (n + 1) * 128].astype(BF)
                if group > 1:
                    val = jnp.broadcast_to(val.reshape(-1, 1, 16, 128), (z_size * x_size // group, group, 16, 128))
                GS[0, yy, :, :, 16 * n : 16 * n + 16, hs] = val.reshape(z_size, x_size, 16, 128)
    rnn_copy.wait_recv()

    @pl.loop(0, half // T)
    def _(i):
        rows = rows_of(i, T)
        v = PS[1, rows, :].astype(F32)
        gn = GM[rows, :] + PR[0, rows, :].astype(F32)
        s = lax.rsqrt(jnp.mean(v * v, axis=1, keepdims=True) + EPS)
        q = gn * gains[0:1, :]
        pgain[0:1, :] += jnp.sum(gn * v * s, axis=0, keepdims=True)
        o_gtok[rows, :] += s * q - (s * s * s) * v * jnp.mean(q * v, axis=1, keepdims=True)

    gain_copy = pair_copy(net, pgain.at[0:8], pgain.at[8:16], ps, pr, 4)
    gain_copy.start()
    step(OUT, 2)
    gain_copy.wait_recv()
    for n in range(2):
        row = pgain[n : n + 1, :] + pgain[8 + n : 9 + n, :]
        row = jnp.concatenate([row, jnp.zeros((1, 3 * ch - depth), F32)], axis=1)
        for k in range(3):
            for yy in range(y_size):
                acc[yy, 8 + 3 * n + k : 9 + 3 * n + k, :] = row[:, k * ch : (k + 1) * ch]

    @pl.loop(0, z_size)
    def _(z):
        for yy in range(y_size):
            for xx in range(x_size):
                GS[0, yy, z, xx, 32:48, :] = acc[yy].astype(BF)

    small.start(0, 0)
    step(UP0, 2)
    step(UP1, 2)
    small.step(0, 0)
    step(RNN, 0)
    step(GEL, 0)
    small.step(0, 1)
    step(RNN, 1)
    step(GEL, 1)
    small.step(0, 2, o_gs)
    step(RNN, 2)
    step(GEL, 2)
    for u in range(UNITS):
        big.drain(u)
    small.drain(0)
    for cp in (row_copy, rnn_copy, gain_copy):
        cp.wait_send()
    block_copy.wait()


def params_block(args, dp_index, dp, ch, depth):
    (mix_gain, conv_weight, conv_bias, recur_weight, input_weight, recur_bias, input_bias, decay_param, mlp_gain) = args
    rows8 = jnp.concatenate([conv_weight, conv_bias[None], recur_bias[None], input_bias[None], decay_param[None]], axis=0)
    rows8 = lax.dynamic_update_slice(jnp.zeros((8, ch), BF), rows8, (0, dp_index * rows8.shape[1]))
    gains = jnp.stack([mix_gain, mlp_gain])
    gains = lax.dynamic_update_slice(jnp.zeros((2, 3 * ch), BF), gains, (0, dp_index * gains.shape[1]))
    heads = []
    for w in (recur_weight, input_weight):
        w = jnp.transpose(w, (1, 0, 2)).reshape(w.shape[1], ch)
        if w.shape[0] < 16:
            w = lax.dynamic_update_slice(jnp.zeros((16, ch), BF), w, (lax.rem(dp_index * w.shape[0], 16), 0))
        heads.append(w)
    return jnp.concatenate([*heads, rows8, gains.reshape(6, ch), jnp.zeros((2, ch), BF)], axis=0)


def any_spec():
    return pl.BlockSpec(memory_space=pl.ANY)


def vmem_spec():
    return pl.BlockSpec(memory_space=pltpu.VMEM)


def body(sizes, tokens, mix_gain, rnn_weight, gelu_weight, conv_weight, conv_bias, recur_weight, input_weight,
         recur_bias, input_bias, decay_param, out_weight, mlp_gain, gate_weight, up_weight, down_weight, cotangent):
    z_size, x_size, y_size = sizes
    dp = z_size * x_size
    dp_index = lax.axis_index("dp")
    rows, depth = tokens.shape
    part, ch = rnn_weight.shape
    head_rows = recur_weight.shape[1]
    group = max(1, 16 // head_rows)
    wide = y_size * ch
    wp = jnp.stack([rnn_weight, gelu_weight, out_weight.T, gate_weight[:, :ch], up_weight[:, :ch],
                    gate_weight[:, ch:], up_weight[:, ch:], down_weight[:ch].T, down_weight[ch:].T])
    sp = params_block((mix_gain, conv_weight, conv_bias, recur_weight, input_weight, recur_bias, input_bias,
                       decay_param, mlp_gain), dp_index, dp, ch, depth)
    shape = jax.ShapeDtypeStruct
    grid = (y_size, z_size, x_size)
    hops = z_size + x_size + y_size - 3
    f_out = [
        shape((UNITS, *grid, part, ch), BF), shape((SEQ, depth), BF), shape((depth, SEQ), BF),
        shape((depth, SEQ), BF), shape((depth, SEQ), BF), shape((6, SEQ, wide), BF), shape((6, SEQ, wide), BF),
        shape((SEQ, wide), F32), shape((SEQ + 8, wide), F32), shape((SEQ, wide), BF), shape((SEQ, wide), BF),
        shape((rows, depth), F32), shape((y_size, 16, ch), F32), shape((8, depth), F32), shape((2, 128, wide), BF),
    ]
    dma, sem = pltpu.SemaphoreType.DMA, pltpu.SemaphoreType.REGULAR
    kept = pl.pallas_call(
        functools.partial(forward_kernel, sizes, group),
        out_shape=f_out,
        in_specs=[vmem_spec(), any_spec(), any_spec(), any_spec()],
        out_specs=[any_spec()] * 12 + [vmem_spec()] * 3,
        scratch_shapes=[
            pltpu.VMEM((UNITS, *grid, part, ch), BF), pltpu.VMEM((1, *grid, SMALL, ch), BF),
            pltpu.VMEM((SEQ, depth), BF), pltpu.VMEM((SEQ, depth), BF), pltpu.VMEM((depth, SEQ), BF),
            pltpu.VMEM((SEQ, depth), BF), pltpu.VMEM((SEQ + 8, wide), F32), pltpu.VMEM((SEQ, wide), F32),
            pltpu.VMEM((SEQ, wide), BF), pltpu.VMEM((6, SEQ, wide), BF), pltpu.VMEM((SEQ, wide), BF),
            pltpu.VMEM((rows, depth), F32), pltpu.VMEM((rows, depth), F32), pltpu.VMEM((rows, depth), F32),
            dma((UNITS, hops)), dma((UNITS, hops)), dma((1, hops)), dma((1, hops)), dma((4,)), dma((4,)), dma((4,)),
            dma((24,)),
        ],
        compiler_params=pltpu.CompilerParams(collective_id=0, has_side_effects=True, vmem_limit_bytes=VMEM_LIMIT),
        name="gather_forward",
    )(tokens, cotangent, wp, sp)
    small_shape = (SMALL, ch)
    block_out, grad_tokens, gw, gs = pl.pallas_call(
        functools.partial(backward_kernel, sizes, group),
        out_shape=[shape((rows, depth), BF), shape((rows, depth), F32), shape((UNITS, part, ch), F32),
                   shape((1, SMALL, ch), F32)],
        in_specs=[any_spec()] * 13 + [vmem_spec()] * 3,
        out_specs=[any_spec()] + [vmem_spec()] * 3,
        scratch_shapes=[
            pltpu.VMEM((UNITS + 2, *grid, part, ch), BF), pltpu.VMEM((6, SEQ, wide), BF), pltpu.VMEM((SEQ, depth), BF),
            pltpu.VMEM((depth, SEQ), BF), pltpu.VMEM((depth, SEQ), BF), pltpu.VMEM((rows, depth), F32),
            pltpu.VMEM((2, rows, depth), BF), pltpu.VMEM((2, rows, depth), BF), pltpu.VMEM((SEQ, wide), BF),
            pltpu.VMEM((2, 128, wide), F32), pltpu.VMEM((2, 136, wide), F32), pltpu.VMEM((y_size, 16, ch), F32),
            pltpu.VMEM((1, *grid, SMALL, ch), BF), pltpu.VMEM((16, depth), F32),
            pltpu.VMEM((2, y_size - 1, z_size, x_size, part, ch), BF),
            pltpu.VMEM((2, x_size - 1, z_size, part, ch), BF),
            pltpu.VMEM((4, z_size - 1, part, ch), BF),
            pltpu.VMEM((2, x_size - 1, y_size, z_size, part, ch), BF),
            pltpu.VMEM((2, y_size - 1, z_size, part, ch), BF),
            pltpu.VMEM((4, z_size - 1, part, ch), BF),
            pltpu.VMEM((1, z_size - 1, y_size, x_size, part, ch), BF),
            pltpu.VMEM((1, x_size - 1, y_size, part, ch), BF),
            pltpu.VMEM((1, y_size - 1, part, ch), BF),
            pltpu.VMEM((1, y_size - 1, z_size, x_size, *small_shape), BF),
            pltpu.VMEM((1, x_size - 1, z_size, *small_shape), BF),
            pltpu.VMEM((1, z_size - 1, *small_shape), BF),
            dma((UNITS, hops)), dma((UNITS, hops)), dma((1, hops)), dma((1, hops)),
            sem((2, 2)), sem((2, 2)), dma((5,)), dma((5,)), dma((16,)), dma((2,)), dma((2,)),
        ],
        compiler_params=pltpu.CompilerParams(collective_id=1, has_side_effects=True, vmem_limit_bytes=VMEM_LIMIT),
        name="backward_scatter",
    )(*kept[:12], tokens, *kept[12:])
    gs = gs[0]
    heads = []
    for n in range(2):
        g = gs[16 * n : 16 * n + 16]
        if head_rows < 16:
            g = lax.dynamic_slice(g, (lax.rem(dp_index * head_rows, 16), 0), (head_rows, ch))
        heads.append(jnp.transpose(g.reshape(head_rows, ch // 128, 128), (1, 0, 2)))
    own = ch // dp
    par = lax.dynamic_slice(gs[32:40], (0, dp_index * own), (8, own))
    gains = lax.dynamic_slice(gs[40:46].reshape(2, 3 * ch), (0, dp_index * part), (2, part))
    return (
        block_out, grad_tokens, gains[0], gw[RNN], gw[GEL], par[0:4], par[4], heads[0], heads[1],
        par[5], par[6], par[7], gw[OUT].T, gains[1],
        jnp.concatenate([gw[GA0], gw[GA1]], axis=1), jnp.concatenate([gw[UP0], gw[UP1]], axis=1),
        jnp.concatenate([gw[DN0], gw[DN1]], axis=1).T,
    )


def solution(mesh):
    dp, tensor = mesh.shape["dp"], mesh.shape["tensor"]
    x_size = 2
    sizes = (dp // x_size, x_size, tensor // 2)
    rows, split, vec = P(("dp", "tensor"), None), P("dp", "tensor"), P(("tensor", "dp"))
    head, flip, taps = P("tensor", "dp", None), P("tensor", "dp"), P(None, ("tensor", "dp"))
    return jax.shard_map(
        functools.partial(body, sizes),
        mesh=mesh,
        in_specs=(rows, P("dp"), split, split, taps, vec, head, head, vec, vec, vec, flip, P("dp"), split, split, flip,
                  rows),
        out_specs=(rows, rows, P("dp"), split, split, taps, vec, head, head, vec, vec, vec, flip, P("dp"), split, split,
                   flip),
        check_vma=False,
    )
```

```python
import functools

import jax
import jax.numpy as jnp
from jax import lax
from jax.experimental import pallas as pl
from jax.experimental.pallas import tpu as pltpu
from jax.sharding import PartitionSpec as P

SEQ = 1024
EPS = 1e-06
GUARD = 0.01
DECAY_SCALE = 8.0
GELU_K = 0.7978845608028654
GELU_C = 0.044715
BF = jnp.bfloat16
F32 = jnp.float32
MESH = pl.DeviceIdType.MESH
VMEM_LIMIT = 63 * 1024 * 1024

RNN, GEL, OUT, GA0, UP0, GA1, UP1, DN0, DN1 = range(9)
UNITS = 9
GATE, UP, DOWN = (GA0, GA1), (UP0, UP1), (DN0, DN1)
CHUNKS = 2 * UNITS
SMALL = 48
F_FLOW = (
    "zyx", "zxy", "zyx", "zyx", "zxy", "zyx", "xzy", "zyx", "zyx", "zyx", "xzy", "xzy", "zyx", "zxy", "yzx", "xyz",
    "xzy", "zyx",
)
F_PLAN = (
    0, 4, 8, "pre1", 1, "pre2", 12, 5, "pre3", 16, 2, 9, 20, 6, 13, 24, 10, 17, 28, 3, 25, 32, 21, 36, 7, "rnn", 29,
    40, 14, 11, 22, 18, 26, 41, 44, 30, 33, 48, 37, 52, 15, "br", 19, "br", "br", 42, 23, 45, 56, 27, "br", 49, 60,
    34, "br", 53, 64, 31, "br", 61, 68, 38, "br", 46, "br", 35, 43, 57, 69, "out", 54, "mix", 65, 50, 62, "n2", 58,
    39, "ffa", 47, "ffa", "ffa", 70, 66, "ffa", 51, 55, "ffb", 59, "ffb", "ffb", "ffb", 67, 63, 71,
)
B_FLOW = (
    "yxz", "xyz", "yzx", "xyz", "yxz", "yxz", "yzx", "xyz", "xzy", "xzy", "xyz", "yxz", "yxz", "xyz", "xzy", "yxz",
    "yzx", "xyz",
)
B_PLAN = (
    "d0", 56, 60, "d1", 64, 68, "gh", "gh", "gh", "gh", "gh", "gh", "gh", 57, 61, "gh", "bo", "bw", "ga0", 69, 65,
    24, 28, "ga1", 58, 62, 40, 44, "gno", 70, "gno", "gnw", 66, 29, "gnw", 25, 63, 59, "norm", "up0", 71, 41, 67, 32,
    36, "up1", 45, 48, 52, "outg", 26, 30, 16, 20, "t", 42, 33, "t", 31, "t", 49, 43, 37, "t", "t", 46, "t", 17, 34,
    "t", 53, "t", 27, 21, 38, 35, 50, "gel", 8, 47, 54, 12, 18, 39, "rnn", 51, 0, 4, 22, "gn1o", "gn1w", 55, 9,
    "heads", 19, 13, "fin", 23, "s0", 1, 5, 14, "s1", 10, 2, 11, 6, "s2", 15, 3, "s3", 7,
)


def run_plan(plan, blocks, event):
    i = 0
    while i < len(plan):
        name = plan[i]
        i += 1
        if isinstance(name, int):
            event(name // 4, name % 4)
            continue
        turns, fn = blocks[name]
        if turns == 1:
            fn()
            continue
        hooks = {}
        for turn in range(1, turns):
            hooks[turn] = []
            while isinstance(plan[i], int):
                hooks[turn].append(plan[i])
                i += 1
            i += 1

        def hook(n, hooks=hooks):
            for turn, steps in hooks.items():
                if steps:
                    @pl.when(n == turn)
                    def _(steps=steps):
                        for step in steps:
                            event(step // 4, step % 4)

        fn(hook)


def nn(a, b):
    return jnp.dot(a, b, preferred_element_type=F32)


def nt(a, b):
    return lax.dot_general(a, b, (((1,), (1,)), ((), ())), preferred_element_type=F32)


def gelu_parts(v):
    v2 = v * v
    th = jnp.tanh(GELU_K * v * (1.0 + GELU_C * v2))
    half = 0.5 * (1.0 + th)
    return v * half, half + (0.5 * GELU_K) * v * (1.0 - th * th) * (1.0 + (3.0 * GELU_C) * v2)


class Net:
    def __init__(self, z_size, x_size, y_size):
        self.size = {"z": z_size, "x": x_size, "y": y_size, "c": 2}
        dp, t = lax.axis_index("dp"), lax.axis_index("tensor")
        self.at = {"z": dp // x_size, "x": lax.rem(dp, x_size), "y": t // 2, "c": lax.rem(t, 2)}
        self.off = {"z": 0, "x": z_size - 1, "y": z_size + x_size - 2}

    def shifted(self, d, j):
        n = self.size[d]
        return lax.rem(self.at[d] + (j % n), n)

    def device(self, d, j):
        at = dict(self.at)
        at[d] = self.shifted(d, j)
        return (at["z"] * self.size["x"] + at["x"], at["y"] * 2 + at["c"])

    def barrier(self):
        sem = pltpu.get_barrier_semaphore()
        count = 0
        for d in "zxyc":
            for j in range(1, self.size[d]):
                pl.semaphore_signal(sem, inc=1, device_id=self.device(d, j), device_id_type=MESH)
                count += 1
        pl.semaphore_wait(sem, count)


def chunk_rows(c, part):
    if part % 32:
        return slice(None) if c % 2 == 0 else None
    return slice(c % 2 * (part // 2), (c % 2 + 1) * (part // 2))


class Gather:
    def __init__(self, net, ref, flows, ss, rs, halves):
        self.net, self.ref, self.flows, self.ss, self.rs, self.halves = net, ref, flows, ss, rs, halves

    def region(self, c, s, at):
        order = self.flows[c]
        idx = [slice(None) if d in order[:s] else at[d] for d in "yzx"]
        if not self.halves:
            return self.ref.at[(c, *idx)]
        return self.ref.at[(c // 2, *idx, chunk_rows(c, self.ref.shape[4]))]

    def copy(self, c, s, j, sender):
        d = self.flows[c][s]
        at = dict(self.net.at)
        if sender:
            at[d] = self.net.shifted(d, -j)
        region = self.region(c, s, at)
        k = self.net.off[d] + j - 1
        return pltpu.make_async_remote_copy(
            src_ref=region, dst_ref=region, send_sem=self.ss.at[c, k], recv_sem=self.rs.at[c, k],
            device_id=self.net.device(d, j), device_id_type=MESH)

    def hops(self, c, s):
        return range(1, self.net.size[self.flows[c][s]])

    def event(self, c, k):
        if self.halves and chunk_rows(c, self.ref.shape[4]) is None:
            return
        if k:
            for j in self.hops(c, k - 1):
                self.copy(c, k - 1, j, True).wait_recv()
        if k < 3:
            for j in self.hops(c, k):
                self.copy(c, k, j, False).start()

    def drain(self, c):
        if self.halves and chunk_rows(c, self.ref.shape[4]) is None:
            return
        for s in range(3):
            for j in self.hops(c, s):
                self.copy(c, s, j, False).wait_send()


def pair_copy(net, src, dst, ss, rs, k):
    return pltpu.make_async_remote_copy(
        src_ref=src, dst_ref=dst, send_sem=ss.at[k], recv_sem=rs.at[k],
        device_id=net.device("c", 1), device_id_type=MESH)


def scan_forward(a, b, carry):
    rows, cols = a.shape
    a = a.reshape(rows // 8, 8, cols)
    b = b.reshape(rows // 8, 8, cols)
    place = lax.broadcasted_iota(jnp.int32, (rows // 8, 8, cols), 1)
    for k in (1, 2, 4):
        keep = place >= k
        b = b + a * jnp.where(keep, pltpu.roll(b, k, 1), 0.0)
        a = a * jnp.where(keep, pltpu.roll(a, k, 1), 1.0)
    out = []
    for g in range(rows // 8):
        s = b[g] + a[g] * carry
        out.append(s)
        carry = s[7:8]
    return jnp.concatenate(out, axis=0), carry


def scan_backward(a, b, carry):
    rows, cols = a.shape
    a = a.reshape(rows // 8, 8, cols)
    b = b.reshape(rows // 8, 8, cols)
    place = lax.broadcasted_iota(jnp.int32, (rows // 8, 8, cols), 1)
    for k in (1, 2, 4):
        keep = place < 8 - k
        b = b + a * jnp.where(keep, pltpu.roll(b, 8 - k, 1), 0.0)
        a = a * jnp.where(keep, pltpu.roll(a, 8 - k, 1), 1.0)
    out = []
    for g in reversed(range(rows // 8)):
        s = b[g] + a[g] * carry
        out.append(s)
        carry = s[0:1]
    return jnp.concatenate(out[::-1], axis=0), carry


def rows_of(i, n):
    return pl.ds(pl.multiple_of(i * n, n), n)


def join_params(gs, prm, gains, sizes):
    y_size = sizes[2]
    for yy in range(y_size):
        prm[yy] = jnp.sum(gs[0, yy, :, :, 32:48, :].astype(F32), axis=(0, 1))
    d = gains.shape[1]
    for n in range(2):
        row = jnp.concatenate([prm[0, 8 + 3 * n + k : 9 + 3 * n + k, :] for k in range(3)], axis=1)
        gains[n : n + 1, :] = row[:, :d]


def head_weight(gs, yy, first, group):
    blocks = gs[0, yy, :, :, first : first + 16, :]
    z, x, r, c = blocks.shape
    if group > 1:
        blocks = jnp.sum(blocks.astype(F32).reshape(z * x // group, group, r, c), axis=1).astype(BF)
    return blocks.reshape(-1, c)


def transpose_into(dst, src, n, step=256):
    @pl.loop(0, n // step)
    def _(i):
        dst[:, rows_of(i, step)] = src[rows_of(i, step), :].T


def forward_kernel(sizes, group,
                   tok, cot, w_rnn, w_gel, w_out, w_gate, w_up, w_down, small_in, rec_in, inp_in,
                   o_w, o_cot, o_cott, o_n1t, o_n2t, o_c6, o_cf, o_a, o_ri, o_lru, o_cv, o_mix, prm, gains, hw,
                   W, gs, T1, SA, SB, N1, RI, A, CV, C6, LRU, PS, PR, MIX, pack,
                   ss, rs, sss, srs, ps, pr, ls, outs):
    net = Net(*sizes)
    z_size, x_size, y_size = sizes
    c = net.at["c"]
    half = SEQ // 2
    ch = W.shape[-1]
    part = W.shape[4]
    depth = T1.shape[1]
    own, other = pl.ds(pl.multiple_of(c * half, half), half), pl.ds(pl.multiple_of((1 - c) * half, half), half)
    mine = (net.at["y"], net.at["z"], net.at["x"])
    dp_index = lax.axis_index("dp")

    sources = {RNN: w_rnn, GEL: w_gel, GA0: w_gate.at[:, 0:ch], GA1: w_gate.at[:, ch : 2 * ch], UP0: w_up.at[:, 0:ch],
               UP1: w_up.at[:, ch : 2 * ch]}
    place = {u: pltpu.make_async_copy(src, W.at[(u, *mine)], ls.at[u]) for u, src in sources.items()}
    place["tok"] = pltpu.make_async_copy(tok, T1.at[own], ls.at[OUT])
    place["cot"] = pltpu.make_async_copy(cot, SA.at[own], ls.at[DN0])
    for cp in place.values():
        cp.start()

    lanes = small_in[...].astype(F32)
    lanes = jnp.concatenate([lanes, jnp.zeros((16, 3 * ch - 128), F32)], axis=1)
    pack[...] = jnp.zeros_like(pack)
    pack[0:8, :] = pltpu.roll(lanes, dp_index * (ch // (z_size * x_size)), 1)[0:8, 0:ch]
    spread = pltpu.roll(lanes, dp_index * part, 1)
    for n in range(2):
        for k in range(3):
            pack[8 + 3 * n + k : 9 + 3 * n + k, :] = spread[8 + n : 9 + n, k * ch : (k + 1) * ch]
    gs[(0, *mine, slice(32, 48))] = pack[...].astype(BF)
    for n, src in enumerate((rec_in, inp_in)):
        for h in range(ch // 128):
            gs[(0, *mine, slice(16 * n, 16 * n + 16), slice(h * 128, (h + 1) * 128))] = src[h]
    if part % 128:
        W[(OUT, *mine)] = w_out[...]
        W[(DN0, *mine)] = w_down[:, :ch]
        W[(DN1, *mine)] = w_down[:, ch:]
    else:
        W[(OUT, *mine)] = w_out[...].T
        W[(DN0, *mine)] = w_down[:ch, :].T
        W[(DN1, *mine)] = w_down[ch:, :].T
    net.barrier()

    big = Gather(net, W, F_FLOW, ss, rs, True)
    small = Gather(net, gs, ("zxy",), sss, srs, False)
    tok_copy = pair_copy(net, tok, T1.at[own], ps, pr, 0)
    cot_copy = pair_copy(net, cot, SA.at[own], ps, pr, 1)
    tok_in = pair_copy(net, tok, T1.at[other], ps, pr, 0)
    cot_in = pair_copy(net, cot, SA.at[other], ps, pr, 1)
    mix_copy = pair_copy(net, PS, PR, ps, pr, 2)
    n2_copy = pair_copy(net, SA.at[own], SA.at[own], ps, pr, 3)
    n2_in = pair_copy(net, SA.at[other], SA.at[other], ps, pr, 3)
    out_copies = {}

    def send_out(name, src, dst):
        out_copies[name] = pltpu.make_async_copy(src, dst, outs.at[len(out_copies)])
        out_copies[name].start()

    waited = set()

    def sent(name):
        if name not in waited:
            waited.add(name)
            out_copies[name].wait()

    small.event(0, 0)
    tok_copy.start()
    cot_copy.start()
    for u in sources:
        place[u].wait()

    def pre1():
        place["tok"].wait()
        place["cot"].wait()
        cot_in.wait_recv()
        send_out("cot", SA, o_cot)
        transpose_into(SB, SA, SEQ)
        send_out("cott", SB, o_cott)
        small.event(0, 1)

    def pre2():
        RI[0:8, :] = jnp.zeros((8, y_size * ch), F32)
        tok_in.wait_recv()
        small.event(0, 2)

    def pre3():
        small.event(0, 3)
        join_params(gs, prm, gains, sizes)
        for yy in range(y_size):
            for n in range(2):
                hw[n, :, yy * ch : (yy + 1) * ch] = head_weight(gs, yy, 16 * n, group)

        @pl.loop(0, SEQ // 128)
        def _(i):
            v = T1[rows_of(i, 128), :].astype(F32)
            s = lax.rsqrt(jnp.mean(v * v, axis=1, keepdims=True) + EPS)
            N1[rows_of(i, 128), :] = (v * s * gains[0:1, :]).astype(BF)

        sent("cott")
        transpose_into(SB, N1, SEQ)
        send_out("n1t", SB, o_n1t)

    def full(u):
        return jnp.concatenate([W[u, yy].reshape(depth, ch) for yy in range(y_size)], axis=1)

    def unit_out(*units):
        for u in units:
            send_out(("w", u), W.at[u], o_w.at[u])

    def rnn():
        @pl.loop(0, SEQ // 512)
        def _(i):
            RI[pl.ds(pl.multiple_of(i * 512 + 8, 8), 512), :] = nn(N1[rows_of(i, 512), :], full(RNN))

        unit_out(RNN)
        send_out("ri", RI, o_ri)

    T = 128

    def branch(hook):
        def branch_tile(i, carries):
            hook(i)
            rows = rows_of(i, T)
            br = nn(N1[rows, :], full(GEL))
            new = []
            for yy in range(y_size):
                cols = slice(yy * ch, (yy + 1) * ch)
                p = prm[yy]
                x = RI[pl.ds(pl.multiple_of(i * T, T), T + 8), cols]
                cv = p[4:5] + p[0:1] * x[8:]
                for k in range(1, 4):
                    cv = cv + p[k : k + 1] * pltpu.roll(x, k, 0)[8:]
                cv_low = cv.astype(BF)
                CV[rows, cols] = cv_low
                cv = cv_low.astype(F32)
                rec, inp = [], []
                for h in range(ch // 128):
                    hc = slice(yy * ch + h * 128, yy * ch + (h + 1) * 128)
                    both = nn(cv_low[:, h * 128 : (h + 1) * 128], jnp.concatenate([hw[0, :, hc], hw[1, :, hc]], axis=1))
                    rec.append(both[:, :128])
                    inp.append(both[:, 128:])
                r = jax.nn.sigmoid(jnp.concatenate(rec, axis=1) + p[5:6])
                w = jax.nn.sigmoid(jnp.concatenate(inp, axis=1) + p[6:7])
                soft = jnp.log1p(jnp.exp(-jnp.abs(p[7:8]))) + jnp.maximum(p[7:8], 0.0)
                a = jnp.exp((-DECAY_SCALE * soft) * r)
                u = 1.0 - a * a + GUARD
                inv = lax.rsqrt(u)
                root = u * inv
                wc = w * cv
                state, last = scan_forward(a, root * wc, carries[yy])
                first = lax.broadcasted_iota(jnp.int32, (T, ch), 0) == 0
                prev = jnp.where(first, carries[yy], pltpu.roll(state, 1, 0))
                new.append(last)
                g, gp = gelu_parts(br[:, cols])
                LRU[rows, cols] = (state * g).astype(BF)
                cp = (prev - a * wc * inv) * a * r * (-DECAY_SCALE)
                A[rows, cols] = a
                C6[0, rows, cols] = g.astype(BF)
                C6[1, rows, cols] = (state * gp).astype(BF)
                C6[2, rows, cols] = cp.astype(BF)
                C6[3, rows, cols] = (cp * soft * (1.0 - r)).astype(BF)
                C6[4, rows, cols] = (root * wc * (1.0 - w)).astype(BF)
                C6[5, rows, cols] = (root * w).astype(BF)
            return tuple(new)

        lax.fori_loop(0, SEQ // T, branch_tile, tuple(jnp.zeros((1, ch), F32) for _ in range(y_size)))
        unit_out(GEL)
        send_out("cf", C6, o_cf)
        send_out("a", A, o_a)
        send_out("lru", LRU, o_lru)
        send_out("cv", CV, o_cv)

    def out_rows(rows):
        return nt(LRU[rows, :], full(OUT))

    def out():
        PS[...] = out_rows(other)
        sent("cot")
        sent("n1t")
        mix_copy.start()
        MIX[...] = out_rows(own)
        unit_out(OUT)

    def mix():
        mix_copy.wait_recv()

        @pl.loop(0, half // 128)
        def _(i):
            rows = rows_of(i, 128)
            v = tok[rows, :].astype(F32) + MIX[rows, :] + PR[rows, :]
            MIX[rows, :] = v
            s = lax.rsqrt(jnp.mean(v * v, axis=1, keepdims=True) + EPS)
            SA[pl.ds(pl.multiple_of(c * half + i * 128, 128), 128), :] = (v * s * gains[1:2, :]).astype(BF)

        n2_copy.start()
        send_out("mix", MIX, o_mix)

    def n2():
        n2_in.wait_recv()
        transpose_into(SB, SA, SEQ)
        send_out("n2t", SB, o_n2t)
        sent("cf")

    F = 256

    def ff(j):
        def loop(hook):
            @pl.loop(0, SEQ // F)
            def _(i):
                hook(i)
                rows = rows_of(i, F)
                up = nn(SA[rows, :], full(UP[j]))
                g, gp = gelu_parts(nn(SA[rows, :], full(GATE[j])))
                C6[j, rows, :] = (g * up).astype(BF)
                C6[2 + j, rows, :] = (gp * up).astype(BF)
                C6[4 + j, rows, :] = g.astype(BF)

            unit_out(GATE[j], UP[j])
        return loop

    run_plan(F_PLAN, {"pre1": (1, pre1), "pre2": (1, pre2), "pre3": (1, pre3), "rnn": (1, rnn), "br": (SEQ // T, branch),
                      "out": (1, out), "mix": (1, mix), "n2": (1, n2), "ffa": (SEQ // F, ff(0)), "ffb": (SEQ // F, ff(1))},
             big.event)
    send_out("c6", C6, o_c6)
    unit_out(DN0, DN1)
    for chunk in range(CHUNKS):
        big.drain(chunk)
    small.drain(0)
    for cp in (tok_copy, cot_copy, mix_copy, n2_copy):
        cp.wait_send()
    for name in out_copies:
        sent(name)


class Scatter:
    def __init__(self, net, ref, flows, bufs, ss, rs, halves):
        self.net, self.ref, self.flows, self.bufs, self.ss, self.rs, self.halves = net, ref, flows, bufs, ss, rs, halves

    def rows(self, c):
        return chunk_rows(c, self.ref.shape[4]) if self.halves else slice(None)

    def slot(self, c):
        return SLOT[c // 2] if self.halves else c

    def copy(self, c, s, j):
        order = self.flows[c]
        d = order[s]
        at = dict(self.net.at)
        at[d] = self.net.shifted(d, j)
        idx = [at[e] if e in order[: s + 1] else slice(None) for e in "yzx"]
        k = self.net.off[d] + j - 1
        return pltpu.make_async_remote_copy(
            src_ref=self.ref.at[(self.slot(c), *idx, self.rows(c))], dst_ref=self.bufs[c, s].at[j - 1],
            send_sem=self.ss.at[c, k], recv_sem=self.rs.at[c, k],
            device_id=self.net.device(d, j), device_id_type=MESH)

    def hops(self, c, s):
        return range(1, self.net.size[self.flows[c][s]])

    def add(self, c, s, out):
        order = self.flows[c]
        for j in self.hops(c, s):
            self.copy(c, s, j).wait_recv()
        rest = [e for e in "zyx" if e not in order[: s + 1]]
        buf = self.bufs[c, s]
        rows = self.rows(c)

        def block(place):
            idx = (self.slot(c), *[place[e] if e in place else self.net.at[e] for e in "yzx"], rows)
            total = self.ref[idx].astype(F32)
            for j in self.hops(c, s):
                total = total + buf[(j - 1, *[place[e] for e in "yzx" if e in place])].astype(F32)
            if s < 2:
                self.ref[idx] = total.astype(BF)
            elif self.halves:
                out[c // 2, rows] = total
            else:
                out[c] = total

        def over(names, place):
            if not names:
                block(place)
            elif names[0] == "z":
                @pl.loop(0, self.net.size["z"])
                def _(z):
                    over(names[1:], {**place, "z": z})
            else:
                for n in range(self.net.size[names[0]]):
                    over(names[1:], {**place, names[0]: n})

        over(rest, {})

    def event(self, c, k, out):
        if self.rows(c) is None:
            return
        if k:
            self.add(c, k - 1, out)
        if k < 3:
            for j in self.hops(c, k):
                self.copy(c, k, j).start()

    def drain(self, c):
        if self.rows(c) is None:
            return
        for s in range(3):
            for j in self.hops(c, s):
                self.copy(c, s, j).wait_send()


def landing(flows, sizes, rows, ch):
    size = dict(zip("zxy", sizes))
    shapes = {}
    for c, order in enumerate(flows):
        n = rows(c)
        for s in range(3):
            if n:
                rest = [size[e] for e in "yzx" if e not in order[: s + 1]]
                shapes[c, s] = (size[order[s]] - 1, *rest, n, ch)
    return shapes


SLOT = {DN0: 9, DN1: 10, GA0: DN0, GA1: DN1, UP0: GA0, UP1: GA1, OUT: UP0, GEL: UP1, RNN: OUT}


def big_landing(sizes, part, ch):
    def rows(c):
        cut = chunk_rows(c, part)
        return 0 if cut is None else len(range(part)[cut])

    return landing(B_FLOW, sizes, rows, ch)


def small_landing(sizes, ch):
    return landing(("yxz",), sizes, lambda c: SMALL, ch)


def backward_kernel(sizes, group,
                    w_h, cot_h, cott_h, n1t_h, n2t_h, c6_h, cf_h, a_h, ri_h, lru_h, cv_h, mix_h, tok_h, prm, gains, hw,
                    o_block, o_gtok, o_gw, o_gs,
                    W, C6, COT, TT, NT, GM, PS, PR, LRU, AS, RS, acc, GS, pgain,
                    ss, rs, sss, srs, ps, pr, ls, ast, rst, *landed):
    net = Net(*sizes)
    z_size, x_size, y_size = sizes
    c = net.at["c"]
    half = SEQ // 2
    ch = W.shape[-1]
    depth = COT.shape[1]
    own, other = pl.ds(pl.multiple_of(c * half, half), half), pl.ds(pl.multiple_of((1 - c) * half, half), half)
    loads = {}

    def load(name, src, dst):
        loads[name] = pltpu.make_async_copy(src, dst, ls.at[len(loads)])
        loads[name].start()

    def loaded(*names):
        for name in names:
            loads[name].wait()

    load("cott", cott_h, TT)
    load("h", c6_h.at[0:2], C6.at[0:2])
    load("cot", cot_h, COT)
    load("w_dn", w_h.at[DN0:], W.at[DN0:9])
    load("ab", c6_h.at[2:6], C6.at[2:6])
    load("mix", mix_h, GM)
    load("n2t", n2t_h, NT)
    load("w_ff", w_h.at[GA0:DN0], W.at[GA0:DN0])
    load("w_rnn", w_h.at[0:GA0], W.at[0:GA0])
    load("lru", lru_h, LRU)
    load("tok", tok_h, PS.at[1])
    net.barrier()
    shapes = big_landing(sizes, W.shape[4], ch)
    big = Scatter(net, W, B_FLOW, dict(zip(shapes, landed)), ss, rs, True)
    small = None
    if group == 1:
        tail = landed[len(shapes):]
        small = Scatter(net, GS, ("yxz",), dict(zip(small_landing(sizes, ch), tail)), sss, srs, False)

    def full(u):
        return jnp.concatenate([W[u, yy].reshape(depth, ch) for yy in range(y_size)], axis=1)

    zh = z_size // 2

    def weight_grad(u, left, right):
        @pl.loop(0, 2)
        def _(i):
            val = nn(left[rows_of(i, depth // 2), :], right[...]).astype(BF)
            for yy in range(y_size):
                W[SLOT[u], yy, pl.ds(i * zh, zh)] = val[:, yy * ch : (yy + 1) * ch].reshape(
                    zh, x_size, depth // (z_size * x_size), ch)

    F = 256
    base_own, base_other = c * half, (1 - c) * half
    back_copy = pair_copy(net, PS.at[0], PR.at[0], ps, pr, 0)
    row_copy = pair_copy(net, COT.at[own], COT.at[own], ps, pr, 1)
    row_in = pair_copy(net, COT.at[other], COT.at[other], ps, pr, 1)
    out_copy = pair_copy(net, PS.at[0], PR.at[1], ps, pr, 2)
    rnn_copy = pair_copy(net, PS.at[0], PR.at[0], ps, pr, 3)
    gain_copy = pair_copy(net, pgain.at[0:8], pgain.at[8:16], ps, pr, 4)
    block_copy = pltpu.make_async_copy(PR.at[1], o_block, ls.at[15])

    def d0():
        loaded("cott", "h")
        weight_grad(DN0, TT, C6.at[0])

    def d1():
        weight_grad(DN1, TT, C6.at[1])

    def gh(hook):
        loaded("cot", "w_dn", "ab")

        @pl.loop(0, 2 * (SEQ // F))
        def _(n):
            hook(n)
            j, i = n // (SEQ // F), lax.rem(n, SEQ // F)
            rows = rows_of(i, F)
            g = nn(COT[rows, :], full(DN0 + j))
            C6[2 + j, rows, :] = (g * C6[2 + j, rows, :].astype(F32)).astype(BF)
            C6[4 + j, rows, :] = (g * C6[4 + j, rows, :].astype(F32)).astype(BF)

    def span(base, i):
        return pl.ds(pl.multiple_of(base + i * F, F), F)

    def mlp_back(rows):
        return (nt(C6[2, rows, :], full(GA0)) + nt(C6[3, rows, :], full(GA1))
                + nt(C6[4, rows, :], full(UP0)) + nt(C6[5, rows, :], full(UP1)))

    def mlp_out(rows):
        return nt(C6[0, rows, :], full(DN0)) + nt(C6[1, rows, :], full(DN1))

    def rnn_back(rows):
        return nt(C6[5, rows, :], full(RNN)) + nt(C6[1, rows, :], full(GEL))

    def partial_rows(fn, base, dst, hook=None):
        @pl.loop(0, half // F)
        def _(i):
            if hook is not None:
                hook(i)
            dst[rows_of(i, F), :] = fn(span(base, i)).astype(dst.dtype)

    def bo():
        partial_rows(mlp_out, base_other, PS.at[0])
        out_copy.start()

    def bw():
        partial_rows(mlp_out, base_own, o_gtok)

    def gno(hook):
        loaded("w_ff", "mix")
        out_copy.wait_recv()

        @pl.loop(0, half // F)
        def _(i):
            rows = rows_of(i, F)
            PR[1, rows, :] = (GM[rows, :] + o_gtok[rows, :] + PR[1, rows, :].astype(F32)).astype(BF)

        block_copy.start()
        out_copy.wait_send()
        partial_rows(mlp_back, base_other, PS.at[0], hook)
        back_copy.start()

    def gnw(hook):
        partial_rows(mlp_back, base_own, o_gtok, hook)

    T = 128

    def norm():
        acc[...] = jnp.zeros_like(acc)
        pgain[...] = jnp.zeros_like(pgain)
        back_copy.wait_recv()

        @pl.loop(0, half // T)
        def _(i):
            rows = rows_of(i, T)
            at = pl.ds(pl.multiple_of(base_own + i * T, T), T)
            v = GM[rows, :]
            gn = o_gtok[rows, :] + PR[0, rows, :].astype(F32)
            s = lax.rsqrt(jnp.mean(v * v, axis=1, keepdims=True) + EPS)
            q = gn * gains[1:2, :]
            pgain[1:2, :] += jnp.sum(gn * v * s, axis=0, keepdims=True)
            gm = COT[at, :].astype(F32) + s * q - (s * s * s) * v * jnp.mean(q * v, axis=1, keepdims=True)
            o_gtok[rows, :] = gm
            COT[at, :] = gm.astype(BF)

        row_copy.start()

    def ga0():
        loaded("n2t")
        weight_grad(GA0, NT, C6.at[2])

    def ga1():
        weight_grad(GA1, NT, C6.at[3])

    def up0():
        weight_grad(UP0, NT, C6.at[4])

    def up1():
        weight_grad(UP1, NT, C6.at[5])
        load("n1t", n1t_h, NT)
        load("cf", cf_h, C6)

    tiles = SEQ // T

    def fetch(n, slot):
        at = (tiles - 1 - n) * T
        return (
            pltpu.make_async_copy(a_h.at[pl.ds(pl.multiple_of(at, T), T)], AS.at[slot], ast.at[slot]),
            pltpu.make_async_copy(ri_h.at[pl.ds(pl.multiple_of(at, T), T + 8)], RS.at[slot], rst.at[slot]),
        )

    def outg():
        row_in.wait_recv()
        loaded("w_rnn", "lru")
        transpose_into(TT, COT, SEQ)
        weight_grad(OUT, TT, LRU)
        load("cv", cv_h, LRU)
        for cp in fetch(0, 0):
            cp.start()
        loaded("cf")

    def back(hook):
        def back_tile(n, carries):
            hook(n)
            slot = lax.rem(n, 2)
            for cp in fetch(n, slot):
                cp.wait()

            @pl.when(n + 1 < tiles)
            def _():
                for cp in fetch(n + 1, 1 - slot):
                    cp.start()

            i = tiles - 1 - n
            rows = rows_of(i, T)
            gl_all = nn(COT[rows, :], full(OUT))
            new = []
            for yy in range(y_size):
                adj_next, a_next, gco_next = carries[yy]
                cols = slice(yy * ch, (yy + 1) * ch)
                p = prm[yy]
                gl = gl_all[:, cols]
                at = AS[slot, :, cols]
                last = lax.broadcasted_iota(jnp.int32, (T, ch), 0) == T - 1
                shifted = jnp.where(last, a_next, pltpu.roll(at, T - 1, 0))
                adj, adj_first = scan_backward(shifted, gl * C6[0, rows, cols].astype(F32), adj_next)
                C6[1, rows, cols] = (gl * C6[1, rows, cols].astype(F32)).astype(BF)
                grp = adj * C6[3, rows, cols].astype(F32)
                gip = adj * C6[4, rows, cols].astype(F32)
                gr_low, gi_low = grp.astype(BF), gip.astype(BF)
                gcd = adj * C6[5, rows, cols].astype(F32)
                acc[yy, 5:6] += jnp.sum(grp, axis=0, keepdims=True)
                acc[yy, 6:7] += jnp.sum(gip, axis=0, keepdims=True)
                acc[yy, 7:8] += jnp.sum(adj * C6[2, rows, cols].astype(F32), axis=0, keepdims=True)
                C6[3, rows, cols] = gr_low
                C6[4, rows, cols] = gi_low
                parts = []
                for h in range(ch // 128):
                    hs = slice(h * 128, (h + 1) * 128)
                    hc = slice(yy * ch + h * 128, yy * ch + (h + 1) * 128)
                    parts.append(nt(jnp.concatenate([gr_low[:, hs], gi_low[:, hs]], axis=1),
                                    jnp.concatenate([hw[0, :, hc], hw[1, :, hc]], axis=1)))
                gco = gcd + jnp.concatenate(parts, axis=1)
                ext = jnp.concatenate([gco, gco_next], axis=0)
                x = RS[slot, :, cols]
                grn = p[0:1] * gco
                acc[yy, 0:1] += jnp.sum(gco * x[8:], axis=0, keepdims=True)
                acc[yy, 4:5] += jnp.sum(gco, axis=0, keepdims=True)
                for k in range(1, 4):
                    grn = grn + p[k : k + 1] * pltpu.roll(ext, T + 8 - k, 0)[:T]
                    acc[yy, k : k + 1] += jnp.sum(gco * pltpu.roll(x, k, 0)[8:], axis=0, keepdims=True)
                C6[5, rows, cols] = grn.astype(BF)
                new.append((adj_first, at[0:1], gco[0:8]))
            return tuple(new)

        zero = (jnp.zeros((1, ch), F32), jnp.zeros((1, ch), F32), jnp.zeros((8, ch), F32))
        lax.fori_loop(0, tiles, back_tile, (zero,) * y_size)
        loaded("n1t")

    def gel():
        weight_grad(GEL, NT, C6.at[1])

    def rnn():
        weight_grad(RNN, NT, C6.at[5])

    def gn1o():
        loaded("tok")
        back_copy.wait_send()
        partial_rows(rnn_back, base_other, PS.at[0])
        rnn_copy.start()

    def gn1w():
        partial_rows(rnn_back, base_own, GM)

    def heads():
        loaded("cv")
        for yy in range(y_size):
            acc[yy, 7:8] = acc[yy, 7:8] * jax.nn.sigmoid(prm[yy, 7:8])
            for h in range(ch // 128):
                hs = slice(h * 128, (h + 1) * 128)
                hc = slice(yy * ch + h * 128, yy * ch + (h + 1) * 128)
                both = lax.dot_general(LRU[:, hc], jnp.concatenate([C6[3, :, hc], C6[4, :, hc]], axis=1),
                                       (((0,), (0,)), ((), ())), preferred_element_type=F32)
                for n in range(2):
                    val = both[:, n * 128 : (n + 1) * 128]
                    if group > 1:
                        o_gs[yy, 128 * n : 128 * n + 128, hs] = val
                    else:
                        GS[0, yy, :, :, 16 * n : 16 * n + 16, hs] = val.astype(BF).reshape(z_size, x_size, 16, 128)

    def fin():
        rnn_copy.wait_recv()

        @pl.loop(0, half // T)
        def _(i):
            rows = rows_of(i, T)
            v = PS[1, rows, :].astype(F32)
            gn = GM[rows, :] + PR[0, rows, :].astype(F32)
            s = lax.rsqrt(jnp.mean(v * v, axis=1, keepdims=True) + EPS)
            q = gn * gains[0:1, :]
            pgain[0:1, :] += jnp.sum(gn * v * s, axis=0, keepdims=True)
            o_gtok[rows, :] += s * q - (s * s * s) * v * jnp.mean(q * v, axis=1, keepdims=True)

        gain_copy.start()

    def small_step(k):
        def fn():
            if k == 0:
                gain_copy.wait_recv()
                for n in range(2):
                    row = pgain[n : n + 1, :] + pgain[8 + n : 9 + n, :]
                    row = jnp.concatenate([row, jnp.zeros((1, 3 * ch - depth), F32)], axis=1)
                    for m in range(3):
                        for yy in range(y_size):
                            acc[yy, 8 + 3 * n + m : 9 + 3 * n + m, :] = row[:, m * ch : (m + 1) * ch]
                if group > 1:
                    for yy in range(y_size):
                        o_gs[yy, 256:272, :] = acc[yy]
                    return

                @pl.loop(0, z_size)
                def _(z):
                    for yy in range(y_size):
                        for xx in range(x_size):
                            GS[0, yy, z, xx, 32:48, :] = acc[yy].astype(BF)

            if group == 1:
                small.event(0, k, o_gs)
        return fn

    blocks = dict(d0=d0, d1=d1, bo=bo, bw=bw, ga0=ga0, ga1=ga1, norm=norm, up0=up0, up1=up1, outg=outg, gel=gel, rnn=rnn,
                  gn1o=gn1o, gn1w=gn1w, heads=heads, fin=fin)
    blocks = {name: (1, fn) for name, fn in blocks.items()}
    for k in range(4):
        blocks["s" + str(k)] = (1, small_step(k))
    blocks.update(gh=(2 * SEQ // F, gh), gno=(half // F, gno), gnw=(half // F, gnw), t=(tiles, back))
    run_plan(B_PLAN, blocks, lambda chunk, k: big.event(chunk, k, o_gw))
    for chunk in range(CHUNKS):
        big.drain(chunk)
    if group == 1:
        small.drain(0)
    for cp in (row_copy, rnn_copy, gain_copy):
        cp.wait_send()
    block_copy.wait()


def finish_kernel(sizes, block_in, gtok_in, gw, gs,
                  o_block, o_gtok, o_mg, o_rnn, o_gel, o_cw, o_cb, o_rw, o_iw, o_rb, o_ib, o_dp, o_out, o_lg, o_gate, o_up,
                  o_down):
    ch = gw.shape[2]
    dp = sizes[0] * sizes[1]
    part, own = o_mg.shape[1], ch // dp
    dp_index = lax.axis_index("dp")
    o_block[...] = block_in[...]
    o_gtok[...] = gtok_in[...]
    o_rnn[...] = gw[RNN]
    o_gel[...] = gw[GEL]
    o_out[...] = gw[OUT].T
    for j in range(2):
        cols = slice(j * ch, (j + 1) * ch)
        o_gate[:, cols] = gw[GATE[j]]
        o_up[:, cols] = gw[UP[j]]
        o_down[cols, :] = gw[DOWN[j]].T
    for h in range(ch // 128):
        o_rw[h] = gs[0, 0:16, h * 128 : (h + 1) * 128]
        o_iw[h] = gs[0, 16:32, h * 128 : (h + 1) * 128]
    rows = pltpu.roll(gs[0, 32:40, :], ch - dp_index * own, 1)
    o_cw[...] = rows[0:4, 0:own]
    for k, ref in ((4, o_cb), (5, o_rb), (6, o_ib), (7, o_dp)):
        ref[...] = rows[k : k + 1, 0:own]
    for n, ref in ((0, o_mg), (1, o_lg)):
        row = jnp.concatenate([gs[0, 40 + 3 * n + k : 41 + 3 * n + k, :] for k in range(3)], axis=1)
        row = jnp.broadcast_to(row, (8, 3 * ch))
        ref[...] = pltpu.roll(row, 3 * ch - dp_index * part, 1)[0:1, 0:part]


def any_spec():
    return pl.BlockSpec(memory_space=pl.ANY)


def vmem_spec():
    return pl.BlockSpec(memory_space=pltpu.VMEM)


def body(sizes, tokens, mix_gain, rnn_weight, gelu_weight, conv_weight, conv_bias, recur_weight, input_weight,
         recur_bias, input_bias, decay_param, out_weight, mlp_gain, gate_weight, up_weight, down_weight, cotangent):
    z_size, x_size, y_size = sizes
    dp = z_size * x_size
    dp_index = lax.axis_index("dp")
    rows, depth = tokens.shape
    part, ch = rnn_weight.shape
    head_rows = recur_weight.shape[1]
    group = max(1, 16 // head_rows)
    wide = y_size * ch
    own = ch // dp
    small_in = jnp.concatenate([conv_weight, conv_bias[None], recur_bias[None], input_bias[None], decay_param[None]], axis=0)
    small_in = jnp.concatenate([jnp.pad(small_in, ((0, 0), (0, 128 - own))),
                                jnp.pad(jnp.stack([mix_gain, mlp_gain]), ((0, 6), (0, 128 - part)))], axis=0)
    heads = [recur_weight, input_weight]
    out_w, down_w = out_weight, down_weight
    if part % 128:
        out_w, down_w = out_weight.T, down_weight.T
    if group > 1:
        heads = [lax.dynamic_update_slice(jnp.zeros((w.shape[0], 16, 128), BF), w, (0, lax.rem(dp_index * head_rows, 16), 0))
                 for w in heads]
    shape = jax.ShapeDtypeStruct
    grid = (y_size, z_size, x_size)
    hops = z_size + x_size + y_size - 3
    f_out = [
        shape((UNITS, *grid, part, ch), BF), shape((SEQ, depth), BF), shape((depth, SEQ), BF),
        shape((depth, SEQ), BF), shape((depth, SEQ), BF), shape((6, SEQ, wide), BF), shape((6, SEQ, wide), BF),
        shape((SEQ, wide), F32), shape((SEQ + 8, wide), F32), shape((SEQ, wide), BF), shape((SEQ, wide), BF),
        shape((rows, depth), F32), shape((y_size, 16, ch), F32), shape((8, depth), F32), shape((2, 128, wide), BF),
    ]
    dma = pltpu.SemaphoreType.DMA
    kept = pl.pallas_call(
        functools.partial(forward_kernel, sizes, group),
        out_shape=f_out,
        in_specs=[vmem_spec(), any_spec(), any_spec(), any_spec(), vmem_spec(), any_spec(), any_spec(), vmem_spec(),
                  vmem_spec(), vmem_spec(), vmem_spec()],
        out_specs=[any_spec()] * 12 + [vmem_spec()] * 3,
        scratch_shapes=[
            pltpu.VMEM((UNITS, *grid, part, ch), BF), pltpu.VMEM((1, *grid, SMALL, ch), BF),
            pltpu.VMEM((SEQ, depth), BF), pltpu.VMEM((SEQ, depth), BF), pltpu.VMEM((depth, SEQ), BF),
            pltpu.VMEM((SEQ, depth), BF), pltpu.VMEM((SEQ + 8, wide), F32), pltpu.VMEM((SEQ, wide), F32),
            pltpu.VMEM((SEQ, wide), BF), pltpu.VMEM((6, SEQ, wide), BF), pltpu.VMEM((SEQ, wide), BF),
            pltpu.VMEM((rows, depth), F32), pltpu.VMEM((rows, depth), F32), pltpu.VMEM((rows, depth), F32),
            pltpu.VMEM((16, ch), F32),
            dma((CHUNKS, hops)), dma((CHUNKS, hops)), dma((1, hops)), dma((1, hops)), dma((4,)), dma((4,)), dma((9,)),
            dma((24,)),
        ],
        compiler_params=pltpu.CompilerParams(collective_id=0, has_side_effects=True, vmem_limit_bytes=VMEM_LIMIT),
        name="gather_forward",
    )(tokens, cotangent, rnn_weight, gelu_weight, out_w, gate_weight, up_weight, down_w, small_in, *heads)
    landed = list(big_landing(sizes, part, ch).values())
    gs_shape, small_grid = (y_size, 272, ch), (1, 1, 1)
    if group == 1:
        landed += list(small_landing(sizes, ch).values())
        gs_shape, small_grid = (1, SMALL, ch), grid
    block_out, grad_tokens, gw, gs = pl.pallas_call(
        functools.partial(backward_kernel, sizes, group),
        out_shape=[shape((rows, depth), BF), shape((rows, depth), F32), shape((UNITS, part, ch), F32), shape(gs_shape, F32)],
        in_specs=[any_spec()] * 13 + [vmem_spec()] * 3,
        out_specs=[any_spec()] + [vmem_spec()] * 3,
        scratch_shapes=[
            pltpu.VMEM((UNITS + 2, *grid, part, ch), BF), pltpu.VMEM((6, SEQ, wide), BF), pltpu.VMEM((SEQ, depth), BF),
            pltpu.VMEM((depth, SEQ), BF), pltpu.VMEM((depth, SEQ), BF), pltpu.VMEM((rows, depth), F32),
            pltpu.VMEM((2, rows, depth), BF), pltpu.VMEM((2, rows, depth), BF), pltpu.VMEM((SEQ, wide), BF),
            pltpu.VMEM((2, 128, wide), F32), pltpu.VMEM((2, 136, wide), F32), pltpu.VMEM((y_size, 16, ch), F32),
            pltpu.VMEM((1, *small_grid, SMALL, ch), BF), pltpu.VMEM((16, depth), F32),
            dma((CHUNKS, hops)), dma((CHUNKS, hops)), dma((1, hops)), dma((1, hops)),
            dma((5,)), dma((5,)), dma((16,)), dma((2,)), dma((2,)),
            *[pltpu.VMEM(s, BF) for s in landed],
        ],
        compiler_params=pltpu.CompilerParams(collective_id=1, has_side_effects=True, vmem_limit_bytes=VMEM_LIMIT),
        name="backward_scatter",
    )(*kept[:12], tokens, *kept[12:])
    if group > 1:
        t = lax.axis_index("tensor")
        every = jnp.zeros((2 * y_size, 272, ch), F32)
        for yy in range(y_size):
            every = lax.dynamic_update_slice(every, gs[yy : yy + 1], (2 * yy + lax.rem(t, 2), 0, 0))
        gs = lax.dynamic_slice(lax.psum(every, ("dp", "tensor")), (t, 0, 0), (1, 272, ch))
        first = dp_index * head_rows
        rec = lax.dynamic_slice(gs[0], (first, 0), (head_rows, ch))
        inp = lax.dynamic_slice(gs[0], (128 + first, 0), (head_rows, ch))
        fill = jnp.zeros((16 - head_rows, ch), F32)
        gs = jnp.concatenate([rec, fill, inp, fill, gs[0, 256:]], axis=0)[None]
    f_shapes = [
        shape((rows, depth), BF), shape((rows, depth), F32), shape((1, part), F32), shape((part, ch), F32),
        shape((part, ch), F32), shape((4, own), F32), shape((1, own), F32), shape((ch // 128, 16, 128), F32),
        shape((ch // 128, 16, 128), F32), shape((1, own), F32), shape((1, own), F32), shape((1, own), F32),
        shape((ch, part), F32), shape((1, part), F32), shape((part, 2 * ch), F32), shape((part, 2 * ch), F32),
        shape((2 * ch, part), F32),
    ]
    res = list(pl.pallas_call(
        functools.partial(finish_kernel, sizes),
        out_shape=f_shapes,
        in_specs=[vmem_spec()] * 4,
        out_specs=[vmem_spec()] * 17,
        compiler_params=pltpu.CompilerParams(vmem_limit_bytes=VMEM_LIMIT),
        name="unpack",
    )(block_out, grad_tokens, gw, gs))
    for k in (2, 6, 9, 10, 11, 13):
        res[k] = res[k][0]
    for k in (7, 8):
        res[k] = res[k][:, :head_rows]
    return tuple(res)


def solution(mesh):
    dp, tensor = mesh.shape["dp"], mesh.shape["tensor"]
    x_size = 2
    sizes = (dp // x_size, x_size, tensor // 2)
    rows, split, vec = P(("dp", "tensor"), None), P("dp", "tensor"), P(("tensor", "dp"))
    head, flip, taps = P("tensor", "dp", None), P("tensor", "dp"), P(None, ("tensor", "dp"))
    return jax.shard_map(
        functools.partial(body, sizes),
        mesh=mesh,
        in_specs=(rows, P("dp"), split, split, taps, vec, head, head, vec, vec, vec, flip, P("dp"), split, split, flip,
                  rows),
        out_specs=(rows, rows, P("dp"), split, split, taps, vec, head, head, vec, vec, vec, flip, P("dp"), split, split,
                   flip),
        check_vma=False,
    )
```

```python
import functools

import jax
import jax.numpy as jnp
from jax import lax
from jax.experimental import pallas as pl
from jax.experimental.pallas import tpu as pltpu
from jax.sharding import PartitionSpec as P

SEQ = 1024
EPS = 1e-06
GUARD = 0.01
DECAY_SCALE = 8.0
GELU_K = 0.7978845608028654
GELU_C = 0.044715
BF = jnp.bfloat16
F32 = jnp.float32
MESH = pl.DeviceIdType.MESH
VMEM_LIMIT = 63 * 1024 * 1024

RNN, GEL, OUT, GA0, UP0, GA1, UP1, DN0, DN1 = range(9)
UNITS = 9
GATE, UP, DOWN = (GA0, GA1), (UP0, UP1), (DN0, DN1)
CHUNKS = 2 * UNITS
SMALL = 48
FLOW = (
    "zxy", "zyx", "zxy", "zyx", "zxy", "yxz", "zxy", "xzy", "yzx", "zyx", "zyx", "zxy", "zyx", "xyz", "zyx", "xzy",
    "zyx", "xyz",
)
BACK = (
    "xyz", "xzy", "yxz", "yxz", "yxz", "yzx", "xzy", "yxz", "xzy", "yxz", "yxz", "xzy", "zyx", "xyz", "zxy", "xzy",
    "yzx", "zyx",
)
PLAN = (
    15, 75, 85, 40, 0, 65, 25, 66, 19, 86, 5, "pre1", "pre2", 26, "pre25", 4, 10, 9, "pre3", 30, 16, 1, 6, 35, 14,
    41, 11, 2, 7, 34, 20, 60, 17, 44, 12, 50, 64, 24, 45, 21, 61, 54, 55, 49, 80, 46, 31, 8, 3, 18, 13, 70, "br", 51,
    42, 59, 36, "br", 22, 47, 27, "br", "br", 84, 56, 32, "br", 39, 74, "br", 76, "br", 52, 37, 71, "br", 48, 62, 33,
    23, 29, 79, 67, 28, "out", "mix", 38, "n2", 43, 57, "ffa", "ffa", 69, 81, 87, 53, 72, 77, "ffa", "ffa", "d0",
    160, 63, 68, 58, "ffb", 82, "ffb", "ffb", "ffb", 89, "d1", 170, 165, 164, 73, 78, 175, 88, 83, "gh", "gh", "gh",
    "gh", "gh", "gh", "gh", "gh", "bo", "bw", "ga0", 120, 166, 171, 125, 179, "ga1", 145, 140, "gno", "gno", 169,
    "gnw", "gnw", 121, 174, "norm", "up0", 130, 135, "up1", 146, "outg", 124, 110, 126, 150, "t", 155, "t", "t", 115,
    "t", 141, 154, 149, "t", "t", 111, 131, "t", 156, 136, "t", 142, "gel", 134, 100, 127, 112, "rnn", 105, 95, 137,
    90, 144, "gn1o", 122, 129, 167, 157, 114, "gn1w", 116, "heads", 113, 101, 159, 143, 139, 161, 96, 176, "fin", 91,
    "s0", 106, 119, 99, 132, 123, 128, "s1", 102, 151, 168, 177, 92, 162, 172, "s2", 117, 104, 97, 147, 107, 94, 138,
    "sr", 152, 178, 173, 158, 133, 163, 109, "s3", 103, 98, 153, 148, 93, 118, 108,
)


def run_plan(plan, blocks, event):
    i = 0
    while i < len(plan):
        name = plan[i]
        i += 1
        if isinstance(name, int):
            event(name // 5, name % 5)
            continue
        turns, fn = blocks[name]
        if turns == 1:
            fn()
            continue
        hooks = {}
        for turn in range(1, turns):
            hooks[turn] = []
            while isinstance(plan[i], int):
                hooks[turn].append(plan[i])
                i += 1
            i += 1

        def hook(n, hooks=hooks):
            for turn, steps in hooks.items():
                if steps:
                    @pl.when(n == turn)
                    def _(steps=steps):
                        for step in steps:
                            event(step // 5, step % 5)

        fn(hook)


def nn(a, b):
    return jnp.dot(a, b, preferred_element_type=F32)


def nt(a, b):
    return lax.dot_general(a, b, (((1,), (1,)), ((), ())), preferred_element_type=F32)


def gelu_parts(v):
    v2 = v * v
    th = jnp.tanh(GELU_K * v * (1.0 + GELU_C * v2))
    half = 0.5 * (1.0 + th)
    return v * half, half + (0.5 * GELU_K) * v * (1.0 - th * th) * (1.0 + (3.0 * GELU_C) * v2)


class Net:
    def __init__(self, z_size, x_size, y_size):
        self.size = {"z": z_size, "x": x_size, "y": y_size, "c": 2}
        dp, t = lax.axis_index("dp"), lax.axis_index("tensor")
        self.at = {"z": dp // x_size, "x": lax.rem(dp, x_size), "y": t // 2, "c": lax.rem(t, 2)}
        self.off = {"z": 0, "x": z_size - 1, "y": z_size + x_size - 2}
        self.relay = z_size + x_size + y_size - 3 if z_size == 4 else None

    def shifted(self, d, j):
        n = self.size[d]
        return lax.rem(self.at[d] + (j % n), n)

    def device(self, d, j):
        at = dict(self.at)
        at[d] = self.shifted(d, j)
        return (at["z"] * self.size["x"] + at["x"], at["y"] * 2 + at["c"])

    def barrier(self):
        sem = pltpu.get_barrier_semaphore()
        count = 0
        for d in "zxyc":
            for j in range(1, self.size[d]):
                pl.semaphore_signal(sem, inc=1, device_id=self.device(d, j), device_id_type=MESH)
                count += 1
        pl.semaphore_wait(sem, count)


def chunk_rows(c, part):
    if part % 32:
        return slice(None) if c % 2 == 0 else None
    return slice(c % 2 * (part // 2), (c % 2 + 1) * (part // 2))


class Gather:
    def __init__(self, net, ref, flows, ss, rs, halves):
        self.net, self.ref, self.flows, self.ss, self.rs, self.halves = net, ref, flows, ss, rs, halves

    def region(self, c, s, at):
        order = self.flows[c]
        idx = [slice(None) if d in order[:s] else at[d] for d in "yzx"]
        if not self.halves:
            return self.ref.at[(c, *idx)]
        return self.ref.at[(c // 2, *idx, chunk_rows(c, self.ref.shape[4]))]

    def copy(self, c, s, j, sender, origin=None, send=None, recv=None):
        d = self.flows[c][s]
        at = dict(self.net.at)
        if sender:
            at[d] = self.net.shifted(d, -j)
        if origin is not None:
            at[d] = origin
        region = self.region(c, s, at)
        k = self.net.off[d] + j - 1
        return pltpu.make_async_remote_copy(
            src_ref=region, dst_ref=region, send_sem=self.ss.at[c, k if send is None else send],
            recv_sem=self.rs.at[c, k if recv is None else recv], device_id=self.net.device(d, j), device_id_type=MESH)

    def relayed(self, c, s):
        return self.net.relay is not None and self.flows[c][s] == "z"

    def sends(self, c, s, act):
        if not self.relayed(c, s):
            for j in range(1, self.net.size[self.flows[c][s]]):
                act(self.copy(c, s, j, False))
            return
        z = self.net.at["z"]
        act(self.copy(c, s, 2, False))
        pl.when(z != 3)(lambda: act(self.copy(c, s, 1, False)))
        pl.when(z != 0)(lambda: act(self.copy(c, s, 3, False)))

    def passes_on(self, c, s, act):
        z = self.net.at["z"]
        k = self.net.relay
        pl.when(z == 2)(lambda: act(self.copy(c, s, 1, False, 0, k, 2)))
        pl.when(z == 1)(lambda: act(self.copy(c, s, 3, False, 3, k, 0)))

    def event(self, c, k):
        if self.halves and chunk_rows(c, self.ref.shape[4]) is None:
            return
        if k == 4:
            s = self.flows[c].index("z")
            if self.relayed(c, s):
                self.copy(c, s, 2, True).wait_recv()
                self.passes_on(c, s, lambda cp: cp.start())
            return
        if k:
            for j in range(1, self.net.size[self.flows[c][k - 1]]):
                if not (self.relayed(c, k - 1) and j == 2):
                    self.copy(c, k - 1, j, True).wait_recv()
        if k < 3:
            self.sends(c, k, lambda cp: cp.start())

    def drain(self, c):
        if self.halves and chunk_rows(c, self.ref.shape[4]) is None:
            return
        for s in range(3):
            self.sends(c, s, lambda cp: cp.wait_send())
            if self.relayed(c, s):
                self.passes_on(c, s, lambda cp: cp.wait_send())


def pair_copy(net, src, dst, ss, rs, k):
    return pltpu.make_async_remote_copy(
        src_ref=src, dst_ref=dst, send_sem=ss.at[k], recv_sem=rs.at[k],
        device_id=net.device("c", 1), device_id_type=MESH)


def scan_forward(a, b, carry):
    rows, cols = a.shape
    a = a.reshape(rows // 8, 8, cols)
    b = b.reshape(rows // 8, 8, cols)
    place = lax.broadcasted_iota(jnp.int32, (rows // 8, 8, cols), 1)
    for k in (1, 2, 4):
        keep = place >= k
        b = b + a * jnp.where(keep, pltpu.roll(b, k, 1), 0.0)
        a = a * jnp.where(keep, pltpu.roll(a, k, 1), 1.0)
    out = []
    for g in range(rows // 8):
        s = b[g] + a[g] * carry
        out.append(s)
        carry = s[7:8]
    return jnp.concatenate(out, axis=0), carry


def scan_backward(a, b, carry):
    rows, cols = a.shape
    a = a.reshape(rows // 8, 8, cols)
    b = b.reshape(rows // 8, 8, cols)
    place = lax.broadcasted_iota(jnp.int32, (rows // 8, 8, cols), 1)
    for k in (1, 2, 4):
        keep = place < 8 - k
        b = b + a * jnp.where(keep, pltpu.roll(b, 8 - k, 1), 0.0)
        a = a * jnp.where(keep, pltpu.roll(a, 8 - k, 1), 1.0)
    out = []
    for g in reversed(range(rows // 8)):
        s = b[g] + a[g] * carry
        out.append(s)
        carry = s[0:1]
    return jnp.concatenate(out[::-1], axis=0), carry


def rows_of(i, n):
    return pl.ds(pl.multiple_of(i * n, n), n)


def join_params(gs, prm, gains, sizes):
    y_size = sizes[2]
    for yy in range(y_size):
        prm[yy] = jnp.sum(gs[0, yy, :, :, 32:48, :].astype(F32), axis=(0, 1))
    d = gains.shape[1]
    for n in range(2):
        row = jnp.concatenate([prm[0, 8 + 3 * n + k : 9 + 3 * n + k, :] for k in range(3)], axis=1)
        gains[n : n + 1, :] = row[:, :d]


def head_weight(gs, yy, first):
    blocks = gs[0, yy, :, :, first : first + 16, :]
    return blocks.reshape(-1, blocks.shape[-1])


def transpose_into(dst, src, n, step=256):
    @pl.loop(0, n // step)
    def _(i):
        dst[:, rows_of(i, step)] = src[rows_of(i, step), :].T


class Scatter:
    def __init__(self, net, ref, flows, bufs, ss, rs, halves):
        self.net, self.ref, self.flows, self.bufs, self.ss, self.rs, self.halves = net, ref, flows, bufs, ss, rs, halves

    def rows(self, c):
        return chunk_rows(c, self.ref.shape[4]) if self.halves else slice(None)

    def slot(self, c):
        return SLOT[c // 2] if self.halves else c

    def copy(self, c, s, j, owner=None, slot=None, k=None):
        order = self.flows[c]
        d = order[s]
        at = dict(self.net.at)
        at[d] = self.net.shifted(d, j) if owner is None else owner
        idx = [at[e] if e in order[: s + 1] else slice(None) for e in "yzx"]
        k = self.net.off[d] + j - 1 if k is None else k
        return pltpu.make_async_remote_copy(
            src_ref=self.ref.at[(self.slot(c), *idx, self.rows(c))], dst_ref=self.bufs[c, s].at[j - 1 if slot is None else slot],
            send_sem=self.ss.at[c, k], recv_sem=self.rs.at[c, k],
            device_id=self.net.device(d, j), device_id_type=MESH)

    def relayed(self, c, s):
        return self.net.relay is not None and self.flows[c][s] == "z"

    def hops(self, c, s):
        return range(1, self.net.size[self.flows[c][s]])

    def far(self, c, s, act):
        z = self.net.at["z"]
        pl.when(z == 3)(lambda: act(self.copy(c, s, 3, 0, 3, self.net.relay)))
        pl.when(z == 0)(lambda: act(self.copy(c, s, 1, 3, 3, self.net.relay)))

    def sends(self, c, s, act):
        if not self.relayed(c, s):
            for j in self.hops(c, s):
                act(self.copy(c, s, j))
            return
        z = self.net.at["z"]
        self.far(c, s, act)
        pl.when(jnp.logical_or(z == 0, z == 3))(lambda: act(self.copy(c, s, 2)))
        pl.when(z != 3)(lambda: act(self.copy(c, s, 1)))
        pl.when(z != 0)(lambda: act(self.copy(c, s, 3)))

    def over(self, names, fn, place):
        if not names:
            fn(place)
        elif names[0] == "z":
            @pl.loop(0, self.net.size["z"])
            def _(z):
                self.over(names[1:], fn, {**place, "z": z})
        else:
            for n in range(self.net.size[names[0]]):
                self.over(names[1:], fn, {**place, names[0]: n})

    def pass_on(self, c, s):
        order = self.flows[c]
        rest = [e for e in "zyx" if e not in order[: s + 1]]
        buf = self.bufs[c, s]
        rows = self.rows(c)
        z = self.net.at["z"]

        def middle(owner):
            def fn():
                self.copy(c, s, 1, None, 3, self.net.relay).wait_recv()

                def block(place):
                    place = {**place, "z": owner}
                    idx = (self.slot(c), *[place[e] if e in place else self.net.at[e] for e in "yzx"], rows)
                    got = buf[(3, *[place[e] for e in "yzx" if e in rest])]
                    self.ref[idx] = (self.ref[idx].astype(F32) + got.astype(F32)).astype(BF)

                self.over(rest, block, {})
                self.copy(c, s, 2).start()
            return fn

        def end(unused):
            def fn():
                def block(place):
                    buf[(unused, *[place[e] for e in "yzx" if e in rest])] = jnp.zeros(buf.shape[-2:], BF)

                self.over(rest, block, {})
            return fn

        pl.when(z == 0)(end(0))
        pl.when(z == 1)(middle(3))
        pl.when(z == 2)(middle(0))
        pl.when(z == 3)(end(2))

    def add(self, c, s, out):
        order = self.flows[c]
        z = self.net.at["z"]
        for j in self.hops(c, s):
            take = self.copy(c, s, j).wait_recv
            if self.relayed(c, s) and j != 2:
                pl.when(z != (0 if j == 1 else 3))(take)
            else:
                take()
        rest = [e for e in "zyx" if e not in order[: s + 1]]
        buf = self.bufs[c, s]
        rows = self.rows(c)

        def block(place):
            idx = (self.slot(c), *[place[e] if e in place else self.net.at[e] for e in "yzx"], rows)
            total = self.ref[idx].astype(F32)
            for j in self.hops(c, s):
                total = total + buf[(j - 1, *[place[e] for e in "yzx" if e in place])].astype(F32)
            if s < 2:
                self.ref[idx] = total.astype(BF)
            elif self.halves:
                out.put(c // 2, rows, total)
            else:
                out[c] = total

        self.over(rest, block, {})

    def event(self, c, k, out):
        if self.rows(c) is None:
            return
        if k == 4:
            s = self.flows[c].index("z")
            if self.relayed(c, s):
                self.pass_on(c, s)
            return
        if k:
            self.add(c, k - 1, out)
        if k < 3:
            self.sends(c, k, lambda cp: cp.start())

    def drain(self, c):
        if self.rows(c) is None:
            return
        z = self.net.at["z"]
        for s in range(3):
            self.sends(c, s, lambda cp: cp.wait_send())
            if self.relayed(c, s):
                pl.when(jnp.logical_or(z == 1, z == 2))(lambda: self.copy(c, s, 2).wait_send())


def landing(flows, sizes, rows, ch):
    size = dict(zip("zxy", sizes))
    shapes = {}
    for c, order in enumerate(flows):
        n = rows(c)
        for s in range(3):
            if n:
                rest = [size[e] for e in "yzx" if e not in order[: s + 1]]
                places = 4 if order[s] == "z" and size["z"] == 4 else size[order[s]] - 1
                shapes[c, s] = (places, *rest, n, ch)
    return shapes


SLOT = {DN0: 9, DN1: 10, GA0: DN0, GA1: DN1, UP0: GA0, UP1: GA1, OUT: UP0, GEL: UP1, RNN: OUT}


def big_landing(sizes, part, ch):
    def rows(c):
        cut = chunk_rows(c, part)
        return 0 if cut is None else len(range(part)[cut])

    return landing(BACK, sizes, rows, ch)


def small_landing(sizes, ch):
    return landing(("yxz",), sizes, lambda c: SMALL, ch)


class Finals:
    def __init__(self, ref, out, sem):
        self.ref, self.out, self.sem, self.copies = ref, out, sem, []

    def copy(self, n):
        u, rows = self.copies[n]
        return pltpu.make_async_copy(self.ref.at[n % 2], self.out.at[u, rows], self.sem.at[n % 2])

    def put(self, u, rows, total):
        n = len(self.copies)
        self.copies.append((u, rows))
        if n >= 2:
            self.copy(n - 2).wait()
        self.ref[n % 2] = total
        self.copy(n).start()

    def drain(self):
        for n in range(max(0, len(self.copies) - 2), len(self.copies)):
            self.copy(n).wait()


def block_kernel(sizes, group,
                 tok, cot, w_rnn, w_gel, w_out, w_gate, w_up, w_down, small_in, rec_in, inp_in, prm_in, gains_in, hw_in,
                 o_block, o_gtok, o_gw, o_gs, h_cf, h_a, h_ri, h_cv,
                 W, gs, C6, LRU, T1, SA, N1, TT, MIX, PS, PR, AS, RS, FB, acc, pgain, pack, prm, gains, hw,
                 ss, rs, bss, brs, sss, srs, bsss, bsrs, ps, pr, ls, ts, fs, *landed):
    net = Net(*sizes)
    z_size, x_size, y_size = sizes
    c = net.at["c"]
    half = SEQ // 2
    ch = W.shape[-1]
    part = W.shape[4]
    depth = T1.shape[1]
    own, other = pl.ds(pl.multiple_of(c * half, half), half), pl.ds(pl.multiple_of((1 - c) * half, half), half)
    base_own, base_other = c * half, (1 - c) * half
    mine = (net.at["y"], net.at["z"], net.at["x"])
    dp_index = lax.axis_index("dp")

    sources = {RNN: w_rnn, GEL: w_gel, GA0: w_gate.at[:, 0:ch], GA1: w_gate.at[:, ch : 2 * ch], UP0: w_up.at[:, 0:ch],
               UP1: w_up.at[:, ch : 2 * ch]}
    place = {u: pltpu.make_async_copy(src, W.at[(u, *mine)], ls.at[u]) for u, src in sources.items()}
    place["tok"] = pltpu.make_async_copy(tok, T1.at[own], ls.at[OUT])
    place["cot"] = pltpu.make_async_copy(cot, SA.at[own], ls.at[DN0])
    for cp in place.values():
        cp.start()
    if group == 1:
        lanes = small_in[...].astype(F32)
        lanes = jnp.concatenate([lanes, jnp.zeros((16, 3 * ch - 128), F32)], axis=1)
        pack[...] = jnp.zeros_like(pack)
        pack[0:8, :] = pltpu.roll(lanes, dp_index * (ch // (z_size * x_size)), 1)[0:8, 0:ch]
        spread = pltpu.roll(lanes, dp_index * part, 1)
        for n in range(2):
            for k in range(3):
                pack[8 + 3 * n + k : 9 + 3 * n + k, :] = spread[8 + n : 9 + n, k * ch : (k + 1) * ch]
        gs[(0, *mine, slice(32, 48))] = pack[...].astype(BF)
        for n, src in enumerate((rec_in, inp_in)):
            for h in range(ch // 128):
                gs[(0, *mine, slice(16 * n, 16 * n + 16), slice(h * 128, (h + 1) * 128))] = src[h]
    if part % 128:
        W[(OUT, *mine)] = w_out[...]
        W[(DN0, *mine)] = w_down[:, :ch]
        W[(DN1, *mine)] = w_down[:, ch:]
    else:
        W[(OUT, *mine)] = w_out[...].T
        W[(DN0, *mine)] = w_down[:ch, :].T
        W[(DN1, *mine)] = w_down[ch:, :].T
    net.barrier()

    ag = Gather(net, W, FLOW, ss, rs, True)
    shapes = big_landing(sizes, part, ch)
    back = Scatter(net, W, BACK, dict(zip(shapes, landed)), bss, brs, True)
    small = back_small = None
    if group == 1:
        small = Gather(net, gs, ("zxy",), sss, srs, False)
        tail = landed[len(shapes):]
        back_small = Scatter(net, gs, ("yxz",), dict(zip(small_landing(sizes, ch), tail)), bsss, bsrs, False)

    tok_copy = pair_copy(net, tok, T1.at[own], ps, pr, 0)
    cot_copy = pair_copy(net, cot, SA.at[own], ps, pr, 1)
    tok_in = pair_copy(net, tok, T1.at[other], ps, pr, 0)
    cot_in = pair_copy(net, cot, SA.at[other], ps, pr, 1)
    mix_copy = pair_copy(net, PS, PR.at[0], ps, pr, 2)
    n2_copy = pair_copy(net, T1.at[own], T1.at[own], ps, pr, 3)
    n2_in = pair_copy(net, T1.at[other], T1.at[other], ps, pr, 3)
    back_copy = pair_copy(net, PS, PR.at[0], ps, pr, 4)
    row_copy = pair_copy(net, SA.at[own], SA.at[own], ps, pr, 5)
    row_in = pair_copy(net, SA.at[other], SA.at[other], ps, pr, 5)
    out_copy = pair_copy(net, PS, PR.at[1], ps, pr, 6)
    rnn_copy = pair_copy(net, PS, PR.at[0], ps, pr, 7)
    gain_copy = pair_copy(net, pgain.at[0:8], pgain.at[8:16], ps, pr, 8)
    cf_out = pltpu.make_async_copy(C6, h_cf, ls.at[9])
    cf_in = pltpu.make_async_copy(h_cf, C6, ls.at[10])
    cv_in = pltpu.make_async_copy(h_cv, LRU, ls.at[11])
    tok_again = pltpu.make_async_copy(tok, PR.at[1], ls.at[12])
    block_copy = pltpu.make_async_copy(PR.at[1], o_block, ls.at[13])

    if group == 1:
        small.event(0, 0)
    tok_copy.start()
    cot_copy.start()
    for u in sources:
        place[u].wait()

    def full(u):
        return jnp.concatenate([W[u, yy].reshape(depth, ch) for yy in range(y_size)], axis=1)

    finals = Finals(FB, o_gw, fs)


    def pre1():
        place["tok"].wait()
        place["cot"].wait()
        if group == 1:
            small.event(0, 4)
        cot_in.wait_recv()
        transpose_into(TT, SA, SEQ)

    def pre2():
        tok_in.wait_recv()
        if group == 1:
            small.event(0, 1)

    def pre25():
        if group == 1:
            small.event(0, 2)

    def pre3():
        if group == 1:
            small.event(0, 3)
            join_params(gs, prm, gains, sizes)
            for yy in range(y_size):
                for n in range(2):
                    hw[n, :, yy * ch : (yy + 1) * ch] = head_weight(gs, yy, 16 * n)
        else:
            prm[...] = prm_in[...]
            gains[...] = gains_in[...]
            hw[...] = hw_in[...]
        RS[1, 128:136, :] = jnp.zeros((8, y_size * ch), F32)

        @pl.loop(0, SEQ // 128)
        def _(i):
            v = T1[rows_of(i, 128), :].astype(F32)
            s = lax.rsqrt(jnp.mean(v * v, axis=1, keepdims=True) + EPS)
            N1[rows_of(i, 128), :] = (v * s * gains[0:1, :]).astype(BF)

    T = 128
    tiles = SEQ // T

    def kept(i, slot):
        return (pltpu.make_async_copy(AS.at[slot], h_a.at[i], ts.at[0, slot]),
                pltpu.make_async_copy(RS.at[slot], h_ri.at[i], ts.at[1, slot]),
                pltpu.make_async_copy(PS.at[rows_of(slot, T), 0 : y_size * ch], h_cv.at[rows_of(i, T)], ts.at[2, slot]))

    def branch(hook):
        def branch_tile(i, carries):
            hook(i)
            slot = lax.rem(i, 2)

            @pl.when(i >= 2)
            def _():
                for cp in kept(i - 2, slot):
                    cp.wait()

            RS[slot, 0:8, :] = RS[1 - slot, 128:136, :]
            RS[slot, 8:136, :] = nn(N1[rows_of(i, T), :], full(RNN))
            rows = rows_of(i, T)
            br = nn(N1[rows, :], full(GEL))
            new = []
            for yy in range(y_size):
                cols = slice(yy * ch, (yy + 1) * ch)
                p = prm[yy]
                x = RS[slot, :, cols]
                cv = p[4:5] + p[0:1] * x[8:]
                for k in range(1, 4):
                    cv = cv + p[k : k + 1] * pltpu.roll(x, k, 0)[8:]
                cv_low = cv.astype(BF)
                PS[pl.ds(pl.multiple_of(slot * T, T), T), cols] = cv_low
                cv = cv_low.astype(F32)
                rec, inp = [], []
                for h in range(ch // 128):
                    hc = slice(yy * ch + h * 128, yy * ch + (h + 1) * 128)
                    both = nn(cv_low[:, h * 128 : (h + 1) * 128], jnp.concatenate([hw[0, :, hc], hw[1, :, hc]], axis=1))
                    rec.append(both[:, :128])
                    inp.append(both[:, 128:])
                r = jax.nn.sigmoid(jnp.concatenate(rec, axis=1) + p[5:6])
                w = jax.nn.sigmoid(jnp.concatenate(inp, axis=1) + p[6:7])
                soft = jnp.log1p(jnp.exp(-jnp.abs(p[7:8]))) + jnp.maximum(p[7:8], 0.0)
                a = jnp.exp((-DECAY_SCALE * soft) * r)
                u = 1.0 - a * a + GUARD
                inv = lax.rsqrt(u)
                root = u * inv
                wc = w * cv
                state, last = scan_forward(a, root * wc, carries[yy])
                first = lax.broadcasted_iota(jnp.int32, (T, ch), 0) == 0
                prev = jnp.where(first, carries[yy], pltpu.roll(state, 1, 0))
                new.append(last)
                g, gp = gelu_parts(br[:, cols])
                LRU[rows, cols] = (state * g).astype(BF)
                cp = (prev - a * wc * inv) * a * r * (-DECAY_SCALE)
                AS[slot, :, cols] = a
                C6[0, rows, cols] = g.astype(BF)
                C6[1, rows, cols] = (state * gp).astype(BF)
                C6[2, rows, cols] = cp.astype(BF)
                C6[3, rows, cols] = (cp * soft * (1.0 - r)).astype(BF)
                C6[4, rows, cols] = (root * wc * (1.0 - w)).astype(BF)
                C6[5, rows, cols] = (root * w).astype(BF)
            for cp in kept(i, slot):
                cp.start()
            return tuple(new)

        lax.fori_loop(0, tiles, branch_tile, tuple(jnp.zeros((1, ch), F32) for _ in range(y_size)))
        cf_out.start()
        for i in (tiles - 2, tiles - 1):
            for cp in kept(i, i % 2):
                cp.wait()

    def out_rows(rows):
        return nt(LRU[rows, :], full(OUT))

    def out():
        PS[...] = out_rows(other).astype(BF)
        mix_copy.start()
        MIX[...] = out_rows(own)

    def mix():
        mix_copy.wait_recv()

        @pl.loop(0, half // T)
        def _(i):
            rows = rows_of(i, T)
            at = pl.ds(pl.multiple_of(base_own + i * T, T), T)
            v = T1[at, :].astype(F32) + MIX[rows, :] + PR[0, rows, :].astype(F32)
            MIX[rows, :] = v
            s = lax.rsqrt(jnp.mean(v * v, axis=1, keepdims=True) + EPS)
            T1[at, :] = (v * s * gains[1:2, :]).astype(BF)

        n2_copy.start()

    def n2():
        n2_in.wait_recv()
        cf_out.wait()

    F = 256

    def ff(j):
        def loop(hook):
            @pl.loop(0, SEQ // F)
            def _(i):
                hook(i)
                rows = rows_of(i, F)
                up = nn(T1[rows, :], full(UP[j]))
                g, gp = gelu_parts(nn(T1[rows, :], full(GATE[j])))
                C6[j, rows, :] = (g * up).astype(BF)
                C6[2 + j, rows, :] = (gp * up).astype(BF)
                C6[4 + j, rows, :] = g.astype(BF)
        return loop


    zh = z_size // 2

    def weight_grad(u, left, right):
        if SLOT[u] < UNITS:
            for chunk in (2 * SLOT[u], 2 * SLOT[u] + 1):
                ag.drain(chunk)

        @pl.loop(0, 2)
        def _(i):
            val = nn(left[rows_of(i, depth // 2), :], right[...]).astype(BF)
            for yy in range(y_size):
                W[SLOT[u], yy, pl.ds(i * zh, zh)] = val[:, yy * ch : (yy + 1) * ch].reshape(
                    zh, x_size, depth // (z_size * x_size), ch)

    def d0():
        weight_grad(DN0, TT, C6.at[0])

    def d1():
        weight_grad(DN1, TT, C6.at[1])

    def gh(hook):
        @pl.loop(0, 2 * (SEQ // F))
        def _(n):
            hook(n)
            j, i = n // (SEQ // F), lax.rem(n, SEQ // F)
            rows = rows_of(i, F)
            g = nn(SA[rows, :], full(DN0 + j))
            C6[2 + j, rows, :] = (g * C6[2 + j, rows, :].astype(F32)).astype(BF)
            C6[4 + j, rows, :] = (g * C6[4 + j, rows, :].astype(F32)).astype(BF)

    def span(base, i):
        return pl.ds(pl.multiple_of(base + i * F, F), F)

    def mlp_back(rows):
        return (nt(C6[2, rows, :], full(GA0)) + nt(C6[3, rows, :], full(GA1))
                + nt(C6[4, rows, :], full(UP0)) + nt(C6[5, rows, :], full(UP1)))

    def mlp_out(rows):
        return nt(C6[0, rows, :], full(DN0)) + nt(C6[1, rows, :], full(DN1))

    def rnn_back(rows):
        return nt(C6[5, rows, :], full(RNN)) + nt(C6[1, rows, :], full(GEL))

    def partial_rows(fn, base, dst, hook=None):
        @pl.loop(0, half // F)
        def _(i):
            if hook is not None:
                hook(i)
            dst[rows_of(i, F), :] = fn(span(base, i)).astype(dst.dtype)

    def bo():
        mix_copy.wait_send()
        partial_rows(mlp_out, base_other, PS)
        out_copy.start()

    def bw():
        partial_rows(mlp_out, base_own, o_gtok)

    def gno(hook):
        out_copy.wait_recv()

        @pl.loop(0, half // F)
        def _(i):
            rows = rows_of(i, F)
            PR[1, rows, :] = (MIX[rows, :] + o_gtok[rows, :] + PR[1, rows, :].astype(F32)).astype(BF)

        block_copy.start()
        out_copy.wait_send()
        partial_rows(mlp_back, base_other, PS, hook)
        back_copy.start()

    def gnw(hook):
        partial_rows(mlp_back, base_own, o_gtok, hook)

    def norm():
        acc[...] = jnp.zeros_like(acc)
        pgain[...] = jnp.zeros_like(pgain)
        n2_copy.wait_send()
        back_copy.wait_recv()

        @pl.loop(0, half // T)
        def _(i):
            rows = rows_of(i, T)
            at = pl.ds(pl.multiple_of(base_own + i * T, T), T)
            v = MIX[rows, :]
            gn = o_gtok[rows, :] + PR[0, rows, :].astype(F32)
            s = lax.rsqrt(jnp.mean(v * v, axis=1, keepdims=True) + EPS)
            q = gn * gains[1:2, :]
            pgain[1:2, :] += jnp.sum(gn * v * s, axis=0, keepdims=True)
            gm = SA[at, :].astype(F32) + s * q - (s * s * s) * v * jnp.mean(q * v, axis=1, keepdims=True)
            o_gtok[rows, :] = gm
            SA[at, :] = gm.astype(BF)

        row_copy.start()

    def ga0():
        transpose_into(TT, T1, SEQ)
        weight_grad(GA0, TT, C6.at[2])

    def ga1():
        weight_grad(GA1, TT, C6.at[3])

    def up0():
        weight_grad(UP0, TT, C6.at[4])

    def up1():
        weight_grad(UP1, TT, C6.at[5])
        cf_in.start()
        block_copy.wait()
        tok_again.start()

    def fetch(n, slot):
        i = tiles - 1 - n
        return (pltpu.make_async_copy(h_a.at[i], AS.at[slot], ts.at[0, slot]),
                pltpu.make_async_copy(h_ri.at[i], RS.at[slot], ts.at[1, slot]))

    def outg():
        for cp in fetch(0, 0):
            cp.start()
        row_in.wait_recv()
        transpose_into(TT, SA, SEQ)
        weight_grad(OUT, TT, LRU)
        cv_in.start()
        cf_in.wait()

    def back_rows(hook):
        def back_tile(n, carries):
            hook(n)
            slot = lax.rem(n, 2)
            for cp in fetch(n, slot):
                cp.wait()

            @pl.when(n + 1 < tiles)
            def _():
                for cp in fetch(n + 1, 1 - slot):
                    cp.start()

            i = tiles - 1 - n
            rows = rows_of(i, T)
            gl_all = nn(SA[rows, :], full(OUT))
            new = []
            for yy in range(y_size):
                adj_next, a_next, gco_next = carries[yy]
                cols = slice(yy * ch, (yy + 1) * ch)
                p = prm[yy]
                gl = gl_all[:, cols]
                at = AS[slot, :, cols]
                last = lax.broadcasted_iota(jnp.int32, (T, ch), 0) == T - 1
                shifted = jnp.where(last, a_next, pltpu.roll(at, T - 1, 0))
                adj, adj_first = scan_backward(shifted, gl * C6[0, rows, cols].astype(F32), adj_next)
                C6[1, rows, cols] = (gl * C6[1, rows, cols].astype(F32)).astype(BF)
                grp = adj * C6[3, rows, cols].astype(F32)
                gip = adj * C6[4, rows, cols].astype(F32)
                gr_low, gi_low = grp.astype(BF), gip.astype(BF)
                gcd = adj * C6[5, rows, cols].astype(F32)
                acc[yy, 5:6] += jnp.sum(grp, axis=0, keepdims=True)
                acc[yy, 6:7] += jnp.sum(gip, axis=0, keepdims=True)
                acc[yy, 7:8] += jnp.sum(adj * C6[2, rows, cols].astype(F32), axis=0, keepdims=True)
                C6[3, rows, cols] = gr_low
                C6[4, rows, cols] = gi_low
                parts = []
                for h in range(ch // 128):
                    hs = slice(h * 128, (h + 1) * 128)
                    hc = slice(yy * ch + h * 128, yy * ch + (h + 1) * 128)
                    parts.append(nt(jnp.concatenate([gr_low[:, hs], gi_low[:, hs]], axis=1),
                                    jnp.concatenate([hw[0, :, hc], hw[1, :, hc]], axis=1)))
                gco = gcd + jnp.concatenate(parts, axis=1)
                ext = jnp.concatenate([gco, gco_next], axis=0)
                x = RS[slot, :, cols]
                grn = p[0:1] * gco
                acc[yy, 0:1] += jnp.sum(gco * x[8:], axis=0, keepdims=True)
                acc[yy, 4:5] += jnp.sum(gco, axis=0, keepdims=True)
                for k in range(1, 4):
                    grn = grn + p[k : k + 1] * pltpu.roll(ext, T + 8 - k, 0)[:T]
                    acc[yy, k : k + 1] += jnp.sum(gco * pltpu.roll(x, k, 0)[8:], axis=0, keepdims=True)
                C6[5, rows, cols] = grn.astype(BF)
                new.append((adj_first, at[0:1], gco[0:8]))
            return tuple(new)

        zero = (jnp.zeros((1, ch), F32), jnp.zeros((1, ch), F32), jnp.zeros((8, ch), F32))
        lax.fori_loop(0, tiles, back_tile, (zero,) * y_size)

    def gel():
        transpose_into(TT, N1, SEQ)
        weight_grad(GEL, TT, C6.at[1])

    def rnn():
        weight_grad(RNN, TT, C6.at[5])

    def gn1o():
        back_copy.wait_send()
        partial_rows(rnn_back, base_other, PS)
        rnn_copy.start()

    def gn1w():
        partial_rows(rnn_back, base_own, MIX)

    def heads():
        cv_in.wait()
        if group == 1:
            small.drain(0)
        for yy in range(y_size):
            acc[yy, 7:8] = acc[yy, 7:8] * jax.nn.sigmoid(prm[yy, 7:8])
            for h in range(ch // 128):
                hs = slice(h * 128, (h + 1) * 128)
                hc = slice(yy * ch + h * 128, yy * ch + (h + 1) * 128)
                both = lax.dot_general(LRU[:, hc], jnp.concatenate([C6[3, :, hc], C6[4, :, hc]], axis=1),
                                       (((0,), (0,)), ((), ())), preferred_element_type=F32)
                for n in range(2):
                    val = both[:, n * 128 : (n + 1) * 128]
                    if group > 1:
                        o_gs[yy, 128 * n : 128 * n + 128, hs] = val
                    else:
                        gs[0, yy, :, :, 16 * n : 16 * n + 16, hs] = val.astype(BF).reshape(z_size, x_size, 16, 128)

    def fin():
        tok_again.wait()
        rnn_copy.wait_recv()

        @pl.loop(0, half // T)
        def _(i):
            rows = rows_of(i, T)
            v = PR[1, rows, :].astype(F32)
            gn = MIX[rows, :] + PR[0, rows, :].astype(F32)
            s = lax.rsqrt(jnp.mean(v * v, axis=1, keepdims=True) + EPS)
            q = gn * gains[0:1, :]
            pgain[0:1, :] += jnp.sum(gn * v * s, axis=0, keepdims=True)
            o_gtok[rows, :] += s * q - (s * s * s) * v * jnp.mean(q * v, axis=1, keepdims=True)

        gain_copy.start()

    def small_step(k):
        def fn():
            if k == 0:
                gain_copy.wait_recv()
                for n in range(2):
                    row = pgain[n : n + 1, :] + pgain[8 + n : 9 + n, :]
                    row = jnp.concatenate([row, jnp.zeros((1, 3 * ch - depth), F32)], axis=1)
                    for m in range(3):
                        for yy in range(y_size):
                            acc[yy, 8 + 3 * n + m : 9 + 3 * n + m, :] = row[:, m * ch : (m + 1) * ch]
                if group > 1:
                    for yy in range(y_size):
                        o_gs[yy, 256:272, :] = acc[yy]
                    return

                @pl.loop(0, z_size)
                def _(z):
                    for yy in range(y_size):
                        for xx in range(x_size):
                            gs[0, yy, z, xx, 32:48, :] = acc[yy].astype(BF)

            if group == 1:
                back_small.event(0, k, o_gs)
        return fn

    blocks = dict(pre1=pre1, pre2=pre2, pre25=pre25, pre3=pre3, out=out, mix=mix, n2=n2, d0=d0, d1=d1, bo=bo, bw=bw, ga0=ga0,
                  ga1=ga1, norm=norm, up0=up0, up1=up1, outg=outg, gel=gel, rnn=rnn, gn1o=gn1o, gn1w=gn1w, heads=heads,
                  fin=fin, s0=small_step(0), s1=small_step(1), s2=small_step(2), sr=small_step(4), s3=small_step(3))
    blocks = {name: (1, fn) for name, fn in blocks.items()}
    blocks.update(br=(tiles, branch), ffa=(SEQ // F, ff(0)), ffb=(SEQ // F, ff(1)), gh=(2 * SEQ // F, gh),
                  gno=(half // F, gno), gnw=(half // F, gnw), t=(tiles, back_rows))

    def event(chunk, k):
        if chunk < CHUNKS:
            ag.event(chunk, k)
        else:
            back.event(chunk - CHUNKS, k, finals)

    run_plan(PLAN, blocks, event)
    for u in (RNN, GEL):
        for chunk in (2 * u, 2 * u + 1):
            ag.drain(chunk)
    for chunk in range(CHUNKS):
        back.drain(chunk)
    if group == 1:
        back_small.drain(0)
    finals.drain()
    for cp in (tok_copy, cot_copy, row_copy, rnn_copy, gain_copy):
        cp.wait_send()


def finish_kernel(sizes, block_in, gtok_in, gw, gs,
                  o_block, o_gtok, o_mg, o_rnn, o_gel, o_cw, o_cb, o_rw, o_iw, o_rb, o_ib, o_dp, o_out, o_lg, o_gate, o_up,
                  o_down):
    ch = gw.shape[2]
    dp = sizes[0] * sizes[1]
    part, own = o_mg.shape[1], ch // dp
    dp_index = lax.axis_index("dp")
    o_block[...] = block_in[...]
    o_gtok[...] = gtok_in[...]
    o_rnn[...] = gw[RNN]
    o_gel[...] = gw[GEL]
    o_out[...] = gw[OUT].T
    for j in range(2):
        cols = slice(j * ch, (j + 1) * ch)
        o_gate[:, cols] = gw[GATE[j]]
        o_up[:, cols] = gw[UP[j]]
        o_down[cols, :] = gw[DOWN[j]].T
    for h in range(ch // 128):
        o_rw[h] = gs[0, 0:16, h * 128 : (h + 1) * 128]
        o_iw[h] = gs[0, 16:32, h * 128 : (h + 1) * 128]
    rows = pltpu.roll(gs[0, 32:40, :], ch - dp_index * own, 1)
    o_cw[...] = rows[0:4, 0:own]
    for k, ref in ((4, o_cb), (5, o_rb), (6, o_ib), (7, o_dp)):
        ref[...] = rows[k : k + 1, 0:own]
    for n, ref in ((0, o_mg), (1, o_lg)):
        row = jnp.concatenate([gs[0, 40 + 3 * n + k : 41 + 3 * n + k, :] for k in range(3)], axis=1)
        row = jnp.broadcast_to(row, (8, 3 * ch))
        ref[...] = pltpu.roll(row, 3 * ch - dp_index * part, 1)[0:1, 0:part]


def any_spec():
    return pl.BlockSpec(memory_space=pl.ANY)


def vmem_spec():
    return pl.BlockSpec(memory_space=pltpu.VMEM)


def body(sizes, tokens, mix_gain, rnn_weight, gelu_weight, conv_weight, conv_bias, recur_weight, input_weight,
         recur_bias, input_bias, decay_param, out_weight, mlp_gain, gate_weight, up_weight, down_weight, cotangent):
    z_size, x_size, y_size = sizes
    dp = z_size * x_size
    dp_index = lax.axis_index("dp")
    rows, depth = tokens.shape
    part, ch = rnn_weight.shape
    head_rows = recur_weight.shape[1]
    group = max(1, 16 // head_rows)
    wide = y_size * ch
    own = ch // dp
    small_in = jnp.concatenate([conv_weight, conv_bias[None], recur_bias[None], input_bias[None], decay_param[None]], axis=0)
    small_in = jnp.concatenate([jnp.pad(small_in, ((0, 0), (0, 128 - own))),
                                jnp.pad(jnp.stack([mix_gain, mlp_gain]), ((0, 6), (0, 128 - part)))], axis=0)
    heads = [recur_weight, input_weight]
    out_w, down_w = out_weight, down_weight
    if part % 128:
        out_w, down_w = out_weight.T, down_weight.T
    shape = jax.ShapeDtypeStruct
    grid = (y_size, z_size, x_size)
    hops = z_size + x_size + y_size - 2
    t = lax.axis_index("tensor")
    joined = [small_in] * 3
    if group > 1:
        lanes = jnp.pad(small_in[0:8, :own].astype(F32), ((0, 8), (0, ch - own)))
        lanes = jnp.roll(lanes, dp_index * own, axis=1)
        gain = jnp.pad(jnp.stack([mix_gain, mlp_gain]).astype(F32), ((0, 6), (0, depth - part)))
        gain = lax.psum(jnp.roll(gain, dp_index * part, axis=1), "dp")
        every = jnp.zeros((2 * y_size, 272, ch), F32)
        for n, w in enumerate(heads):
            w = jnp.transpose(w, (1, 0, 2)).reshape(1, head_rows, ch).astype(F32)
            every = lax.dynamic_update_slice(every, w, (t, 128 * n + dp_index * head_rows, 0))
        every = lax.psum(lax.dynamic_update_slice(every, lanes[None], (t, 256, 0)), ("dp", "tensor"))
        mine = [every[2 * yy] * (1 - lax.rem(t, 2)) + every[2 * yy + 1] * lax.rem(t, 2) for yy in range(y_size)]
        joined = [jnp.stack([m[256:] for m in mine]), gain,
                  jnp.concatenate([m[0:256].reshape(2, 128, ch) for m in mine], axis=2).astype(BF)]
        heads = [jnp.zeros((ch // 128, 16, 128), BF)] * 2
    dma = pltpu.SemaphoreType.DMA
    landed = list(big_landing(sizes, part, ch).values())
    gs_out, small_grid = (y_size, 272, ch), (1, 1, 1)
    if group == 1:
        landed += list(small_landing(sizes, ch).values())
        gs_out, small_grid = (1, SMALL, ch), grid
    block_out, grad_tokens, gw, gs = pl.pallas_call(
        functools.partial(block_kernel, sizes, group),
        out_shape=[shape((rows, depth), BF), shape((rows, depth), F32), shape((UNITS, part, ch), F32), shape(gs_out, F32),
                   shape((6, SEQ, wide), BF), shape((SEQ // 128, 128, wide), F32), shape((SEQ // 128, 136, wide), F32),
                   shape((SEQ, wide), BF)],
        in_specs=[any_spec(), any_spec(), any_spec(), any_spec(), vmem_spec(), any_spec(), any_spec(), vmem_spec(),
                  vmem_spec(), vmem_spec(), vmem_spec(), *([vmem_spec()] * 3 if group > 1 else [any_spec()] * 3)],
        out_specs=[any_spec(), vmem_spec(), any_spec(), vmem_spec()] + [any_spec()] * 4,
        scratch_shapes=[
            pltpu.VMEM((UNITS + 2, *grid, part, ch), BF), pltpu.VMEM((1, *small_grid, SMALL, ch), BF),
            pltpu.VMEM((6, SEQ, wide), BF), pltpu.VMEM((SEQ, wide), BF),
            *[pltpu.VMEM((SEQ, depth), BF)] * 4, pltpu.VMEM((rows, depth), F32),
            pltpu.VMEM((rows, depth), BF), pltpu.VMEM((2, rows, depth), BF),
            pltpu.VMEM((2, 128, wide), F32), pltpu.VMEM((2, 136, wide), F32),
            pltpu.VMEM((2, max(part // 2, 16), ch), F32),
            pltpu.VMEM((y_size, 16, ch), F32), pltpu.VMEM((16, depth), F32), pltpu.VMEM((16, ch), F32),
            pltpu.VMEM((y_size, 16, ch), F32), pltpu.VMEM((8, depth), F32), pltpu.VMEM((2, 128, wide), BF),
            dma((CHUNKS, hops)), dma((CHUNKS, hops)), dma((CHUNKS, hops)), dma((CHUNKS, hops)),
            dma((1, hops)), dma((1, hops)), dma((1, hops)), dma((1, hops)), dma((9,)), dma((9,)), dma((14,)), dma((3, 2)), dma((2,)),
            *[pltpu.VMEM(s, BF) for s in landed],
        ],
        compiler_params=pltpu.CompilerParams(collective_id=0, has_side_effects=True, vmem_limit_bytes=VMEM_LIMIT),
        name="residual_block",
    )(tokens, cotangent, rnn_weight, gelu_weight, out_w, gate_weight, up_weight, down_w, small_in, *heads, *joined)[:4]
    if group > 1:
        every = jnp.zeros((2 * y_size, 272, ch), F32)
        for yy in range(y_size):
            every = lax.dynamic_update_slice(every, gs[yy : yy + 1], (2 * yy + lax.rem(t, 2), 0, 0))
        gs = lax.dynamic_slice(lax.psum(every, ("dp", "tensor")), (t, 0, 0), (1, 272, ch))
        first = dp_index * head_rows
        rec = lax.dynamic_slice(gs[0], (first, 0), (head_rows, ch))
        inp = lax.dynamic_slice(gs[0], (128 + first, 0), (head_rows, ch))
        fill = jnp.zeros((16 - head_rows, ch), F32)
        gs = jnp.concatenate([rec, fill, inp, fill, gs[0, 256:]], axis=0)[None]
    f_shapes = [
        shape((rows, depth), BF), shape((rows, depth), F32), shape((1, part), F32), shape((part, ch), F32),
        shape((part, ch), F32), shape((4, own), F32), shape((1, own), F32), shape((ch // 128, 16, 128), F32),
        shape((ch // 128, 16, 128), F32), shape((1, own), F32), shape((1, own), F32), shape((1, own), F32),
        shape((ch, part), F32), shape((1, part), F32), shape((part, 2 * ch), F32), shape((part, 2 * ch), F32),
        shape((2 * ch, part), F32),
    ]
    res = list(pl.pallas_call(
        functools.partial(finish_kernel, sizes),
        out_shape=f_shapes,
        in_specs=[vmem_spec()] * 4,
        out_specs=[vmem_spec()] * 17,
        compiler_params=pltpu.CompilerParams(vmem_limit_bytes=VMEM_LIMIT),
        name="unpack",
    )(block_out, grad_tokens, gw, gs))
    for k in (2, 6, 9, 10, 11, 13):
        res[k] = res[k][0]
    for k in (7, 8):
        res[k] = res[k][:, :head_rows]
    return tuple(res)


def solution(mesh):
    dp, tensor = mesh.shape["dp"], mesh.shape["tensor"]
    x_size = 2
    sizes = (dp // x_size, x_size, tensor // 2)
    rows, split, vec = P(("dp", "tensor"), None), P("dp", "tensor"), P(("tensor", "dp"))
    head, flip, taps = P("tensor", "dp", None), P("tensor", "dp"), P(None, ("tensor", "dp"))
    return jax.shard_map(
        functools.partial(body, sizes),
        mesh=mesh,
        in_specs=(rows, P("dp"), split, split, taps, vec, head, head, vec, vec, vec, flip, P("dp"), split, split, flip,
                  rows),
        out_specs=(rows, rows, P("dp"), split, split, taps, vec, head, head, vec, vec, vec, flip, P("dp"), split, split,
                   flip),
        check_vma=False,
    )
```

```python
import functools

import jax
import jax.numpy as jnp
from jax import lax
from jax.experimental import pallas as pl
from jax.experimental.pallas import tpu as pltpu
from jax.sharding import PartitionSpec as P

SEQ = 1024
EPS = 1e-06
GUARD = 0.01
DECAY_SCALE = 8.0
GELU_K = 0.7978845608028654
GELU_C = 0.044715
BF = jnp.bfloat16
F32 = jnp.float32
MESH = pl.DeviceIdType.MESH
VMEM_LIMIT = 63 * 1024 * 1024

RNN, GEL, OUT, GA0, UP0, GA1, UP1, DN0, DN1 = range(9)
UNITS = 9
GATE, UP, DOWN = (GA0, GA1), (UP0, UP1), (DN0, DN1)
CHUNKS = 2 * UNITS
SMALL = 48
FLOW = (
    "zxy", "zxy", "zyx", "zyx", "zxy", "yzx", "xzy", "yzx", "zyx", "zyx", "xzy", "xzy", "yxz", "zyx", "zyx", "zyx",
    "xyz", "xzy",
)
BACK = (
    "xyz", "yxz", "xyz", "yzx", "xyz", "yzx", "xzy", "zyx", "yzx", "xyz", "yxz", "xzy", "xzy", "yxz", "zyx", "xyz",
    "zxy", "yzx",
)
SMALL_FLOW, SMALL_BACK = ("zxy",), ("xyz",)
PLAN = (
    0, 45, 60, "pre0", 25, 50, 80, 35, 30, 4, "pre1", 180, 81, 1, 49, 46, 10, 184, 15, 61, 20, 2, 181, 47, 5, 24, 85,
    55, 14, 65, 40, 19, 182, 9, 44, 11, 70, 36, 21, 41, 75, 16, 6, 12, 69, 48, 31, 39, 7, 183, 26, 66, 17, "pre3",
    13, 79, 34, 74, 42, 8, 22, 76, 56, 29, 3, 18, 32, 86, 51, "br", "br", 27, "br", "br", 37, "br", 59, 62, "br",
    "br", 57, "br", 43, 54, 33, 23, 28, 89, "out", 67, "mix", 77, 71, "n2", 82, 38, "ffa", 52, "ffa", 87, 64, "ffa",
    58, "ffa", 68, "d0", 160, 72, 165, 63, 53, "ffb", 84, 78, "ffb", "ffb", "ffb", 164, "d1", 170, 175, 88, 73, 83,
    "gh", "gh", "gh", "gh", "gh", "gh", "gh", "gh", "bo", "bw", "ga0", 120, 166, 174, 125, "ga1", "gno", 140, 145,
    161, "gno", "gnw", "gnw", "norm", 129, "up0", 167, 130, 176, 135, "up1", 169, 141, 155, 146, "outg", "t", 150,
    "t", "t", "t", 149, 121, 179, 110, 131, 115, "t", "t", "t", 168, 124, "t", 136, 151, "gel", 134, 105, "rnn", 100,
    95, "gn1o", "gn1w", 142, 154, "heads", 90, 144, 111, 156, 177, 137, 106, "fin", "s0", 116, 139, 91, 185, 119,
    109, 101, 147, 96, 126, 112, 171, 157, 143, 92, 132, 102, 148, 159, 162, 186, 152, 117, 94, 114, 97, 122, 187,
    127, 172, 133, 104, 113, 138, 163, 158, 178, 107, 99, 128, 93, 103, 153, 173, 189, 123, 108, 118, 98, 188,
)


def run_plan(plan, blocks, event):
    i = 0
    while i < len(plan):
        name = plan[i]
        i += 1
        if isinstance(name, int):
            event(name // 5, name % 5)
            continue
        turns, fn = blocks[name]
        if turns == 1:
            fn()
            continue
        hooks = {}
        for turn in range(1, turns):
            hooks[turn] = []
            while isinstance(plan[i], int):
                hooks[turn].append(plan[i])
                i += 1
            i += 1

        def hook(n, hooks=hooks):
            for turn, steps in hooks.items():
                if steps:
                    @pl.when(n == turn)
                    def _(steps=steps):
                        for step in steps:
                            event(step // 5, step % 5)

        fn(hook)


def nn(a, b):
    return jnp.dot(a, b, preferred_element_type=F32)


def nt(a, b):
    return lax.dot_general(a, b, (((1,), (1,)), ((), ())), preferred_element_type=F32)


def gelu_parts(v):
    v2 = v * v
    th = jnp.tanh(GELU_K * v * (1.0 + GELU_C * v2))
    half = 0.5 * (1.0 + th)
    return v * half, half + (0.5 * GELU_K) * v * (1.0 - th * th) * (1.0 + (3.0 * GELU_C) * v2)


class Net:
    def __init__(self, z_size, x_size, y_size):
        self.size = {"z": z_size, "x": x_size, "y": y_size, "c": 2}
        dp, t = lax.axis_index("dp"), lax.axis_index("tensor")
        self.at = {"z": dp // x_size, "x": lax.rem(dp, x_size), "y": t // 2, "c": lax.rem(t, 2)}
        self.off = {"z": 0, "x": z_size - 1, "y": z_size + x_size - 2}
        self.relay = z_size + x_size + y_size - 3 if z_size == 4 else None

    def shifted(self, d, j):
        n = self.size[d]
        return lax.rem(self.at[d] + (j % n), n)

    def device(self, d, j):
        at = dict(self.at)
        at[d] = self.shifted(d, j)
        return (at["z"] * self.size["x"] + at["x"], at["y"] * 2 + at["c"])

    def barrier(self):
        sem = pltpu.get_barrier_semaphore()
        count = 0
        for d in "zxyc":
            for j in range(1, self.size[d]):
                pl.semaphore_signal(sem, inc=1, device_id=self.device(d, j), device_id_type=MESH)
                count += 1
        pl.semaphore_wait(sem, count)


def chunk_rows(c, part):
    if part % 32:
        return slice(None) if c % 2 == 0 else None
    return slice(c % 2 * (part // 2), (c % 2 + 1) * (part // 2))


class Gather:
    def __init__(self, net, ref, flows, ss, rs, halves):
        self.net, self.ref, self.flows, self.ss, self.rs, self.halves = net, ref, flows, ss, rs, halves

    def region(self, c, s, at):
        order = self.flows[c]
        idx = [slice(None) if d in order[:s] else at[d] for d in "yzx"]
        if not self.halves:
            return self.ref.at[(c, *idx)]
        return self.ref.at[(c // 2, *idx, chunk_rows(c, self.ref.shape[4]))]

    def copy(self, c, s, j, sender, origin=None, send=None, recv=None):
        d = self.flows[c][s]
        at = dict(self.net.at)
        if sender:
            at[d] = self.net.shifted(d, -j)
        if origin is not None:
            at[d] = origin
        region = self.region(c, s, at)
        k = self.net.off[d] + j - 1
        return pltpu.make_async_remote_copy(
            src_ref=region, dst_ref=region, send_sem=self.ss.at[c, k if send is None else send],
            recv_sem=self.rs.at[c, k if recv is None else recv], device_id=self.net.device(d, j), device_id_type=MESH)

    def relayed(self, c, s):
        return self.net.relay is not None and self.flows[c][s] == "z"

    def sends(self, c, s, act):
        if not self.relayed(c, s):
            for j in range(1, self.net.size[self.flows[c][s]]):
                act(self.copy(c, s, j, False))
            return
        z = self.net.at["z"]
        act(self.copy(c, s, 2, False))
        pl.when(z != 3)(lambda: act(self.copy(c, s, 1, False)))
        pl.when(z != 0)(lambda: act(self.copy(c, s, 3, False)))

    def passes_on(self, c, s, act):
        z = self.net.at["z"]
        k = self.net.relay
        pl.when(z == 2)(lambda: act(self.copy(c, s, 1, False, 0, k, 2)))
        pl.when(z == 1)(lambda: act(self.copy(c, s, 3, False, 3, k, 0)))

    def event(self, c, k):
        if self.halves and chunk_rows(c, self.ref.shape[4]) is None:
            return
        if k == 4:
            s = self.flows[c].index("z")
            if self.relayed(c, s):
                self.copy(c, s, 2, True).wait_recv()
                self.passes_on(c, s, lambda cp: cp.start())
            return
        if k:
            for j in range(1, self.net.size[self.flows[c][k - 1]]):
                if not (self.relayed(c, k - 1) and j == 2):
                    self.copy(c, k - 1, j, True).wait_recv()
        if k < 3:
            self.sends(c, k, lambda cp: cp.start())

    def drain(self, c):
        if self.halves and chunk_rows(c, self.ref.shape[4]) is None:
            return
        for s in range(3):
            self.sends(c, s, lambda cp: cp.wait_send())
            if self.relayed(c, s):
                self.passes_on(c, s, lambda cp: cp.wait_send())


def pair_copy(net, src, dst, ss, rs, k):
    return pltpu.make_async_remote_copy(
        src_ref=src, dst_ref=dst, send_sem=ss.at[k], recv_sem=rs.at[k],
        device_id=net.device("c", 1), device_id_type=MESH)


def scan_forward(a, b, carry):
    rows, cols = a.shape
    a = a.reshape(rows // 8, 8, cols)
    b = b.reshape(rows // 8, 8, cols)
    place = lax.broadcasted_iota(jnp.int32, (rows // 8, 8, cols), 1)
    for k in (1, 2, 4):
        keep = place >= k
        b = b + a * jnp.where(keep, pltpu.roll(b, k, 1), 0.0)
        a = a * jnp.where(keep, pltpu.roll(a, k, 1), 1.0)
    out = []
    for g in range(rows // 8):
        s = b[g] + a[g] * carry
        out.append(s)
        carry = s[7:8]
    return jnp.concatenate(out, axis=0), carry


def scan_backward(a, b, carry):
    rows, cols = a.shape
    a = a.reshape(rows // 8, 8, cols)
    b = b.reshape(rows // 8, 8, cols)
    place = lax.broadcasted_iota(jnp.int32, (rows // 8, 8, cols), 1)
    for k in (1, 2, 4):
        keep = place < 8 - k
        b = b + a * jnp.where(keep, pltpu.roll(b, 8 - k, 1), 0.0)
        a = a * jnp.where(keep, pltpu.roll(a, 8 - k, 1), 1.0)
    out = []
    for g in reversed(range(rows // 8)):
        s = b[g] + a[g] * carry
        out.append(s)
        carry = s[0:1]
    return jnp.concatenate(out[::-1], axis=0), carry


def rows_of(i, n):
    return pl.ds(pl.multiple_of(i * n, n), n)


def join_params(gs, prm, gains, sizes):
    y_size = sizes[2]
    for yy in range(y_size):
        prm[yy] = jnp.sum(gs[0, yy, :, :, 32:48, :].astype(F32), axis=(0, 1))
    d = gains.shape[1]
    for n in range(2):
        row = jnp.concatenate([prm[0, 8 + 3 * n + k : 9 + 3 * n + k, :] for k in range(3)], axis=1)
        gains[n : n + 1, :] = row[:, :d]


def head_weight(gs, yy, first):
    blocks = gs[0, yy, :, :, first : first + 16, :]
    return blocks.reshape(-1, blocks.shape[-1])


def transpose_into(dst, src, n, step=256):
    @pl.loop(0, n // step)
    def _(i):
        dst[:, rows_of(i, step)] = src[rows_of(i, step), :].T


class Scatter:
    def __init__(self, net, ref, flows, bufs, ss, rs, halves):
        self.net, self.ref, self.flows, self.bufs, self.ss, self.rs, self.halves = net, ref, flows, bufs, ss, rs, halves

    def rows(self, c):
        return chunk_rows(c, self.ref.shape[4]) if self.halves else slice(None)

    def slot(self, c):
        return SLOT[c // 2] if self.halves else c

    def copy(self, c, s, j, owner=None, slot=None, k=None):
        order = self.flows[c]
        d = order[s]
        at = dict(self.net.at)
        at[d] = self.net.shifted(d, j) if owner is None else owner
        idx = [at[e] if e in order[: s + 1] else slice(None) for e in "yzx"]
        k = self.net.off[d] + j - 1 if k is None else k
        return pltpu.make_async_remote_copy(
            src_ref=self.ref.at[(self.slot(c), *idx, self.rows(c))], dst_ref=self.bufs[c, s].at[j - 1 if slot is None else slot],
            send_sem=self.ss.at[c, k], recv_sem=self.rs.at[c, k],
            device_id=self.net.device(d, j), device_id_type=MESH)

    def relayed(self, c, s):
        return self.net.relay is not None and self.flows[c][s] == "z"

    def hops(self, c, s):
        return range(1, self.net.size[self.flows[c][s]])

    def far(self, c, s, act):
        z = self.net.at["z"]
        pl.when(z == 3)(lambda: act(self.copy(c, s, 3, 0, 3, self.net.relay)))
        pl.when(z == 0)(lambda: act(self.copy(c, s, 1, 3, 3, self.net.relay)))

    def sends(self, c, s, act):
        if not self.relayed(c, s):
            for j in self.hops(c, s):
                act(self.copy(c, s, j))
            return
        z = self.net.at["z"]
        self.far(c, s, act)
        pl.when(jnp.logical_or(z == 0, z == 3))(lambda: act(self.copy(c, s, 2)))
        pl.when(z != 3)(lambda: act(self.copy(c, s, 1)))
        pl.when(z != 0)(lambda: act(self.copy(c, s, 3)))

    def over(self, names, fn, place):
        if not names:
            fn(place)
        elif names[0] == "z":
            @pl.loop(0, self.net.size["z"])
            def _(z):
                self.over(names[1:], fn, {**place, "z": z})
        else:
            for n in range(self.net.size[names[0]]):
                self.over(names[1:], fn, {**place, names[0]: n})

    def pass_on(self, c, s):
        order = self.flows[c]
        rest = [e for e in "zyx" if e not in order[: s + 1]]
        buf = self.bufs[c, s]
        rows = self.rows(c)
        z = self.net.at["z"]

        def middle(owner):
            def fn():
                self.copy(c, s, 1, None, 3, self.net.relay).wait_recv()

                def block(place):
                    place = {**place, "z": owner}
                    idx = (self.slot(c), *[place[e] if e in place else self.net.at[e] for e in "yzx"], rows)
                    got = buf[(3, *[place[e] for e in "yzx" if e in rest])]
                    self.ref[idx] = (self.ref[idx].astype(F32) + got.astype(F32)).astype(BF)

                self.over(rest, block, {})
                self.copy(c, s, 2).start()
            return fn

        def end(unused):
            def fn():
                def block(place):
                    buf[(unused, *[place[e] for e in "yzx" if e in rest])] = jnp.zeros(buf.shape[-2:], BF)

                self.over(rest, block, {})
            return fn

        pl.when(z == 0)(end(0))
        pl.when(z == 1)(middle(3))
        pl.when(z == 2)(middle(0))
        pl.when(z == 3)(end(2))

    def add(self, c, s, out):
        order = self.flows[c]
        z = self.net.at["z"]
        for j in self.hops(c, s):
            take = self.copy(c, s, j).wait_recv
            if self.relayed(c, s) and j != 2:
                pl.when(z != (0 if j == 1 else 3))(take)
            else:
                take()
        rest = [e for e in "zyx" if e not in order[: s + 1]]
        buf = self.bufs[c, s]
        rows = self.rows(c)

        def block(place):
            idx = (self.slot(c), *[place[e] if e in place else self.net.at[e] for e in "yzx"], rows)
            total = self.ref[idx].astype(F32)
            for j in self.hops(c, s):
                total = total + buf[(j - 1, *[place[e] for e in "yzx" if e in place])].astype(F32)
            if s < 2:
                self.ref[idx] = total.astype(BF)
            elif self.halves:
                out.put(c // 2, rows, total)
            else:
                out[c] = total

        self.over(rest, block, {})

    def event(self, c, k, out):
        if self.rows(c) is None:
            return
        if k == 4:
            s = self.flows[c].index("z")
            if self.relayed(c, s):
                self.pass_on(c, s)
            return
        if k:
            self.add(c, k - 1, out)
        if k < 3:
            self.sends(c, k, lambda cp: cp.start())

    def drain(self, c):
        if self.rows(c) is None:
            return
        z = self.net.at["z"]
        for s in range(3):
            self.sends(c, s, lambda cp: cp.wait_send())
            if self.relayed(c, s):
                pl.when(jnp.logical_or(z == 1, z == 2))(lambda: self.copy(c, s, 2).wait_send())


def landing(flows, sizes, rows, ch):
    size = dict(zip("zxy", sizes))
    shapes = {}
    for c, order in enumerate(flows):
        n = rows(c)
        for s in range(3):
            if n:
                rest = [size[e] for e in "yzx" if e not in order[: s + 1]]
                places = 4 if order[s] == "z" and size["z"] == 4 else size[order[s]] - 1
                shapes[c, s] = (places, *rest, n, ch)
    return shapes


SLOT = {DN0: 9, DN1: 10, GA0: DN0, GA1: DN1, UP0: GA0, UP1: GA1, OUT: UP0, GEL: UP1, RNN: OUT}


def big_landing(sizes, part, ch):
    def rows(c):
        cut = chunk_rows(c, part)
        return 0 if cut is None else len(range(part)[cut])

    return landing(BACK, sizes, rows, ch)


def small_landing(sizes, ch):
    return landing(SMALL_BACK, sizes, lambda c: SMALL, ch)


class Finals:
    def __init__(self, ref, out, sem):
        self.ref, self.out, self.sem, self.copies = ref, out, sem, []

    def copy(self, n):
        u, rows = self.copies[n]
        return pltpu.make_async_copy(self.ref.at[n % 2], self.out.at[u, rows], self.sem.at[n % 2])

    def put(self, u, rows, total):
        n = len(self.copies)
        self.copies.append((u, rows))
        if n >= 2:
            self.copy(n - 2).wait()
        self.ref[n % 2] = total
        self.copy(n).start()

    def drain(self):
        for n in range(max(0, len(self.copies) - 2), len(self.copies)):
            self.copy(n).wait()


def block_kernel(sizes, group,
                 tok, cot, w_rnn, w_gel, w_out, w_gate, w_up, w_down, small_in, rec_in, inp_in, prm_in, gains_in, hw_in,
                 o_block, o_gtok, o_gw, o_gs, h_cf, h_a, h_ri, h_cv,
                 W, gs, C6, LRU, T1, SA, N1, TT, MIX, PS, PR, gtok, AS, RS, FB, acc, pgain, pack, prm, gains, hw,
                 ss, rs, bss, brs, sss, srs, bsss, bsrs, ps, pr, ls, ts, fs, *landed):
    net = Net(*sizes)
    z_size, x_size, y_size = sizes
    c = net.at["c"]
    half = SEQ // 2
    ch = W.shape[-1]
    part = W.shape[4]
    depth = T1.shape[1]
    own, other = pl.ds(pl.multiple_of(c * half, half), half), pl.ds(pl.multiple_of((1 - c) * half, half), half)
    base_own, base_other = c * half, (1 - c) * half
    mine = (net.at["y"], net.at["z"], net.at["x"])
    dp_index = lax.axis_index("dp")

    sources = {RNN: w_rnn, GEL: w_gel, GA0: w_gate.at[:, 0:ch], GA1: w_gate.at[:, ch : 2 * ch], UP0: w_up.at[:, 0:ch],
               UP1: w_up.at[:, ch : 2 * ch]}
    place = {u: pltpu.make_async_copy(src, W.at[(u, *mine)], ls.at[u]) for u, src in sources.items()}
    place["tok"] = pltpu.make_async_copy(tok, T1.at[own], ls.at[OUT])
    place["cot"] = pltpu.make_async_copy(cot, SA.at[own], ls.at[DN0])
    for cp in place.values():
        cp.start()
    net.barrier()

    ag = Gather(net, W, FLOW, ss, rs, True)
    shapes = big_landing(sizes, part, ch)
    back = Scatter(net, W, BACK, dict(zip(shapes, landed)), bss, brs, True)
    small = back_small = None
    if group == 1:
        small = Gather(net, gs, SMALL_FLOW, sss, srs, False)
        tail = landed[len(shapes):]
        back_small = Scatter(net, gs, SMALL_BACK, dict(zip(small_landing(sizes, ch), tail)), bsss, bsrs, False)

    tok_copy = pair_copy(net, tok, T1.at[own], ps, pr, 0)
    cot_copy = pair_copy(net, cot, SA.at[own], ps, pr, 1)
    tok_in = pair_copy(net, tok, T1.at[other], ps, pr, 0)
    cot_in = pair_copy(net, cot, SA.at[other], ps, pr, 1)
    mix_copy = pair_copy(net, PS, PR.at[0], ps, pr, 2)
    n2_copy = pair_copy(net, T1.at[own], T1.at[own], ps, pr, 3)
    n2_in = pair_copy(net, T1.at[other], T1.at[other], ps, pr, 3)
    back_copy = pair_copy(net, PS, PR.at[0], ps, pr, 4)
    row_copy = pair_copy(net, SA.at[own], SA.at[own], ps, pr, 5)
    row_in = pair_copy(net, SA.at[other], SA.at[other], ps, pr, 5)
    out_copy = pair_copy(net, PS, PR.at[1], ps, pr, 6)
    rnn_copy = pair_copy(net, PS, PR.at[0], ps, pr, 7)
    gain_copy = pair_copy(net, pgain.at[0:8], pgain.at[8:16], ps, pr, 8)
    cf_out = pltpu.make_async_copy(C6, h_cf, ls.at[9])
    cf_in = pltpu.make_async_copy(h_cf, C6, ls.at[10])
    cv_in = pltpu.make_async_copy(h_cv, LRU, ls.at[11])
    tok_again = pltpu.make_async_copy(tok, PR.at[1], ls.at[12])
    block_copy = pltpu.make_async_copy(PR.at[1], o_block, ls.at[13])
    gtok_copy = pltpu.make_async_copy(gtok, o_gtok, ls.at[14])

    tok_copy.start()
    cot_copy.start()

    def full(u):
        return jnp.concatenate([W[u, yy].reshape(depth, ch) for yy in range(y_size)], axis=1)

    finals = Finals(FB, o_gw, fs)


    def pre0():
        if group == 1:
            lanes = small_in[...].astype(F32)
            lanes = jnp.concatenate([lanes, jnp.zeros((16, 3 * ch - 128), F32)], axis=1)
            pack[...] = jnp.zeros_like(pack)
            pack[0:8, :] = pltpu.roll(lanes, dp_index * (ch // (z_size * x_size)), 1)[0:8, 0:ch]
            spread = pltpu.roll(lanes, dp_index * part, 1)
            for n in range(2):
                for k in range(3):
                    pack[8 + 3 * n + k : 9 + 3 * n + k, :] = spread[8 + n : 9 + n, k * ch : (k + 1) * ch]
            gs[(0, *mine, slice(32, 48))] = pack[...].astype(BF)
            for n, src in enumerate((rec_in, inp_in)):
                for h in range(ch // 128):
                    gs[(0, *mine, slice(16 * n, 16 * n + 16), slice(h * 128, (h + 1) * 128))] = src[h]
        if part % 128:
            W[(OUT, *mine)] = w_out[...]
            W[(DN0, *mine)] = w_down[:, :ch]
            W[(DN1, *mine)] = w_down[:, ch:]
        else:
            W[(OUT, *mine)] = w_out[...].T
            W[(DN0, *mine)] = w_down[:ch, :].T
            W[(DN1, *mine)] = w_down[ch:, :].T
    def pre1():
        place["tok"].wait()
        place["cot"].wait()
        cot_in.wait_recv()
        transpose_into(TT, SA, SEQ)
        tok_in.wait_recv()

    def pre3():
        if group == 1:
            join_params(gs, prm, gains, sizes)
            for yy in range(y_size):
                for n in range(2):
                    hw[n, :, yy * ch : (yy + 1) * ch] = head_weight(gs, yy, 16 * n)
        else:
            prm[...] = prm_in[...]
            gains[...] = gains_in[...]
            hw[...] = hw_in[...]
        RS[1, 128:136, :] = jnp.zeros((8, y_size * ch), F32)

        @pl.loop(0, SEQ // 128)
        def _(i):
            v = T1[rows_of(i, 128), :].astype(F32)
            s = lax.rsqrt(jnp.mean(v * v, axis=1, keepdims=True) + EPS)
            N1[rows_of(i, 128), :] = (v * s * gains[0:1, :]).astype(BF)

    T = 128
    tiles = SEQ // T

    def kept(i, slot):
        return (pltpu.make_async_copy(AS.at[slot], h_a.at[i], ts.at[0, slot]),
                pltpu.make_async_copy(RS.at[slot], h_ri.at[i], ts.at[1, slot]),
                pltpu.make_async_copy(PS.at[rows_of(slot, T), 0 : y_size * ch], h_cv.at[rows_of(i, T)], ts.at[2, slot]))

    def branch(hook):
        def branch_tile(i, carries):
            hook(i)
            slot = lax.rem(i, 2)

            @pl.when(i >= 2)
            def _():
                for cp in kept(i - 2, slot):
                    cp.wait()

            RS[slot, 0:8, :] = RS[1 - slot, 128:136, :]
            RS[slot, 8:136, :] = nn(N1[rows_of(i, T), :], full(RNN))
            rows = rows_of(i, T)
            br = nn(N1[rows, :], full(GEL))
            new = []
            for yy in range(y_size):
                cols = slice(yy * ch, (yy + 1) * ch)
                p = prm[yy]
                x = RS[slot, :, cols]
                cv = p[4:5] + p[0:1] * x[8:]
                for k in range(1, 4):
                    cv = cv + p[k : k + 1] * pltpu.roll(x, k, 0)[8:]
                cv_low = cv.astype(BF)
                PS[pl.ds(pl.multiple_of(slot * T, T), T), cols] = cv_low
                cv = cv_low.astype(F32)
                rec, inp = [], []
                for h in range(ch // 128):
                    hc = slice(yy * ch + h * 128, yy * ch + (h + 1) * 128)
                    both = nn(cv_low[:, h * 128 : (h + 1) * 128], jnp.concatenate([hw[0, :, hc], hw[1, :, hc]], axis=1))
                    rec.append(both[:, :128])
                    inp.append(both[:, 128:])
                r = jax.nn.sigmoid(jnp.concatenate(rec, axis=1) + p[5:6])
                w = jax.nn.sigmoid(jnp.concatenate(inp, axis=1) + p[6:7])
                soft = jnp.log1p(jnp.exp(-jnp.abs(p[7:8]))) + jnp.maximum(p[7:8], 0.0)
                a = jnp.exp((-DECAY_SCALE * soft) * r)
                u = 1.0 - a * a + GUARD
                inv = lax.rsqrt(u)
                root = u * inv
                wc = w * cv
                state, last = scan_forward(a, root * wc, carries[yy])
                first = lax.broadcasted_iota(jnp.int32, (T, ch), 0) == 0
                prev = jnp.where(first, carries[yy], pltpu.roll(state, 1, 0))
                new.append(last)
                g, gp = gelu_parts(br[:, cols])
                LRU[rows, cols] = (state * g).astype(BF)
                cp = (prev - a * wc * inv) * a * r * (-DECAY_SCALE)
                AS[slot, :, cols] = a
                C6[0, rows, cols] = g.astype(BF)
                C6[1, rows, cols] = (state * gp).astype(BF)
                C6[2, rows, cols] = cp.astype(BF)
                C6[3, rows, cols] = (cp * soft * (1.0 - r)).astype(BF)
                C6[4, rows, cols] = (root * wc * (1.0 - w)).astype(BF)
                C6[5, rows, cols] = (root * w).astype(BF)
            for cp in kept(i, slot):
                cp.start()
            return tuple(new)

        lax.fori_loop(0, tiles, branch_tile, tuple(jnp.zeros((1, ch), F32) for _ in range(y_size)))
        cf_out.start()
        for i in (tiles - 2, tiles - 1):
            for cp in kept(i, i % 2):
                cp.wait()

    def out_rows(rows):
        return nt(LRU[rows, :], full(OUT))

    def out():
        PS[...] = out_rows(other).astype(BF)
        mix_copy.start()
        MIX[...] = out_rows(own)

    def mix():
        mix_copy.wait_recv()

        @pl.loop(0, half // T)
        def _(i):
            rows = rows_of(i, T)
            at = pl.ds(pl.multiple_of(base_own + i * T, T), T)
            v = T1[at, :].astype(F32) + MIX[rows, :] + PR[0, rows, :].astype(F32)
            MIX[rows, :] = v
            s = lax.rsqrt(jnp.mean(v * v, axis=1, keepdims=True) + EPS)
            T1[at, :] = (v * s * gains[1:2, :]).astype(BF)

        n2_copy.start()

    def n2():
        n2_in.wait_recv()
        cf_out.wait()

    F = 256

    def ff(j):
        def loop(hook):
            @pl.loop(0, SEQ // F)
            def _(i):
                hook(i)
                rows = rows_of(i, F)
                up = nn(T1[rows, :], full(UP[j]))
                g, gp = gelu_parts(nn(T1[rows, :], full(GATE[j])))
                C6[j, rows, :] = (g * up).astype(BF)
                C6[2 + j, rows, :] = (gp * up).astype(BF)
                C6[4 + j, rows, :] = g.astype(BF)
        return loop


    zh = z_size // 2

    def weight_grad(u, left, right):
        if SLOT[u] < UNITS:
            for chunk in (2 * SLOT[u], 2 * SLOT[u] + 1):
                ag.drain(chunk)

        @pl.loop(0, 2)
        def _(i):
            val = nn(left[rows_of(i, depth // 2), :], right[...]).astype(BF)
            for yy in range(y_size):
                W[SLOT[u], yy, pl.ds(i * zh, zh)] = val[:, yy * ch : (yy + 1) * ch].reshape(
                    zh, x_size, depth // (z_size * x_size), ch)

    def d0():
        weight_grad(DN0, TT, C6.at[0])

    def d1():
        weight_grad(DN1, TT, C6.at[1])

    def gh(hook):
        @pl.loop(0, 2 * (SEQ // F))
        def _(n):
            hook(n)
            j, i = n // (SEQ // F), lax.rem(n, SEQ // F)
            rows = rows_of(i, F)
            g = nn(SA[rows, :], full(DN0 + j))
            C6[2 + j, rows, :] = (g * C6[2 + j, rows, :].astype(F32)).astype(BF)
            C6[4 + j, rows, :] = (g * C6[4 + j, rows, :].astype(F32)).astype(BF)

    def span(base, i):
        return pl.ds(pl.multiple_of(base + i * F, F), F)

    def mlp_back(rows):
        return (nt(C6[2, rows, :], full(GA0)) + nt(C6[3, rows, :], full(GA1))
                + nt(C6[4, rows, :], full(UP0)) + nt(C6[5, rows, :], full(UP1)))

    def mlp_out(rows):
        return nt(C6[0, rows, :], full(DN0)) + nt(C6[1, rows, :], full(DN1))

    def rnn_back(rows):
        return nt(C6[5, rows, :], full(RNN)) + nt(C6[1, rows, :], full(GEL))

    def partial_rows(fn, base, dst, hook=None):
        @pl.loop(0, half // F)
        def _(i):
            if hook is not None:
                hook(i)
            dst[rows_of(i, F), :] = fn(span(base, i)).astype(dst.dtype)

    def bo():
        mix_copy.wait_send()
        partial_rows(mlp_out, base_other, PS)
        out_copy.start()

    def bw():
        partial_rows(mlp_out, base_own, gtok)

    def gno(hook):
        out_copy.wait_recv()

        @pl.loop(0, half // F)
        def _(i):
            rows = rows_of(i, F)
            PR[1, rows, :] = (MIX[rows, :] + gtok[rows, :] + PR[1, rows, :].astype(F32)).astype(BF)

        block_copy.start()
        out_copy.wait_send()
        partial_rows(mlp_back, base_other, PS, hook)
        back_copy.start()

    def gnw(hook):
        partial_rows(mlp_back, base_own, gtok, hook)

    def norm():
        acc[...] = jnp.zeros_like(acc)
        pgain[...] = jnp.zeros_like(pgain)
        n2_copy.wait_send()
        back_copy.wait_recv()

        @pl.loop(0, half // T)
        def _(i):
            rows = rows_of(i, T)
            at = pl.ds(pl.multiple_of(base_own + i * T, T), T)
            v = MIX[rows, :]
            gn = gtok[rows, :] + PR[0, rows, :].astype(F32)
            s = lax.rsqrt(jnp.mean(v * v, axis=1, keepdims=True) + EPS)
            q = gn * gains[1:2, :]
            pgain[1:2, :] += jnp.sum(gn * v * s, axis=0, keepdims=True)
            gm = SA[at, :].astype(F32) + s * q - (s * s * s) * v * jnp.mean(q * v, axis=1, keepdims=True)
            gtok[rows, :] = gm
            SA[at, :] = gm.astype(BF)

        row_copy.start()

    def ga0():
        transpose_into(TT, T1, SEQ)
        weight_grad(GA0, TT, C6.at[2])

    def ga1():
        weight_grad(GA1, TT, C6.at[3])

    def up0():
        weight_grad(UP0, TT, C6.at[4])

    def up1():
        weight_grad(UP1, TT, C6.at[5])
        cf_in.start()
        block_copy.wait()
        tok_again.start()

    def fetch(n, slot):
        i = tiles - 1 - n
        return (pltpu.make_async_copy(h_a.at[i], AS.at[slot], ts.at[0, slot]),
                pltpu.make_async_copy(h_ri.at[i], RS.at[slot], ts.at[1, slot]))

    def outg():
        for cp in fetch(0, 0):
            cp.start()
        row_in.wait_recv()
        transpose_into(TT, SA, SEQ)
        weight_grad(OUT, TT, LRU)
        cv_in.start()
        cf_in.wait()

    def back_rows(hook):
        def back_tile(n, carries):
            hook(n)
            slot = lax.rem(n, 2)
            for cp in fetch(n, slot):
                cp.wait()

            @pl.when(n + 1 < tiles)
            def _():
                for cp in fetch(n + 1, 1 - slot):
                    cp.start()

            i = tiles - 1 - n
            rows = rows_of(i, T)
            gl_all = nn(SA[rows, :], full(OUT))
            new = []
            for yy in range(y_size):
                adj_next, a_next, gco_next = carries[yy]
                cols = slice(yy * ch, (yy + 1) * ch)
                p = prm[yy]
                gl = gl_all[:, cols]
                at = AS[slot, :, cols]
                last = lax.broadcasted_iota(jnp.int32, (T, ch), 0) == T - 1
                shifted = jnp.where(last, a_next, pltpu.roll(at, T - 1, 0))
                adj, adj_first = scan_backward(shifted, gl * C6[0, rows, cols].astype(F32), adj_next)
                C6[1, rows, cols] = (gl * C6[1, rows, cols].astype(F32)).astype(BF)
                grp = adj * C6[3, rows, cols].astype(F32)
                gip = adj * C6[4, rows, cols].astype(F32)
                gr_low, gi_low = grp.astype(BF), gip.astype(BF)
                gcd = adj * C6[5, rows, cols].astype(F32)
                acc[yy, 5:6] += jnp.sum(grp, axis=0, keepdims=True)
                acc[yy, 6:7] += jnp.sum(gip, axis=0, keepdims=True)
                acc[yy, 7:8] += jnp.sum(adj * C6[2, rows, cols].astype(F32), axis=0, keepdims=True)
                C6[3, rows, cols] = gr_low
                C6[4, rows, cols] = gi_low
                parts = []
                for h in range(ch // 128):
                    hs = slice(h * 128, (h + 1) * 128)
                    hc = slice(yy * ch + h * 128, yy * ch + (h + 1) * 128)
                    parts.append(nt(jnp.concatenate([gr_low[:, hs], gi_low[:, hs]], axis=1),
                                    jnp.concatenate([hw[0, :, hc], hw[1, :, hc]], axis=1)))
                gco = gcd + jnp.concatenate(parts, axis=1)
                ext = jnp.concatenate([gco, gco_next], axis=0)
                x = RS[slot, :, cols]
                grn = p[0:1] * gco
                acc[yy, 0:1] += jnp.sum(gco * x[8:], axis=0, keepdims=True)
                acc[yy, 4:5] += jnp.sum(gco, axis=0, keepdims=True)
                for k in range(1, 4):
                    grn = grn + p[k : k + 1] * pltpu.roll(ext, T + 8 - k, 0)[:T]
                    acc[yy, k : k + 1] += jnp.sum(gco * pltpu.roll(x, k, 0)[8:], axis=0, keepdims=True)
                C6[5, rows, cols] = grn.astype(BF)
                new.append((adj_first, at[0:1], gco[0:8]))
            return tuple(new)

        zero = (jnp.zeros((1, ch), F32), jnp.zeros((1, ch), F32), jnp.zeros((8, ch), F32))
        lax.fori_loop(0, tiles, back_tile, (zero,) * y_size)

    def gel():
        transpose_into(TT, N1, SEQ)
        weight_grad(GEL, TT, C6.at[1])

    def rnn():
        weight_grad(RNN, TT, C6.at[5])

    def gn1o():
        back_copy.wait_send()
        partial_rows(rnn_back, base_other, PS)
        rnn_copy.start()

    def gn1w():
        partial_rows(rnn_back, base_own, MIX)

    def heads():
        cv_in.wait()
        if group == 1:
            small.drain(0)
        for yy in range(y_size):
            acc[yy, 7:8] = acc[yy, 7:8] * jax.nn.sigmoid(prm[yy, 7:8])
            for h in range(ch // 128):
                hs = slice(h * 128, (h + 1) * 128)
                hc = slice(yy * ch + h * 128, yy * ch + (h + 1) * 128)
                both = lax.dot_general(LRU[:, hc], jnp.concatenate([C6[3, :, hc], C6[4, :, hc]], axis=1),
                                       (((0,), (0,)), ((), ())), preferred_element_type=F32)
                for n in range(2):
                    val = both[:, n * 128 : (n + 1) * 128]
                    if group > 1:
                        o_gs[yy, 128 * n : 128 * n + 128, hs] = val
                    else:
                        gs[0, yy, :, :, 16 * n : 16 * n + 16, hs] = val.astype(BF).reshape(z_size, x_size, 16, 128)

    def fin():
        tok_again.wait()
        rnn_copy.wait_recv()

        @pl.loop(0, half // T)
        def _(i):
            rows = rows_of(i, T)
            v = PR[1, rows, :].astype(F32)
            gn = MIX[rows, :] + PR[0, rows, :].astype(F32)
            s = lax.rsqrt(jnp.mean(v * v, axis=1, keepdims=True) + EPS)
            q = gn * gains[0:1, :]
            pgain[0:1, :] += jnp.sum(gn * v * s, axis=0, keepdims=True)
            gtok[rows, :] += s * q - (s * s * s) * v * jnp.mean(q * v, axis=1, keepdims=True)

        gain_copy.start()
        gtok_copy.start()

    def s0():
        gain_copy.wait_recv()
        for n in range(2):
            row = pgain[n : n + 1, :] + pgain[8 + n : 9 + n, :]
            row = jnp.concatenate([row, jnp.zeros((1, 3 * ch - depth), F32)], axis=1)
            for m in range(3):
                for yy in range(y_size):
                    acc[yy, 8 + 3 * n + m : 9 + 3 * n + m, :] = row[:, m * ch : (m + 1) * ch]
        if group > 1:
            for yy in range(y_size):
                o_gs[yy, 256:272, :] = acc[yy]
            return

        @pl.loop(0, z_size)
        def _(z):
            for yy in range(y_size):
                for xx in range(x_size):
                    gs[0, yy, z, xx, 32:48, :] = acc[yy].astype(BF)

    blocks = dict(pre0=pre0, pre1=pre1, pre3=pre3, out=out, mix=mix, n2=n2, d0=d0, d1=d1, bo=bo, bw=bw, ga0=ga0,
                  ga1=ga1, norm=norm, up0=up0, up1=up1, outg=outg, gel=gel, rnn=rnn, gn1o=gn1o, gn1w=gn1w, heads=heads,
                  fin=fin, s0=s0)
    blocks = {name: (1, fn) for name, fn in blocks.items()}
    blocks.update(br=(tiles, branch), ffa=(SEQ // F, ff(0)), ffb=(SEQ // F, ff(1)), gh=(2 * SEQ // F, gh),
                  gno=(half // F, gno), gnw=(half // F, gnw), t=(tiles, back_rows))

    placed = set()

    def event(chunk, k):
        if chunk < CHUNKS:
            u = chunk // 2
            if k == 0 and u in sources and u not in placed:
                placed.add(u)
                place[u].wait()
            ag.event(chunk, k)
        elif chunk < 2 * CHUNKS:
            back.event(chunk - CHUNKS, k, finals)
        elif group == 1:
            if chunk == 2 * CHUNKS:
                small.event(0, k)
            else:
                back_small.event(0, k, o_gs)

    run_plan(PLAN, blocks, event)
    for u in (RNN, GEL):
        for chunk in (2 * u, 2 * u + 1):
            ag.drain(chunk)
    for chunk in range(CHUNKS):
        back.drain(chunk)
    if group == 1:
        back_small.drain(0)
    finals.drain()
    gtok_copy.wait()
    for cp in (tok_copy, cot_copy, row_copy, rnn_copy, gain_copy):
        cp.wait_send()


def finish_kernel(sizes, block_in, gtok_in, gw, gs,
                  o_block, o_gtok, o_mg, o_rnn, o_gel, o_cw, o_cb, o_rw, o_iw, o_rb, o_ib, o_dp, o_out, o_lg, o_gate, o_up,
                  o_down):
    ch = gw.shape[2]
    dp = sizes[0] * sizes[1]
    part, own = o_mg.shape[1], ch // dp
    dp_index = lax.axis_index("dp")
    o_block[...] = block_in[...]
    o_gtok[...] = gtok_in[...]
    o_rnn[...] = gw[RNN]
    o_gel[...] = gw[GEL]
    o_out[...] = gw[OUT].T
    for j in range(2):
        cols = slice(j * ch, (j + 1) * ch)
        o_gate[:, cols] = gw[GATE[j]]
        o_up[:, cols] = gw[UP[j]]
        o_down[cols, :] = gw[DOWN[j]].T
    for h in range(ch // 128):
        o_rw[h] = gs[0, 0:16, h * 128 : (h + 1) * 128]
        o_iw[h] = gs[0, 16:32, h * 128 : (h + 1) * 128]
    rows = pltpu.roll(gs[0, 32:40, :], ch - dp_index * own, 1)
    o_cw[...] = rows[0:4, 0:own]
    for k, ref in ((4, o_cb), (5, o_rb), (6, o_ib), (7, o_dp)):
        ref[...] = rows[k : k + 1, 0:own]
    for n, ref in ((0, o_mg), (1, o_lg)):
        row = jnp.concatenate([gs[0, 40 + 3 * n + k : 41 + 3 * n + k, :] for k in range(3)], axis=1)
        row = jnp.broadcast_to(row, (8, 3 * ch))
        ref[...] = pltpu.roll(row, 3 * ch - dp_index * part, 1)[0:1, 0:part]


def any_spec():
    return pl.BlockSpec(memory_space=pl.ANY)


def vmem_spec():
    return pl.BlockSpec(memory_space=pltpu.VMEM)


def body(sizes, tokens, mix_gain, rnn_weight, gelu_weight, conv_weight, conv_bias, recur_weight, input_weight,
         recur_bias, input_bias, decay_param, out_weight, mlp_gain, gate_weight, up_weight, down_weight, cotangent):
    z_size, x_size, y_size = sizes
    dp = z_size * x_size
    dp_index = lax.axis_index("dp")
    rows, depth = tokens.shape
    part, ch = rnn_weight.shape
    head_rows = recur_weight.shape[1]
    group = max(1, 16 // head_rows)
    wide = y_size * ch
    own = ch // dp
    small_in = jnp.concatenate([conv_weight, conv_bias[None], recur_bias[None], input_bias[None], decay_param[None]], axis=0)
    small_in = jnp.concatenate([jnp.pad(small_in, ((0, 0), (0, 128 - own))),
                                jnp.pad(jnp.stack([mix_gain, mlp_gain]), ((0, 6), (0, 128 - part)))], axis=0)
    heads = [recur_weight, input_weight]
    out_w, down_w = out_weight, down_weight
    if part % 128:
        out_w, down_w = out_weight.T, down_weight.T
    shape = jax.ShapeDtypeStruct
    grid = (y_size, z_size, x_size)
    hops = z_size + x_size + y_size - 2
    t = lax.axis_index("tensor")
    joined = [small_in] * 3
    if group > 1:
        lanes = jnp.pad(small_in[0:8, :own].astype(F32), ((0, 8), (0, ch - own)))
        lanes = jnp.roll(lanes, dp_index * own, axis=1)
        gain = jnp.pad(jnp.stack([mix_gain, mlp_gain]).astype(F32), ((0, 6), (0, depth - part)))
        gain = lax.psum(jnp.roll(gain, dp_index * part, axis=1), "dp")
        every = jnp.zeros((2 * y_size, 272, ch), F32)
        for n, w in enumerate(heads):
            w = jnp.transpose(w, (1, 0, 2)).reshape(1, head_rows, ch).astype(F32)
            every = lax.dynamic_update_slice(every, w, (t, 128 * n + dp_index * head_rows, 0))
        every = lax.psum(lax.dynamic_update_slice(every, lanes[None], (t, 256, 0)), ("dp", "tensor"))
        mine = [every[2 * yy] * (1 - lax.rem(t, 2)) + every[2 * yy + 1] * lax.rem(t, 2) for yy in range(y_size)]
        joined = [jnp.stack([m[256:] for m in mine]), gain,
                  jnp.concatenate([m[0:256].reshape(2, 128, ch) for m in mine], axis=2).astype(BF)]
        heads = [jnp.zeros((ch // 128, 16, 128), BF)] * 2
    dma = pltpu.SemaphoreType.DMA
    landed = list(big_landing(sizes, part, ch).values())
    gs_out, small_grid = (y_size, 272, ch), (1, 1, 1)
    if group == 1:
        landed += list(small_landing(sizes, ch).values())
        gs_out, small_grid = (1, SMALL, ch), grid
    block_out, grad_tokens, gw, gs = pl.pallas_call(
        functools.partial(block_kernel, sizes, group),
        out_shape=[shape((rows, depth), BF), shape((rows, depth), F32), shape((UNITS, part, ch), F32), shape(gs_out, F32),
                   shape((6, SEQ, wide), BF), shape((SEQ // 128, 128, wide), F32), shape((SEQ // 128, 136, wide), F32),
                   shape((SEQ, wide), BF)],
        in_specs=[any_spec(), any_spec(), any_spec(), any_spec(), vmem_spec(), any_spec(), any_spec(), vmem_spec(),
                  vmem_spec(), vmem_spec(), vmem_spec(), *([vmem_spec()] * 3 if group > 1 else [any_spec()] * 3)],
        out_specs=[any_spec(), any_spec(), any_spec(), vmem_spec()] + [any_spec()] * 4,
        scratch_shapes=[
            pltpu.VMEM((UNITS + 2, *grid, part, ch), BF), pltpu.VMEM((1, *small_grid, SMALL, ch), BF),
            pltpu.VMEM((6, SEQ, wide), BF), pltpu.VMEM((SEQ, wide), BF),
            *[pltpu.VMEM((SEQ, depth), BF)] * 4, pltpu.VMEM((rows, depth), F32),
            pltpu.VMEM((rows, depth), BF), pltpu.VMEM((2, rows, depth), BF),
            pltpu.VMEM((rows, depth), F32), pltpu.VMEM((2, 128, wide), F32), pltpu.VMEM((2, 136, wide), F32),
            pltpu.VMEM((2, max(part // 2, 16), ch), F32),
            pltpu.VMEM((y_size, 16, ch), F32), pltpu.VMEM((16, depth), F32), pltpu.VMEM((16, ch), F32),
            pltpu.VMEM((y_size, 16, ch), F32), pltpu.VMEM((8, depth), F32), pltpu.VMEM((2, 128, wide), BF),
            dma((CHUNKS, hops)), dma((CHUNKS, hops)), dma((CHUNKS, hops)), dma((CHUNKS, hops)),
            dma((1, hops)), dma((1, hops)), dma((1, hops)), dma((1, hops)), dma((9,)), dma((9,)), dma((15,)), dma((3, 2)), dma((2,)),
            *[pltpu.VMEM(s, BF) for s in landed],
        ],
        compiler_params=pltpu.CompilerParams(collective_id=0, has_side_effects=True, vmem_limit_bytes=VMEM_LIMIT),
        name="residual_block",
    )(tokens, cotangent, rnn_weight, gelu_weight, out_w, gate_weight, up_weight, down_w, small_in, *heads, *joined)[:4]
    if group > 1:
        every = jnp.zeros((2 * y_size, 272, ch), F32)
        for yy in range(y_size):
            every = lax.dynamic_update_slice(every, gs[yy : yy + 1], (2 * yy + lax.rem(t, 2), 0, 0))
        gs = lax.dynamic_slice(lax.psum(every, ("dp", "tensor")), (t, 0, 0), (1, 272, ch))
        first = dp_index * head_rows
        rec = lax.dynamic_slice(gs[0], (first, 0), (head_rows, ch))
        inp = lax.dynamic_slice(gs[0], (128 + first, 0), (head_rows, ch))
        fill = jnp.zeros((16 - head_rows, ch), F32)
        gs = jnp.concatenate([rec, fill, inp, fill, gs[0, 256:]], axis=0)[None]
    f_shapes = [
        shape((rows, depth), BF), shape((rows, depth), F32), shape((1, part), F32), shape((part, ch), F32),
        shape((part, ch), F32), shape((4, own), F32), shape((1, own), F32), shape((ch // 128, 16, 128), F32),
        shape((ch // 128, 16, 128), F32), shape((1, own), F32), shape((1, own), F32), shape((1, own), F32),
        shape((ch, part), F32), shape((1, part), F32), shape((part, 2 * ch), F32), shape((part, 2 * ch), F32),
        shape((2 * ch, part), F32),
    ]
    res = list(pl.pallas_call(
        functools.partial(finish_kernel, sizes),
        out_shape=f_shapes,
        in_specs=[vmem_spec()] * 4,
        out_specs=[vmem_spec()] * 17,
        compiler_params=pltpu.CompilerParams(vmem_limit_bytes=VMEM_LIMIT),
        name="unpack",
    )(block_out, grad_tokens, gw, gs))
    for k in (2, 6, 9, 10, 11, 13):
        res[k] = res[k][0]
    for k in (7, 8):
        res[k] = res[k][:, :head_rows]
    return tuple(res)


def solution(mesh):
    dp, tensor = mesh.shape["dp"], mesh.shape["tensor"]
    x_size = 2
    sizes = (dp // x_size, x_size, tensor // 2)
    rows, split, vec = P(("dp", "tensor"), None), P("dp", "tensor"), P(("tensor", "dp"))
    head, flip, taps = P("tensor", "dp", None), P("tensor", "dp"), P(None, ("tensor", "dp"))
    return jax.shard_map(
        functools.partial(body, sizes),
        mesh=mesh,
        in_specs=(rows, P("dp"), split, split, taps, vec, head, head, vec, vec, vec, flip, P("dp"), split, split, flip,
                  rows),
        out_specs=(rows, rows, P("dp"), split, split, taps, vec, head, head, vec, vec, vec, flip, P("dp"), split, split,
                   flip),
        check_vma=False,
    )
```

```python
import functools

import jax
import jax.numpy as jnp
from jax import lax
from jax.experimental import pallas as pl
from jax.experimental.pallas import tpu as pltpu
from jax.sharding import PartitionSpec as P

SEQ = 1024
EPS = 1e-06
GUARD = 0.01
DECAY_SCALE = 8.0
GELU_K = 0.7978845608028654
GELU_C = 0.044715
BF = jnp.bfloat16
F32 = jnp.float32
MESH = pl.DeviceIdType.MESH
VMEM_LIMIT = 63 * 1024 * 1024

RNN, GEL, OUT, GA0, UP0, GA1, UP1, DN0, DN1 = range(9)
UNITS = 9
GATE, UP, DOWN = (GA0, GA1), (UP0, UP1), (DN0, DN1)
CHUNKS = 2 * UNITS
SMALL = 48
FLOW = (
    "zxy", "zxy", "zyx", "zxy", "yzx", "zyx", "zxy", "zyx", "xyz", "xzy", "yxz", "zyx", "zxy", "yzx", "zxy", "xyz",
    "zyx", "zxy",
)
BACK = (
    "yxz", "yxz", "yxz", "xzy", "xzy", "xzy", "xzy", "yzx", "xyz", "yxz", "zyx", "xzy", "yxz", "yxz", "yxz", "zyx",
    "xyz", "zxy",
)
SMALL_FLOW, SMALL_BACK = ("zyx",), ("yxz",)
PLAN = (
    10, 50, 15, 40, "pre0", 51, 41, 14, 20, "pre1", 180, 75, 45, 11, 19, 16, 55, 184, 5, 76, 12, 35, 181, 65, 9, 6,
    17, 0, 39, 30, 36, 21, 182, 59, 4, 25, 7, 1, 37, 34, 29, 80, 24, 60, 26, 13, 46, 2, 56, 64, 31, 84, 183, 18, 85,
    38, 70, 27, "pre3", 66, 3, 74, 81, 8, 22, "br", 89, 49, 32, 42, "br", 47, 71, "br", 61, 57, 86, "br", 69, "br",
    52, 28, "br", "br", "br", 62, 44, 23, 67, "out", 48, 77, "mix", 72, 82, "n2", 43, 33, "ffa", "ffa", "ffa", 54,
    58, 63, 87, "ffa", "d0", 165, 160, 73, 53, 68, "ffb", "ffb", 79, "ffb", "ffb", "d1", 170, 88, 175, 169, 78, 83,
    "gh", "gh", "gh", "gh", "gh", "gh", "gh", "gh", "bo", 161, "bw", "ga0", 120, 125, 179, "ga1", 140, "gno", "gno",
    145, "gnw", 171, "gnw", "norm", "up0", 135, 130, 162, 144, "up1", "outg", 110, 126, "t", 150, "t", 164, "t", 121,
    "t", 115, "t", 155, 129, 131, 136, 124, 146, 172, "t", "t", 149, 111, "t", "gel", "rnn", 90, 116, 114, 156, 105,
    "gn1o", "gn1w", "heads", 100, 132, 119, 95, 174, "fin", "s0", 137, 157, 151, 101, 106, 134, 185, 133, 159, 147,
    141, 139, 91, 109, 152, 112, 117, 102, 96, 154, 166, 92, 186, 148, 176, 97, 122, 142, 94, 163, 104, 113, 158,
    173, 138, 127, 187, 107, 167, 93, 177, 99, 118, 103, 153, 123, 143, 189, 128, 108, 98, 178, 168, 188,
)


def run_plan(plan, blocks, event):
    i = 0
    while i < len(plan):
        name = plan[i]
        i += 1
        if isinstance(name, int):
            event(name // 5, name % 5)
            continue
        turns, fn = blocks[name]
        if turns == 1:
            fn()
            continue
        hooks = {}
        for turn in range(1, turns):
            hooks[turn] = []
            while isinstance(plan[i], int):
                hooks[turn].append(plan[i])
                i += 1
            i += 1

        def hook(n, hooks=hooks):
            for turn, steps in hooks.items():
                if steps:
                    @pl.when(n == turn)
                    def _(steps=steps):
                        for step in steps:
                            event(step // 5, step % 5)

        fn(hook)


def nn(a, b):
    return jnp.dot(a, b, preferred_element_type=F32)


def nt(a, b):
    return lax.dot_general(a, b, (((1,), (1,)), ((), ())), preferred_element_type=F32)


def gelu_parts(v):
    v2 = v * v
    th = jnp.tanh(GELU_K * v * (1.0 + GELU_C * v2))
    half = 0.5 * (1.0 + th)
    return v * half, half + (0.5 * GELU_K) * v * (1.0 - th * th) * (1.0 + (3.0 * GELU_C) * v2)


class Net:
    def __init__(self, z_size, x_size, y_size):
        self.size = {"z": z_size, "x": x_size, "y": y_size, "c": 2}
        dp, t = lax.axis_index("dp"), lax.axis_index("tensor")
        self.at = {"z": dp // x_size, "x": lax.rem(dp, x_size), "y": t // 2, "c": lax.rem(t, 2)}
        self.off = {"z": 0, "x": z_size - 1, "y": z_size + x_size - 2}
        self.relay = z_size + x_size + y_size - 3 if z_size == 4 else None

    def shifted(self, d, j):
        n = self.size[d]
        return lax.rem(self.at[d] + (j % n), n)

    def device(self, d, j):
        at = dict(self.at)
        at[d] = self.shifted(d, j)
        return (at["z"] * self.size["x"] + at["x"], at["y"] * 2 + at["c"])

    def barrier(self):
        sem = pltpu.get_barrier_semaphore()
        count = 0
        for d in "zxyc":
            for j in range(1, self.size[d]):
                pl.semaphore_signal(sem, inc=1, device_id=self.device(d, j), device_id_type=MESH)
                count += 1
        pl.semaphore_wait(sem, count)


def chunk_rows(c, part):
    if part % 32:
        return slice(None) if c % 2 == 0 else None
    return slice(c % 2 * (part // 2), (c % 2 + 1) * (part // 2))


class Gather:
    def __init__(self, net, ref, flows, ss, rs, halves):
        self.net, self.ref, self.flows, self.ss, self.rs, self.halves = net, ref, flows, ss, rs, halves

    def region(self, c, s, at):
        order = self.flows[c]
        idx = [slice(None) if d in order[:s] else at[d] for d in "yzx"]
        if not self.halves:
            return self.ref.at[(c, *idx)]
        return self.ref.at[(c // 2, *idx, chunk_rows(c, self.ref.shape[4]))]

    def copy(self, c, s, j, sender, origin=None, send=None, recv=None):
        d = self.flows[c][s]
        at = dict(self.net.at)
        if sender:
            at[d] = self.net.shifted(d, -j)
        if origin is not None:
            at[d] = origin
        region = self.region(c, s, at)
        k = self.net.off[d] + j - 1
        return pltpu.make_async_remote_copy(
            src_ref=region, dst_ref=region, send_sem=self.ss.at[c, k if send is None else send],
            recv_sem=self.rs.at[c, k if recv is None else recv], device_id=self.net.device(d, j), device_id_type=MESH)

    def relayed(self, c, s):
        return self.net.relay is not None and self.flows[c][s] == "z"

    def sends(self, c, s, act):
        if not self.relayed(c, s):
            for j in range(1, self.net.size[self.flows[c][s]]):
                act(self.copy(c, s, j, False))
            return
        z = self.net.at["z"]
        act(self.copy(c, s, 2, False))
        pl.when(z != 3)(lambda: act(self.copy(c, s, 1, False)))
        pl.when(z != 0)(lambda: act(self.copy(c, s, 3, False)))

    def passes_on(self, c, s, act):
        z = self.net.at["z"]
        k = self.net.relay
        pl.when(z == 2)(lambda: act(self.copy(c, s, 1, False, 0, k, 2)))
        pl.when(z == 1)(lambda: act(self.copy(c, s, 3, False, 3, k, 0)))

    def event(self, c, k):
        if self.halves and chunk_rows(c, self.ref.shape[4]) is None:
            return
        if k == 4:
            s = self.flows[c].index("z")
            if self.relayed(c, s):
                self.copy(c, s, 2, True).wait_recv()
                self.passes_on(c, s, lambda cp: cp.start())
            return
        if k:
            for j in range(1, self.net.size[self.flows[c][k - 1]]):
                if not (self.relayed(c, k - 1) and j == 2):
                    self.copy(c, k - 1, j, True).wait_recv()
        if k < 3:
            self.sends(c, k, lambda cp: cp.start())

    def drain(self, c):
        if self.halves and chunk_rows(c, self.ref.shape[4]) is None:
            return
        for s in range(3):
            self.sends(c, s, lambda cp: cp.wait_send())
            if self.relayed(c, s):
                self.passes_on(c, s, lambda cp: cp.wait_send())


def pair_copy(net, src, dst, ss, rs, k):
    return pltpu.make_async_remote_copy(
        src_ref=src, dst_ref=dst, send_sem=ss.at[k], recv_sem=rs.at[k],
        device_id=net.device("c", 1), device_id_type=MESH)


def scan_forward(a, b, carry):
    rows, cols = a.shape
    a = a.reshape(rows // 8, 8, cols)
    b = b.reshape(rows // 8, 8, cols)
    place = lax.broadcasted_iota(jnp.int32, (rows // 8, 8, cols), 1)
    for k in (1, 2, 4):
        keep = place >= k
        b = b + a * jnp.where(keep, pltpu.roll(b, k, 1), 0.0)
        a = a * jnp.where(keep, pltpu.roll(a, k, 1), 1.0)
    out = []
    for g in range(rows // 8):
        s = b[g] + a[g] * carry
        out.append(s)
        carry = s[7:8]
    return jnp.concatenate(out, axis=0), carry


def scan_backward(a, b, carry):
    rows, cols = a.shape
    a = a.reshape(rows // 8, 8, cols)
    b = b.reshape(rows // 8, 8, cols)
    place = lax.broadcasted_iota(jnp.int32, (rows // 8, 8, cols), 1)
    for k in (1, 2, 4):
        keep = place < 8 - k
        b = b + a * jnp.where(keep, pltpu.roll(b, 8 - k, 1), 0.0)
        a = a * jnp.where(keep, pltpu.roll(a, 8 - k, 1), 1.0)
    out = []
    for g in reversed(range(rows // 8)):
        s = b[g] + a[g] * carry
        out.append(s)
        carry = s[0:1]
    return jnp.concatenate(out[::-1], axis=0), carry


def rows_of(i, n):
    return pl.ds(pl.multiple_of(i * n, n), n)


def join_params(gs, prm, gains, sizes):
    y_size = sizes[2]
    for yy in range(y_size):
        prm[yy] = jnp.sum(gs[0, yy, :, :, 32:48, :].astype(F32), axis=(0, 1))
    d = gains.shape[1]
    for n in range(2):
        row = jnp.concatenate([prm[0, 8 + 3 * n + k : 9 + 3 * n + k, :] for k in range(3)], axis=1)
        gains[n : n + 1, :] = row[:, :d]


def head_weight(gs, yy, first):
    blocks = gs[0, yy, :, :, first : first + 16, :]
    return blocks.reshape(-1, blocks.shape[-1])


def transpose_into(dst, src, n, step=256):
    @pl.loop(0, n // step)
    def _(i):
        dst[:, rows_of(i, step)] = src[rows_of(i, step), :].T


class Scatter:
    def __init__(self, net, ref, flows, bufs, ss, rs, halves):
        self.net, self.ref, self.flows, self.bufs, self.ss, self.rs, self.halves = net, ref, flows, bufs, ss, rs, halves

    def rows(self, c):
        return chunk_rows(c, self.ref.shape[4]) if self.halves else slice(None)

    def slot(self, c):
        return SLOT[c // 2] if self.halves else c

    def copy(self, c, s, j, owner=None, slot=None, k=None):
        order = self.flows[c]
        d = order[s]
        at = dict(self.net.at)
        at[d] = self.net.shifted(d, j) if owner is None else owner
        idx = [at[e] if e in order[: s + 1] else slice(None) for e in "yzx"]
        k = self.net.off[d] + j - 1 if k is None else k
        return pltpu.make_async_remote_copy(
            src_ref=self.ref.at[(self.slot(c), *idx, self.rows(c))], dst_ref=self.bufs[c, s].at[j - 1 if slot is None else slot],
            send_sem=self.ss.at[c, k], recv_sem=self.rs.at[c, k],
            device_id=self.net.device(d, j), device_id_type=MESH)

    def relayed(self, c, s):
        return self.net.relay is not None and self.flows[c][s] == "z"

    def hops(self, c, s):
        return range(1, self.net.size[self.flows[c][s]])

    def far(self, c, s, act):
        z = self.net.at["z"]
        pl.when(z == 3)(lambda: act(self.copy(c, s, 3, 0, 3, self.net.relay)))
        pl.when(z == 0)(lambda: act(self.copy(c, s, 1, 3, 3, self.net.relay)))

    def sends(self, c, s, act):
        if not self.relayed(c, s):
            for j in self.hops(c, s):
                act(self.copy(c, s, j))
            return
        z = self.net.at["z"]
        self.far(c, s, act)
        pl.when(jnp.logical_or(z == 0, z == 3))(lambda: act(self.copy(c, s, 2)))
        pl.when(z != 3)(lambda: act(self.copy(c, s, 1)))
        pl.when(z != 0)(lambda: act(self.copy(c, s, 3)))

    def over(self, names, fn, place):
        if not names:
            fn(place)
        elif names[0] == "z":
            @pl.loop(0, self.net.size["z"])
            def _(z):
                self.over(names[1:], fn, {**place, "z": z})
        else:
            for n in range(self.net.size[names[0]]):
                self.over(names[1:], fn, {**place, names[0]: n})

    def pass_on(self, c, s):
        order = self.flows[c]
        rest = [e for e in "zyx" if e not in order[: s + 1]]
        buf = self.bufs[c, s]
        rows = self.rows(c)
        z = self.net.at["z"]

        def middle(owner):
            def fn():
                self.copy(c, s, 1, None, 3, self.net.relay).wait_recv()

                def block(place):
                    place = {**place, "z": owner}
                    idx = (self.slot(c), *[place[e] if e in place else self.net.at[e] for e in "yzx"], rows)
                    got = buf[(3, *[place[e] for e in "yzx" if e in rest])]
                    self.ref[idx] = (self.ref[idx].astype(F32) + got.astype(F32)).astype(BF)

                self.over(rest, block, {})
                self.copy(c, s, 2).start()
            return fn

        def end(unused):
            def fn():
                def block(place):
                    buf[(unused, *[place[e] for e in "yzx" if e in rest])] = jnp.zeros(buf.shape[-2:], BF)

                self.over(rest, block, {})
            return fn

        pl.when(z == 0)(end(0))
        pl.when(z == 1)(middle(3))
        pl.when(z == 2)(middle(0))
        pl.when(z == 3)(end(2))

    def add(self, c, s, out):
        order = self.flows[c]
        z = self.net.at["z"]
        for j in self.hops(c, s):
            take = self.copy(c, s, j).wait_recv
            if self.relayed(c, s) and j != 2:
                pl.when(z != (0 if j == 1 else 3))(take)
            else:
                take()
        rest = [e for e in "zyx" if e not in order[: s + 1]]
        buf = self.bufs[c, s]
        rows = self.rows(c)

        def block(place):
            idx = (self.slot(c), *[place[e] if e in place else self.net.at[e] for e in "yzx"], rows)
            total = self.ref[idx].astype(F32)
            for j in self.hops(c, s):
                total = total + buf[(j - 1, *[place[e] for e in "yzx" if e in place])].astype(F32)
            if s < 2:
                self.ref[idx] = total.astype(BF)
            elif self.halves:
                out.put(c // 2, rows, total)
            else:
                out[c] = total

        self.over(rest, block, {})

    def event(self, c, k, out):
        if self.rows(c) is None:
            return
        if k == 4:
            s = self.flows[c].index("z")
            if self.relayed(c, s):
                self.pass_on(c, s)
            return
        if k:
            self.add(c, k - 1, out)
        if k < 3:
            self.sends(c, k, lambda cp: cp.start())

    def drain(self, c):
        if self.rows(c) is None:
            return
        z = self.net.at["z"]
        for s in range(3):
            self.sends(c, s, lambda cp: cp.wait_send())
            if self.relayed(c, s):
                pl.when(jnp.logical_or(z == 1, z == 2))(lambda: self.copy(c, s, 2).wait_send())


def landing(flows, sizes, rows, ch):
    size = dict(zip("zxy", sizes))
    shapes = {}
    for c, order in enumerate(flows):
        n = rows(c)
        for s in range(3):
            if n:
                rest = [size[e] for e in "yzx" if e not in order[: s + 1]]
                places = 4 if order[s] == "z" and size["z"] == 4 else size[order[s]] - 1
                shapes[c, s] = (places, *rest, n, ch)
    return shapes


SLOT = {DN0: 9, DN1: 10, GA0: DN0, GA1: DN1, UP0: GA0, UP1: GA1, OUT: UP0, GEL: UP1, RNN: OUT}


def big_landing(sizes, part, ch):
    def rows(c):
        cut = chunk_rows(c, part)
        return 0 if cut is None else len(range(part)[cut])

    return landing(BACK, sizes, rows, ch)


def small_landing(sizes, ch):
    return landing(SMALL_BACK, sizes, lambda c: SMALL, ch)


class Finals:
    def __init__(self, ref, out, sem):
        self.ref, self.out, self.sem, self.copies = ref, out, sem, []

    def copy(self, n):
        u, rows = self.copies[n]
        return pltpu.make_async_copy(self.ref.at[n % 2], self.out.at[u, rows], self.sem.at[n % 2])

    def put(self, u, rows, total):
        n = len(self.copies)
        self.copies.append((u, rows))
        if n >= 2:
            self.copy(n - 2).wait()
        self.ref[n % 2] = total
        self.copy(n).start()

    def drain(self):
        for n in range(max(0, len(self.copies) - 2), len(self.copies)):
            self.copy(n).wait()


def block_kernel(sizes, group,
                 tok, cot, w_rnn, w_gel, out_h, w_gate, w_up, down_h, taps_in, cb_in, rb_in, ib_in, dp_in, mg_in, lg_in, rec_h, inp_h, prm_in, gains_in, hw_in,
                 o_block, o_gtok, o_gw, gs_h, h_cf, h_a, h_ri, h_cv,
                 W, gs, C6, LRU, T1, SA, N1, TT, MIX, PS, PR, gtok, AS, RS, FB, acc, pgain, pack, prm, gains, hw,
                 w_out, w_down, rec_in, inp_in, o_gs, taps,
                 ss, rs, bss, brs, sss, srs, bsss, bsrs, ps, pr, ls, ts, fs, *landed):
    net = Net(*sizes)
    z_size, x_size, y_size = sizes
    c = net.at["c"]
    half = SEQ // 2
    ch = W.shape[-1]
    part = W.shape[4]
    depth = T1.shape[1]
    own, other = pl.ds(pl.multiple_of(c * half, half), half), pl.ds(pl.multiple_of((1 - c) * half, half), half)
    base_own, base_other = c * half, (1 - c) * half
    mine = (net.at["y"], net.at["z"], net.at["x"])
    dp_index = lax.axis_index("dp")

    sources = {RNN: w_rnn, GEL: w_gel, GA0: w_gate.at[:, 0:ch], GA1: w_gate.at[:, ch : 2 * ch], UP0: w_up.at[:, 0:ch],
               UP1: w_up.at[:, ch : 2 * ch]}
    place = {u: pltpu.make_async_copy(src, W.at[(u, *mine)], ls.at[u]) for u, src in sources.items()}
    place["tok"] = pltpu.make_async_copy(tok, T1.at[own], ls.at[OUT])
    place["cot"] = pltpu.make_async_copy(cot, SA.at[own], ls.at[DN0])
    for n, (name, src, dst) in enumerate((("out", out_h, w_out), ("down", down_h, w_down), ("rec", rec_h, rec_in),
                                          ("inp", inp_h, inp_in))):
        place[name] = pltpu.make_async_copy(src, dst, ls.at[15 + n])
    for cp in place.values():
        cp.start()
    net.barrier()

    ag = Gather(net, W, FLOW, ss, rs, True)
    shapes = big_landing(sizes, part, ch)
    back = Scatter(net, W, BACK, dict(zip(shapes, landed)), bss, brs, True)
    small = back_small = None
    if group == 1:
        small = Gather(net, gs, SMALL_FLOW, sss, srs, False)
        tail = landed[len(shapes):]
        back_small = Scatter(net, gs, SMALL_BACK, dict(zip(small_landing(sizes, ch), tail)), bsss, bsrs, False)

    tok_copy = pair_copy(net, tok, T1.at[own], ps, pr, 0)
    cot_copy = pair_copy(net, cot, SA.at[own], ps, pr, 1)
    tok_in = pair_copy(net, tok, T1.at[other], ps, pr, 0)
    cot_in = pair_copy(net, cot, SA.at[other], ps, pr, 1)
    mix_copy = pair_copy(net, PS, PR.at[0], ps, pr, 2)
    n2_copy = pair_copy(net, T1.at[own], T1.at[own], ps, pr, 3)
    n2_in = pair_copy(net, T1.at[other], T1.at[other], ps, pr, 3)
    back_copy = pair_copy(net, PS, PR.at[0], ps, pr, 4)
    row_copy = pair_copy(net, SA.at[own], SA.at[own], ps, pr, 5)
    row_in = pair_copy(net, SA.at[other], SA.at[other], ps, pr, 5)
    out_copy = pair_copy(net, PS, PR.at[1], ps, pr, 6)
    rnn_copy = pair_copy(net, PS, PR.at[0], ps, pr, 7)
    gain_copy = pair_copy(net, pgain.at[0:8], pgain.at[8:16], ps, pr, 8)
    cf_out = pltpu.make_async_copy(C6, h_cf, ls.at[9])
    cf_in = pltpu.make_async_copy(h_cf, C6, ls.at[10])
    cv_in = pltpu.make_async_copy(h_cv, LRU, ls.at[11])
    tok_again = pltpu.make_async_copy(tok, PR.at[1], ls.at[12])
    block_copy = pltpu.make_async_copy(PR.at[1], o_block, ls.at[13])
    gtok_copy = pltpu.make_async_copy(gtok, o_gtok, ls.at[14])
    gs_copy = pltpu.make_async_copy(o_gs, gs_h, ls.at[8])

    tok_copy.start()
    cot_copy.start()

    def full(u):
        return jnp.concatenate([W[u, yy].reshape(depth, ch) for yy in range(y_size)], axis=1)

    finals = Finals(FB, o_gw, fs)


    def pre0():
        for name in ("out", "down", "rec", "inp"):
            place[name].wait()
        if group == 1:
            width = taps_in.shape[1]
            taps[...] = jnp.zeros_like(taps)
            taps[0:4, 0:width] = taps_in[...].astype(F32)
            for n, ref in enumerate((cb_in, rb_in, ib_in, dp_in)):
                taps[4 + n : 5 + n, 0:width] = ref[...].astype(F32)
            pack[...] = jnp.zeros_like(pack)
            pack[0:8, :] = pltpu.roll(taps[...], dp_index * (ch // (z_size * x_size)), 1)[0:8, 0:ch]
            taps[...] = jnp.zeros_like(taps)
            for n, ref in enumerate((mg_in, lg_in)):
                taps[n : n + 1, 0:part] = ref[...].astype(F32)
            spread = pltpu.roll(taps[...], dp_index * part, 1)
            for n in range(2):
                for k in range(3):
                    pack[8 + 3 * n + k : 9 + 3 * n + k, :] = spread[n : n + 1, k * ch : (k + 1) * ch]
            gs[(0, *mine, slice(32, 48))] = pack[...].astype(BF)
            for n, src in enumerate((rec_in, inp_in)):
                for h in range(ch // 128):
                    gs[(0, *mine, slice(16 * n, 16 * n + 16), slice(h * 128, (h + 1) * 128))] = src[h]
        if part % 128:
            W[(OUT, *mine)] = w_out[...]
            W[(DN0, *mine)] = w_down[:, :ch]
            W[(DN1, *mine)] = w_down[:, ch:]
        else:
            W[(OUT, *mine)] = w_out[...].T
            W[(DN0, *mine)] = w_down[:ch, :].T
            W[(DN1, *mine)] = w_down[ch:, :].T

    def pre1():
        place["tok"].wait()
        place["cot"].wait()
        cot_in.wait_recv()
        transpose_into(TT, SA, SEQ)
        tok_in.wait_recv()

    def pre3():
        if group == 1:
            join_params(gs, prm, gains, sizes)
            for yy in range(y_size):
                for n in range(2):
                    hw[n, :, yy * ch : (yy + 1) * ch] = head_weight(gs, yy, 16 * n)
        else:
            prm[...] = prm_in[...]
            gains[...] = gains_in[...]
            hw[...] = hw_in[...]
        RS[1, 128:136, :] = jnp.zeros((8, y_size * ch), F32)

        @pl.loop(0, SEQ // 128)
        def _(i):
            v = T1[rows_of(i, 128), :].astype(F32)
            s = lax.rsqrt(jnp.mean(v * v, axis=1, keepdims=True) + EPS)
            N1[rows_of(i, 128), :] = (v * s * gains[0:1, :]).astype(BF)

    T = 128
    tiles = SEQ // T

    def kept(i, slot):
        return (pltpu.make_async_copy(AS.at[slot], h_a.at[i], ts.at[0, slot]),
                pltpu.make_async_copy(RS.at[slot], h_ri.at[i], ts.at[1, slot]),
                pltpu.make_async_copy(PS.at[rows_of(slot, T), 0 : y_size * ch], h_cv.at[rows_of(i, T)], ts.at[2, slot]))

    def branch(hook):
        def branch_tile(i, carries):
            hook(i)
            slot = lax.rem(i, 2)

            @pl.when(i >= 2)
            def _():
                for cp in kept(i - 2, slot):
                    cp.wait()

            RS[slot, 0:8, :] = RS[1 - slot, 128:136, :]
            RS[slot, 8:136, :] = nn(N1[rows_of(i, T), :], full(RNN))
            rows = rows_of(i, T)
            br = nn(N1[rows, :], full(GEL))
            new = []
            for yy in range(y_size):
                cols = slice(yy * ch, (yy + 1) * ch)
                p = prm[yy]
                x = RS[slot, :, cols]
                cv = p[4:5] + p[0:1] * x[8:]
                for k in range(1, 4):
                    cv = cv + p[k : k + 1] * pltpu.roll(x, k, 0)[8:]
                cv_low = cv.astype(BF)
                PS[pl.ds(pl.multiple_of(slot * T, T), T), cols] = cv_low
                cv = cv_low.astype(F32)
                rec, inp = [], []
                for h in range(ch // 128):
                    hc = slice(yy * ch + h * 128, yy * ch + (h + 1) * 128)
                    both = nn(cv_low[:, h * 128 : (h + 1) * 128], jnp.concatenate([hw[0, :, hc], hw[1, :, hc]], axis=1))
                    rec.append(both[:, :128])
                    inp.append(both[:, 128:])
                r = jax.nn.sigmoid(jnp.concatenate(rec, axis=1) + p[5:6])
                w = jax.nn.sigmoid(jnp.concatenate(inp, axis=1) + p[6:7])
                soft = jnp.log1p(jnp.exp(-jnp.abs(p[7:8]))) + jnp.maximum(p[7:8], 0.0)
                a = jnp.exp((-DECAY_SCALE * soft) * r)
                u = 1.0 - a * a + GUARD
                inv = lax.rsqrt(u)
                root = u * inv
                wc = w * cv
                state, last = scan_forward(a, root * wc, carries[yy])
                first = lax.broadcasted_iota(jnp.int32, (T, ch), 0) == 0
                prev = jnp.where(first, carries[yy], pltpu.roll(state, 1, 0))
                new.append(last)
                g, gp = gelu_parts(br[:, cols])
                LRU[rows, cols] = (state * g).astype(BF)
                cp = (prev - a * wc * inv) * a * r * (-DECAY_SCALE)
                AS[slot, :, cols] = a
                C6[0, rows, cols] = g.astype(BF)
                C6[1, rows, cols] = (state * gp).astype(BF)
                C6[2, rows, cols] = cp.astype(BF)
                C6[3, rows, cols] = (cp * soft * (1.0 - r)).astype(BF)
                C6[4, rows, cols] = (root * wc * (1.0 - w)).astype(BF)
                C6[5, rows, cols] = (root * w).astype(BF)
            for cp in kept(i, slot):
                cp.start()
            return tuple(new)

        lax.fori_loop(0, tiles, branch_tile, tuple(jnp.zeros((1, ch), F32) for _ in range(y_size)))
        cf_out.start()
        for i in (tiles - 2, tiles - 1):
            for cp in kept(i, i % 2):
                cp.wait()

    def out_rows(rows):
        return nt(LRU[rows, :], full(OUT))

    def out():
        PS[...] = out_rows(other).astype(BF)
        mix_copy.start()
        MIX[...] = out_rows(own)

    def mix():
        mix_copy.wait_recv()

        @pl.loop(0, half // T)
        def _(i):
            rows = rows_of(i, T)
            at = pl.ds(pl.multiple_of(base_own + i * T, T), T)
            v = T1[at, :].astype(F32) + MIX[rows, :] + PR[0, rows, :].astype(F32)
            MIX[rows, :] = v
            s = lax.rsqrt(jnp.mean(v * v, axis=1, keepdims=True) + EPS)
            T1[at, :] = (v * s * gains[1:2, :]).astype(BF)

        n2_copy.start()

    def n2():
        n2_in.wait_recv()
        cf_out.wait()

    F = 256

    def ff(j):
        def loop(hook):
            @pl.loop(0, SEQ // F)
            def _(i):
                hook(i)
                rows = rows_of(i, F)
                up = nn(T1[rows, :], full(UP[j]))
                g, gp = gelu_parts(nn(T1[rows, :], full(GATE[j])))
                C6[j, rows, :] = (g * up).astype(BF)
                C6[2 + j, rows, :] = (gp * up).astype(BF)
                C6[4 + j, rows, :] = g.astype(BF)
        return loop


    zh = z_size // 2

    def weight_grad(u, left, right):
        if SLOT[u] < UNITS:
            for chunk in (2 * SLOT[u], 2 * SLOT[u] + 1):
                ag.drain(chunk)

        @pl.loop(0, 2)
        def _(i):
            val = nn(left[rows_of(i, depth // 2), :], right[...]).astype(BF)
            for yy in range(y_size):
                W[SLOT[u], yy, pl.ds(i * zh, zh)] = val[:, yy * ch : (yy + 1) * ch].reshape(
                    zh, x_size, depth // (z_size * x_size), ch)

    def d0():
        weight_grad(DN0, TT, C6.at[0])

    def d1():
        weight_grad(DN1, TT, C6.at[1])

    def gh(hook):
        @pl.loop(0, 2 * (SEQ // F))
        def _(n):
            hook(n)
            j, i = n // (SEQ // F), lax.rem(n, SEQ // F)
            rows = rows_of(i, F)
            g = nn(SA[rows, :], full(DN0 + j))
            C6[2 + j, rows, :] = (g * C6[2 + j, rows, :].astype(F32)).astype(BF)
            C6[4 + j, rows, :] = (g * C6[4 + j, rows, :].astype(F32)).astype(BF)

    def span(base, i):
        return pl.ds(pl.multiple_of(base + i * F, F), F)

    def mlp_back(rows):
        return (nt(C6[2, rows, :], full(GA0)) + nt(C6[3, rows, :], full(GA1))
                + nt(C6[4, rows, :], full(UP0)) + nt(C6[5, rows, :], full(UP1)))

    def mlp_out(rows):
        return nt(C6[0, rows, :], full(DN0)) + nt(C6[1, rows, :], full(DN1))

    def rnn_back(rows):
        return nt(C6[5, rows, :], full(RNN)) + nt(C6[1, rows, :], full(GEL))

    def partial_rows(fn, base, dst, hook=None):
        @pl.loop(0, half // F)
        def _(i):
            if hook is not None:
                hook(i)
            dst[rows_of(i, F), :] = fn(span(base, i)).astype(dst.dtype)

    def bo():
        mix_copy.wait_send()
        partial_rows(mlp_out, base_other, PS)
        out_copy.start()

    def bw():
        partial_rows(mlp_out, base_own, gtok)

    def gno(hook):
        out_copy.wait_recv()

        @pl.loop(0, half // F)
        def _(i):
            rows = rows_of(i, F)
            PR[1, rows, :] = (MIX[rows, :] + gtok[rows, :] + PR[1, rows, :].astype(F32)).astype(BF)

        block_copy.start()
        out_copy.wait_send()
        partial_rows(mlp_back, base_other, PS, hook)
        back_copy.start()

    def gnw(hook):
        partial_rows(mlp_back, base_own, gtok, hook)

    def norm():
        acc[...] = jnp.zeros_like(acc)
        pgain[...] = jnp.zeros_like(pgain)
        n2_copy.wait_send()
        back_copy.wait_recv()

        @pl.loop(0, half // T)
        def _(i):
            rows = rows_of(i, T)
            at = pl.ds(pl.multiple_of(base_own + i * T, T), T)
            v = MIX[rows, :]
            gn = gtok[rows, :] + PR[0, rows, :].astype(F32)
            s = lax.rsqrt(jnp.mean(v * v, axis=1, keepdims=True) + EPS)
            q = gn * gains[1:2, :]
            pgain[1:2, :] += jnp.sum(gn * v * s, axis=0, keepdims=True)
            gm = SA[at, :].astype(F32) + s * q - (s * s * s) * v * jnp.mean(q * v, axis=1, keepdims=True)
            gtok[rows, :] = gm
            SA[at, :] = gm.astype(BF)

        row_copy.start()

    def ga0():
        transpose_into(TT, T1, SEQ)
        weight_grad(GA0, TT, C6.at[2])

    def ga1():
        weight_grad(GA1, TT, C6.at[3])

    def up0():
        weight_grad(UP0, TT, C6.at[4])

    def up1():
        weight_grad(UP1, TT, C6.at[5])
        cf_in.start()
        block_copy.wait()
        tok_again.start()

    def fetch(n, slot):
        i = tiles - 1 - n
        return (pltpu.make_async_copy(h_a.at[i], AS.at[slot], ts.at[0, slot]),
                pltpu.make_async_copy(h_ri.at[i], RS.at[slot], ts.at[1, slot]))

    def outg():
        for cp in fetch(0, 0):
            cp.start()
        row_in.wait_recv()
        transpose_into(TT, SA, SEQ)
        weight_grad(OUT, TT, LRU)
        cv_in.start()
        cf_in.wait()

    def back_rows(hook):
        def back_tile(n, carries):
            hook(n)
            slot = lax.rem(n, 2)
            for cp in fetch(n, slot):
                cp.wait()

            @pl.when(n + 1 < tiles)
            def _():
                for cp in fetch(n + 1, 1 - slot):
                    cp.start()

            i = tiles - 1 - n
            rows = rows_of(i, T)
            gl_all = nn(SA[rows, :], full(OUT))
            new = []
            for yy in range(y_size):
                adj_next, a_next, gco_next = carries[yy]
                cols = slice(yy * ch, (yy + 1) * ch)
                p = prm[yy]
                gl = gl_all[:, cols]
                at = AS[slot, :, cols]
                last = lax.broadcasted_iota(jnp.int32, (T, ch), 0) == T - 1
                shifted = jnp.where(last, a_next, pltpu.roll(at, T - 1, 0))
                adj, adj_first = scan_backward(shifted, gl * C6[0, rows, cols].astype(F32), adj_next)
                C6[1, rows, cols] = (gl * C6[1, rows, cols].astype(F32)).astype(BF)
                grp = adj * C6[3, rows, cols].astype(F32)
                gip = adj * C6[4, rows, cols].astype(F32)
                gr_low, gi_low = grp.astype(BF), gip.astype(BF)
                gcd = adj * C6[5, rows, cols].astype(F32)
                acc[yy, 5:6] += jnp.sum(grp, axis=0, keepdims=True)
                acc[yy, 6:7] += jnp.sum(gip, axis=0, keepdims=True)
                acc[yy, 7:8] += jnp.sum(adj * C6[2, rows, cols].astype(F32), axis=0, keepdims=True)
                C6[3, rows, cols] = gr_low
                C6[4, rows, cols] = gi_low
                parts = []
                for h in range(ch // 128):
                    hs = slice(h * 128, (h + 1) * 128)
                    hc = slice(yy * ch + h * 128, yy * ch + (h + 1) * 128)
                    parts.append(nt(jnp.concatenate([gr_low[:, hs], gi_low[:, hs]], axis=1),
                                    jnp.concatenate([hw[0, :, hc], hw[1, :, hc]], axis=1)))
                gco = gcd + jnp.concatenate(parts, axis=1)
                ext = jnp.concatenate([gco, gco_next], axis=0)
                x = RS[slot, :, cols]
                grn = p[0:1] * gco
                acc[yy, 0:1] += jnp.sum(gco * x[8:], axis=0, keepdims=True)
                acc[yy, 4:5] += jnp.sum(gco, axis=0, keepdims=True)
                for k in range(1, 4):
                    grn = grn + p[k : k + 1] * pltpu.roll(ext, T + 8 - k, 0)[:T]
                    acc[yy, k : k + 1] += jnp.sum(gco * pltpu.roll(x, k, 0)[8:], axis=0, keepdims=True)
                C6[5, rows, cols] = grn.astype(BF)
                new.append((adj_first, at[0:1], gco[0:8]))
            return tuple(new)

        zero = (jnp.zeros((1, ch), F32), jnp.zeros((1, ch), F32), jnp.zeros((8, ch), F32))
        lax.fori_loop(0, tiles, back_tile, (zero,) * y_size)

    def gel():
        transpose_into(TT, N1, SEQ)
        weight_grad(GEL, TT, C6.at[1])

    def rnn():
        weight_grad(RNN, TT, C6.at[5])

    def gn1o():
        back_copy.wait_send()
        partial_rows(rnn_back, base_other, PS)
        rnn_copy.start()

    def gn1w():
        partial_rows(rnn_back, base_own, MIX)

    def heads():
        cv_in.wait()
        if group == 1:
            small.drain(0)
        for yy in range(y_size):
            acc[yy, 7:8] = acc[yy, 7:8] * jax.nn.sigmoid(prm[yy, 7:8])
            for h in range(ch // 128):
                hs = slice(h * 128, (h + 1) * 128)
                hc = slice(yy * ch + h * 128, yy * ch + (h + 1) * 128)
                both = lax.dot_general(LRU[:, hc], jnp.concatenate([C6[3, :, hc], C6[4, :, hc]], axis=1),
                                       (((0,), (0,)), ((), ())), preferred_element_type=F32)
                for n in range(2):
                    val = both[:, n * 128 : (n + 1) * 128]
                    if group > 1:
                        o_gs[yy, 128 * n : 128 * n + 128, hs] = val
                    else:
                        gs[0, yy, :, :, 16 * n : 16 * n + 16, hs] = val.astype(BF).reshape(z_size, x_size, 16, 128)

    def fin():
        tok_again.wait()
        rnn_copy.wait_recv()

        @pl.loop(0, half // T)
        def _(i):
            rows = rows_of(i, T)
            v = PR[1, rows, :].astype(F32)
            gn = MIX[rows, :] + PR[0, rows, :].astype(F32)
            s = lax.rsqrt(jnp.mean(v * v, axis=1, keepdims=True) + EPS)
            q = gn * gains[0:1, :]
            pgain[0:1, :] += jnp.sum(gn * v * s, axis=0, keepdims=True)
            gtok[rows, :] += s * q - (s * s * s) * v * jnp.mean(q * v, axis=1, keepdims=True)

        gain_copy.start()
        gtok_copy.start()

    def s0():
        gain_copy.wait_recv()
        for n in range(2):
            row = pgain[n : n + 1, :] + pgain[8 + n : 9 + n, :]
            row = jnp.concatenate([row, jnp.zeros((1, 3 * ch - depth), F32)], axis=1)
            for m in range(3):
                for yy in range(y_size):
                    acc[yy, 8 + 3 * n + m : 9 + 3 * n + m, :] = row[:, m * ch : (m + 1) * ch]
        if group > 1:
            for yy in range(y_size):
                o_gs[yy, 256:272, :] = acc[yy]
            return

        @pl.loop(0, z_size)
        def _(z):
            for yy in range(y_size):
                for xx in range(x_size):
                    gs[0, yy, z, xx, 32:48, :] = acc[yy].astype(BF)

    blocks = dict(pre0=pre0, pre1=pre1, pre3=pre3, out=out, mix=mix, n2=n2, d0=d0, d1=d1, bo=bo, bw=bw, ga0=ga0,
                  ga1=ga1, norm=norm, up0=up0, up1=up1, outg=outg, gel=gel, rnn=rnn, gn1o=gn1o, gn1w=gn1w, heads=heads,
                  fin=fin, s0=s0)
    blocks = {name: (1, fn) for name, fn in blocks.items()}
    blocks.update(br=(tiles, branch), ffa=(SEQ // F, ff(0)), ffb=(SEQ // F, ff(1)), gh=(2 * SEQ // F, gh),
                  gno=(half // F, gno), gnw=(half // F, gnw), t=(tiles, back_rows))

    placed = set()

    def event(chunk, k):
        if chunk < CHUNKS:
            u = chunk // 2
            if k == 0 and u in sources and u not in placed:
                placed.add(u)
                place[u].wait()
            ag.event(chunk, k)
        elif chunk < 2 * CHUNKS:
            back.event(chunk - CHUNKS, k, finals)
        elif group == 1:
            if chunk == 2 * CHUNKS:
                small.event(0, k)
            else:
                back_small.event(0, k, o_gs)
                if k == 3:
                    gs_copy.start()

    run_plan(PLAN, blocks, event)
    for u in (RNN, GEL):
        for chunk in (2 * u, 2 * u + 1):
            ag.drain(chunk)
    for chunk in range(CHUNKS):
        back.drain(chunk)
    if group == 1:
        back_small.drain(0)
    else:
        gs_copy.start()
    finals.drain()
    gtok_copy.wait()
    gs_copy.wait()
    for cp in (tok_copy, cot_copy, row_copy, rnn_copy, gain_copy):
        cp.wait_send()


def finish_kernel(sizes, block_in, gtok_in, gw, gs,
                  o_block, o_gtok, o_mg, o_rnn, o_gel, o_cw, o_cb, o_rw, o_iw, o_rb, o_ib, o_dp, o_out, o_lg, o_gate, o_up,
                  o_down):
    ch = gw.shape[2]
    dp = sizes[0] * sizes[1]
    part, own = o_mg.shape[1], ch // dp
    dp_index = lax.axis_index("dp")
    o_block[...] = block_in[...]
    o_gtok[...] = gtok_in[...]
    o_rnn[...] = gw[RNN]
    o_gel[...] = gw[GEL]
    o_out[...] = gw[OUT].T
    for j in range(2):
        cols = slice(j * ch, (j + 1) * ch)
        o_gate[:, cols] = gw[GATE[j]]
        o_up[:, cols] = gw[UP[j]]
        o_down[cols, :] = gw[DOWN[j]].T
    for h in range(ch // 128):
        o_rw[h] = gs[0, 0:16, h * 128 : (h + 1) * 128]
        o_iw[h] = gs[0, 16:32, h * 128 : (h + 1) * 128]
    rows = pltpu.roll(gs[0, 32:40, :], ch - dp_index * own, 1)
    o_cw[...] = rows[0:4, 0:own]
    for k, ref in ((4, o_cb), (5, o_rb), (6, o_ib), (7, o_dp)):
        ref[...] = rows[k : k + 1, 0:own]
    for n, ref in ((0, o_mg), (1, o_lg)):
        row = jnp.concatenate([gs[0, 40 + 3 * n + k : 41 + 3 * n + k, :] for k in range(3)], axis=1)
        row = jnp.broadcast_to(row, (8, 3 * ch))
        ref[...] = pltpu.roll(row, 3 * ch - dp_index * part, 1)[0:1, 0:part]


def any_spec():
    return pl.BlockSpec(memory_space=pl.ANY)


def vmem_spec():
    return pl.BlockSpec(memory_space=pltpu.VMEM)


def body(sizes, tokens, mix_gain, rnn_weight, gelu_weight, conv_weight, conv_bias, recur_weight, input_weight,
         recur_bias, input_bias, decay_param, out_weight, mlp_gain, gate_weight, up_weight, down_weight, cotangent):
    z_size, x_size, y_size = sizes
    dp = z_size * x_size
    dp_index = lax.axis_index("dp")
    rows, depth = tokens.shape
    part, ch = rnn_weight.shape
    head_rows = recur_weight.shape[1]
    group = max(1, 16 // head_rows)
    wide = y_size * ch
    own = ch // dp
    vectors = [v[None] for v in (conv_bias, recur_bias, input_bias, decay_param, mix_gain, mlp_gain)]
    heads = [recur_weight, input_weight]
    out_w, down_w = out_weight, down_weight
    if part % 128:
        out_w, down_w = out_weight.T, down_weight.T
    shape = jax.ShapeDtypeStruct
    grid = (y_size, z_size, x_size)
    hops = z_size + x_size + y_size - 2
    t = lax.axis_index("tensor")
    joined = [conv_weight] * 3
    if group > 1:
        lanes = jnp.concatenate([conv_weight, *vectors[0:4]], axis=0).astype(F32)
        lanes = jnp.pad(lanes, ((0, 8), (0, ch - own)))
        lanes = jnp.roll(lanes, dp_index * own, axis=1)
        gain = jnp.pad(jnp.concatenate(vectors[4:6], axis=0).astype(F32), ((0, 6), (0, depth - part)))
        gain = lax.psum(jnp.roll(gain, dp_index * part, axis=1), "dp")
        every = jnp.zeros((2 * y_size, 272, ch), F32)
        for n, w in enumerate(heads):
            w = jnp.transpose(w, (1, 0, 2)).reshape(1, head_rows, ch).astype(F32)
            every = lax.dynamic_update_slice(every, w, (t, 128 * n + dp_index * head_rows, 0))
        every = lax.psum(lax.dynamic_update_slice(every, lanes[None], (t, 256, 0)), ("dp", "tensor"))
        mine = [every[2 * yy] * (1 - lax.rem(t, 2)) + every[2 * yy + 1] * lax.rem(t, 2) for yy in range(y_size)]
        joined = [jnp.stack([m[256:] for m in mine]), gain,
                  jnp.concatenate([m[0:256].reshape(2, 128, ch) for m in mine], axis=2).astype(BF)]
        heads = [jnp.zeros((ch // 128, 16, 128), BF)] * 2
    dma = pltpu.SemaphoreType.DMA
    landed = list(big_landing(sizes, part, ch).values())
    gs_out, small_grid = (y_size, 272, ch), (1, 1, 1)
    if group == 1:
        landed += list(small_landing(sizes, ch).values())
        gs_out, small_grid = (1, SMALL, ch), grid
    block_out, grad_tokens, gw, gs = pl.pallas_call(
        functools.partial(block_kernel, sizes, group),
        out_shape=[shape((rows, depth), BF), shape((rows, depth), F32), shape((UNITS, part, ch), F32), shape(gs_out, F32),
                   shape((6, SEQ, wide), BF), shape((SEQ // 128, 128, wide), F32), shape((SEQ // 128, 136, wide), F32),
                   shape((SEQ, wide), BF)],
        in_specs=[*[any_spec()] * 8, *[vmem_spec()] * 7, any_spec(), any_spec(), *([vmem_spec()] * 3 if group > 1 else [any_spec()] * 3)],
        out_specs=[any_spec()] * 8,
        scratch_shapes=[
            pltpu.VMEM((UNITS + 2, *grid, part, ch), BF), pltpu.VMEM((1, *small_grid, SMALL, ch), BF),
            pltpu.VMEM((6, SEQ, wide), BF), pltpu.VMEM((SEQ, wide), BF),
            *[pltpu.VMEM((SEQ, depth), BF)] * 4, pltpu.VMEM((rows, depth), F32),
            pltpu.VMEM((rows, depth), BF), pltpu.VMEM((2, rows, depth), BF),
            pltpu.VMEM((rows, depth), F32), pltpu.VMEM((2, 128, wide), F32), pltpu.VMEM((2, 136, wide), F32),
            pltpu.VMEM((2, max(part // 2, 16), ch), F32),
            pltpu.VMEM((y_size, 16, ch), F32), pltpu.VMEM((16, depth), F32), pltpu.VMEM((16, ch), F32),
            pltpu.VMEM((y_size, 16, ch), F32), pltpu.VMEM((8, depth), F32), pltpu.VMEM((2, 128, wide), BF),
            pltpu.VMEM(out_w.shape, BF), pltpu.VMEM(down_w.shape, BF), pltpu.VMEM(heads[0].shape, BF),
            pltpu.VMEM(heads[1].shape, BF), pltpu.VMEM(gs_out, F32), pltpu.VMEM((8, 3 * ch), F32),
            dma((CHUNKS, hops)), dma((CHUNKS, hops)), dma((CHUNKS, hops)), dma((CHUNKS, hops)),
            dma((1, hops)), dma((1, hops)), dma((1, hops)), dma((1, hops)), dma((9,)), dma((9,)), dma((19,)), dma((3, 2)), dma((2,)),
            *[pltpu.VMEM(s, BF) for s in landed],
        ],
        compiler_params=pltpu.CompilerParams(collective_id=0, has_side_effects=True, vmem_limit_bytes=VMEM_LIMIT),
        name="residual_block",
    )(tokens, cotangent, rnn_weight, gelu_weight, out_w, gate_weight, up_weight, down_w, conv_weight, *vectors, *heads,
      *joined)[:4]
    if group > 1:
        every = jnp.zeros((2 * y_size, 272, ch), F32)
        for yy in range(y_size):
            every = lax.dynamic_update_slice(every, gs[yy : yy + 1], (2 * yy + lax.rem(t, 2), 0, 0))
        gs = lax.dynamic_slice(lax.psum(every, ("dp", "tensor")), (t, 0, 0), (1, 272, ch))
        first = dp_index * head_rows
        rec = lax.dynamic_slice(gs[0], (first, 0), (head_rows, ch))
        inp = lax.dynamic_slice(gs[0], (128 + first, 0), (head_rows, ch))
        fill = jnp.zeros((16 - head_rows, ch), F32)
        gs = jnp.concatenate([rec, fill, inp, fill, gs[0, 256:]], axis=0)[None]
    f_shapes = [
        shape((rows, depth), BF), shape((rows, depth), F32), shape((1, part), F32), shape((part, ch), F32),
        shape((part, ch), F32), shape((4, own), F32), shape((1, own), F32), shape((ch // 128, 16, 128), F32),
        shape((ch // 128, 16, 128), F32), shape((1, own), F32), shape((1, own), F32), shape((1, own), F32),
        shape((ch, part), F32), shape((1, part), F32), shape((part, 2 * ch), F32), shape((part, 2 * ch), F32),
        shape((2 * ch, part), F32),
    ]
    res = list(pl.pallas_call(
        functools.partial(finish_kernel, sizes),
        out_shape=f_shapes,
        in_specs=[vmem_spec()] * 4,
        out_specs=[vmem_spec()] * 17,
        compiler_params=pltpu.CompilerParams(vmem_limit_bytes=VMEM_LIMIT),
        name="unpack",
    )(block_out, grad_tokens, gw, gs))
    for k in (2, 6, 9, 10, 11, 13):
        res[k] = res[k][0]
    for k in (7, 8):
        res[k] = res[k][:, :head_rows]
    return tuple(res)


def solution(mesh):
    dp, tensor = mesh.shape["dp"], mesh.shape["tensor"]
    x_size = 2
    sizes = (dp // x_size, x_size, tensor // 2)
    rows, split, vec = P(("dp", "tensor"), None), P("dp", "tensor"), P(("tensor", "dp"))
    head, flip, taps = P("tensor", "dp", None), P("tensor", "dp"), P(None, ("tensor", "dp"))
    return jax.shard_map(
        functools.partial(body, sizes),
        mesh=mesh,
        in_specs=(rows, P("dp"), split, split, taps, vec, head, head, vec, vec, vec, flip, P("dp"), split, split, flip,
                  rows),
        out_specs=(rows, rows, P("dp"), split, split, taps, vec, head, head, vec, vec, vec, flip, P("dp"), split, split,
                   flip),
        check_vma=False,
    )
```

```python
import functools

import jax
import jax.numpy as jnp
from jax import lax
from jax.experimental import pallas as pl
from jax.experimental.pallas import tpu as pltpu
from jax.sharding import PartitionSpec as P

SEQ = 1024
EPS = 1e-06
GUARD = 0.01
DECAY_SCALE = 8.0
GELU_K = 0.7978845608028654
GELU_C = 0.044715
BF = jnp.bfloat16
F32 = jnp.float32
MESH = pl.DeviceIdType.MESH
VMEM_LIMIT = 63 * 1024 * 1024

RNN, GEL, OUT, GA0, UP0, GA1, UP1, DN0, DN1 = range(9)
UNITS = 9
GATE, UP, DOWN = (GA0, GA1), (UP0, UP1), (DN0, DN1)
CHUNKS = 2 * UNITS
SMALL = 32
FLOW = (
    "zxy", "zxy", "zyx", "zxy", "yzx", "zyx", "zxy", "zyx", "xyz", "xzy", "yxz", "zyx", "zxy", "yzx", "zxy", "xyz",
    "zyx", "zxy",
)
BACK = (
    "yxz", "yxz", "yxz", "xzy", "xzy", "xzy", "xzy", "yzx", "xyz", "yxz", "zyx", "xzy", "yxz", "yxz", "yxz", "zyx",
    "xyz", "zxy",
)
SMALL_FLOW, SMALL_BACK = ("zyx",), ("yxz",)
PLAN = (
    10, 50, 15, 40, "pre0", 51, 41, 14, 20, "pre1", 180, 75, 45, 11, 19, 16, 55, 184, 5, 76, 12, 35, 181, 65, 9, 6,
    17, 0, 39, 30, 36, 21, 182, 59, 4, 25, 7, 1, 37, 34, 29, 80, 24, 60, 26, 13, 46, 2, 56, 64, 31, 84, 183, 18, 85,
    38, 70, 27, "pre3", 66, 3, 74, 81, 8, 22, "br", 89, 49, 32, 42, "br", 47, 71, "br", 61, 57, 86, "br", 69, "br",
    52, 28, "br", "br", "br", 62, 44, 23, 67, "out", 48, 77, "mix", 72, 82, "n2", 43, 33, "ffa", "ffa", "ffa", 54,
    58, 63, 87, "ffa", "d0", 165, 160, 73, 53, 68, "ffb", "ffb", 79, "ffb", "ffb", "d1", 170, 88, 175, 169, 78, 83,
    "gh", "gh", "gh", "gh", "gh", "gh", "gh", "gh", "bo", 161, "bw", "ga0", 120, 125, 179, "ga1", 140, "gno", "gno",
    145, "gnw", 171, "gnw", "norm", "up0", 135, 130, 162, 144, "up1", "outg", 110, 126, "t", 150, "t", 164, "t", 121,
    "t", 115, "t", 155, 129, 131, 136, 124, 146, 172, "t", "t", 149, 111, "t", "gel", "rnn", 90, 116, 114, 156, 105,
    "gn1o", "gn1w", "heads", 100, 132, 119, 95, 174, "fin", "s0", 137, 157, 151, 101, 106, 134, 185, 133, 159, 147,
    141, 139, 91, 109, 152, 112, 117, 102, 96, 154, 166, 92, 186, 148, 176, 97, 122, 142, 94, 163, 104, 113, 158,
    173, 138, 127, 187, 107, 167, 93, 177, 99, 118, 103, 153, 123, 143, 189, 128, 108, 98, 178, 168, 188,
)


def run_plan(plan, blocks, event):
    i = 0
    while i < len(plan):
        name = plan[i]
        i += 1
        if isinstance(name, int):
            event(name // 5, name % 5)
            continue
        turns, fn = blocks[name]
        if turns == 1:
            fn()
            continue
        hooks = {}
        for turn in range(1, turns):
            hooks[turn] = []
            while isinstance(plan[i], int):
                hooks[turn].append(plan[i])
                i += 1
            i += 1

        def hook(n, hooks=hooks):
            for turn, steps in hooks.items():
                if steps:
                    @pl.when(n == turn)
                    def _(steps=steps):
                        for step in steps:
                            event(step // 5, step % 5)

        fn(hook)


def nn(a, b):
    return jnp.dot(a, b, preferred_element_type=F32)


def nt(a, b):
    return lax.dot_general(a, b, (((1,), (1,)), ((), ())), preferred_element_type=F32)


def gelu_parts(v):
    v2 = v * v
    th = jnp.tanh(GELU_K * v * (1.0 + GELU_C * v2))
    half = 0.5 * (1.0 + th)
    return v * half, half + (0.5 * GELU_K) * v * (1.0 - th * th) * (1.0 + (3.0 * GELU_C) * v2)


class Net:
    def __init__(self, z_size, x_size, y_size):
        self.size = {"z": z_size, "x": x_size, "y": y_size, "c": 2}
        dp, t = lax.axis_index("dp"), lax.axis_index("tensor")
        self.at = {"z": dp // x_size, "x": lax.rem(dp, x_size), "y": t // 2, "c": lax.rem(t, 2)}
        self.off = {"z": 0, "x": z_size - 1, "y": z_size + x_size - 2}
        self.relay = z_size + x_size + y_size - 3 if z_size == 4 else None

    def shifted(self, d, j):
        n = self.size[d]
        return lax.rem(self.at[d] + (j % n), n)

    def device(self, d, j):
        at = dict(self.at)
        at[d] = self.shifted(d, j)
        return (at["z"] * self.size["x"] + at["x"], at["y"] * 2 + at["c"])

    def barrier(self):
        sem = pltpu.get_barrier_semaphore()
        count = 0
        for d in "zxyc":
            for j in range(1, self.size[d]):
                pl.semaphore_signal(sem, inc=1, device_id=self.device(d, j), device_id_type=MESH)
                count += 1
        pl.semaphore_wait(sem, count)


def chunk_rows(c, part):
    if part % 32:
        return slice(None) if c % 2 == 0 else None
    return slice(c % 2 * (part // 2), (c % 2 + 1) * (part // 2))


class Gather:
    def __init__(self, net, ref, flows, ss, rs, halves):
        self.net, self.ref, self.flows, self.ss, self.rs, self.halves = net, ref, flows, ss, rs, halves

    def region(self, c, s, at):
        order = self.flows[c]
        idx = [slice(None) if d in order[:s] else at[d] for d in "yzx"]
        if not self.halves:
            return self.ref.at[(c, *idx)]
        return self.ref.at[(c // 2, *idx, chunk_rows(c, self.ref.shape[4]))]

    def copy(self, c, s, j, sender, origin=None, send=None, recv=None):
        d = self.flows[c][s]
        at = dict(self.net.at)
        if sender:
            at[d] = self.net.shifted(d, -j)
        if origin is not None:
            at[d] = origin
        region = self.region(c, s, at)
        k = self.net.off[d] + j - 1
        return pltpu.make_async_remote_copy(
            src_ref=region, dst_ref=region, send_sem=self.ss.at[c, k if send is None else send],
            recv_sem=self.rs.at[c, k if recv is None else recv], device_id=self.net.device(d, j), device_id_type=MESH)

    def relayed(self, c, s):
        return self.net.relay is not None and self.flows[c][s] == "z"

    def sends(self, c, s, act):
        if not self.relayed(c, s):
            for j in range(1, self.net.size[self.flows[c][s]]):
                act(self.copy(c, s, j, False))
            return
        z = self.net.at["z"]
        act(self.copy(c, s, 2, False))
        pl.when(z != 3)(lambda: act(self.copy(c, s, 1, False)))
        pl.when(z != 0)(lambda: act(self.copy(c, s, 3, False)))

    def passes_on(self, c, s, act):
        z = self.net.at["z"]
        k = self.net.relay
        pl.when(z == 2)(lambda: act(self.copy(c, s, 1, False, 0, k, 2)))
        pl.when(z == 1)(lambda: act(self.copy(c, s, 3, False, 3, k, 0)))

    def event(self, c, k):
        if self.halves and chunk_rows(c, self.ref.shape[4]) is None:
            return
        if k == 4:
            s = self.flows[c].index("z")
            if self.relayed(c, s):
                self.copy(c, s, 2, True).wait_recv()
                self.passes_on(c, s, lambda cp: cp.start())
            return
        if k:
            for j in range(1, self.net.size[self.flows[c][k - 1]]):
                if not (self.relayed(c, k - 1) and j == 2):
                    self.copy(c, k - 1, j, True).wait_recv()
        if k < 3:
            self.sends(c, k, lambda cp: cp.start())

    def drain(self, c):
        if self.halves and chunk_rows(c, self.ref.shape[4]) is None:
            return
        for s in range(3):
            self.sends(c, s, lambda cp: cp.wait_send())
            if self.relayed(c, s):
                self.passes_on(c, s, lambda cp: cp.wait_send())


def pair_copy(net, src, dst, ss, rs, k):
    return pltpu.make_async_remote_copy(
        src_ref=src, dst_ref=dst, send_sem=ss.at[k], recv_sem=rs.at[k],
        device_id=net.device("c", 1), device_id_type=MESH)


def scan_forward(a, b, carry):
    rows, cols = a.shape
    a = a.reshape(rows // 8, 8, cols)
    b = b.reshape(rows // 8, 8, cols)
    place = lax.broadcasted_iota(jnp.int32, (rows // 8, 8, cols), 1)
    for k in (1, 2, 4):
        keep = place >= k
        b = b + a * jnp.where(keep, pltpu.roll(b, k, 1), 0.0)
        a = a * jnp.where(keep, pltpu.roll(a, k, 1), 1.0)
    out = []
    for g in range(rows // 8):
        s = b[g] + a[g] * carry
        out.append(s)
        carry = s[7:8]
    return jnp.concatenate(out, axis=0), carry


def scan_backward(a, b, carry):
    rows, cols = a.shape
    a = a.reshape(rows // 8, 8, cols)
    b = b.reshape(rows // 8, 8, cols)
    place = lax.broadcasted_iota(jnp.int32, (rows // 8, 8, cols), 1)
    for k in (1, 2, 4):
        keep = place < 8 - k
        b = b + a * jnp.where(keep, pltpu.roll(b, 8 - k, 1), 0.0)
        a = a * jnp.where(keep, pltpu.roll(a, 8 - k, 1), 1.0)
    out = []
    for g in reversed(range(rows // 8)):
        s = b[g] + a[g] * carry
        out.append(s)
        carry = s[0:1]
    return jnp.concatenate(out[::-1], axis=0), carry


def rows_of(i, n):
    return pl.ds(pl.multiple_of(i * n, n), n)


def join_params(gp, prm, gains, sizes):
    z_size, x_size, y_size = sizes
    ch = prm.shape[2]
    own = ch // (z_size * x_size)
    lane = lax.broadcasted_iota(jnp.int32, (8, 128), 1)
    for yy in range(y_size):
        total = jnp.zeros((8, ch), F32)
        for i in range(z_size * x_size):
            block = gp[0, yy, i // x_size, i % x_size]
            row = jnp.concatenate([jnp.where(lane < own, block, 0.0), jnp.zeros((8, ch - 128), F32)], axis=1)
            total = total + (pltpu.roll(row, i * own, 1) if i else row)
        prm[yy] = jnp.concatenate([total, jnp.zeros((8, ch), F32)], axis=0)
    for i in range(z_size * x_size):
        block = gp[0, 0, i // x_size, i % x_size]
        turned = pltpu.roll(block, 64, 1)
        for n in range(2):
            gains[n : n + 1, i * 128 : (i + 1) * 128] = jnp.where(
                lane[0:1] < 64, turned[2 * n : 2 * n + 1], block[2 * n + 1 : 2 * n + 2])


def put_gain(block, n, row):
    turned = pltpu.roll(jnp.broadcast_to(row, (8, 128)), 64, 1)
    block[2 * n : 2 * n + 1, 64:128] = turned[0:1, 64:128]
    block[2 * n + 1 : 2 * n + 2, 64:128] = row[:, 64:128]


def head_weight(gs, yy, first):
    blocks = gs[0, yy, :, :, first : first + 16, :]
    return blocks.reshape(-1, blocks.shape[-1])


def transpose_into(dst, src, n, step=256):
    @pl.loop(0, n // step)
    def _(i):
        dst[:, rows_of(i, step)] = src[rows_of(i, step), :].T


class Scatter:
    def __init__(self, net, ref, flows, bufs, ss, rs, halves):
        self.net, self.ref, self.flows, self.bufs, self.ss, self.rs, self.halves = net, ref, flows, bufs, ss, rs, halves

    def rows(self, c):
        return chunk_rows(c, self.ref.shape[4]) if self.halves else slice(None)

    def slot(self, c):
        return SLOT[c // 2] if self.halves else c

    def copy(self, c, s, j, owner=None, slot=None, k=None):
        order = self.flows[c]
        d = order[s]
        at = dict(self.net.at)
        at[d] = self.net.shifted(d, j) if owner is None else owner
        idx = [at[e] if e in order[: s + 1] else slice(None) for e in "yzx"]
        k = self.net.off[d] + j - 1 if k is None else k
        return pltpu.make_async_remote_copy(
            src_ref=self.ref.at[(self.slot(c), *idx, self.rows(c))], dst_ref=self.bufs[c, s].at[j - 1 if slot is None else slot],
            send_sem=self.ss.at[c, k], recv_sem=self.rs.at[c, k],
            device_id=self.net.device(d, j), device_id_type=MESH)

    def relayed(self, c, s):
        return self.net.relay is not None and self.flows[c][s] == "z"

    def hops(self, c, s):
        return range(1, self.net.size[self.flows[c][s]])

    def far(self, c, s, act):
        z = self.net.at["z"]
        pl.when(z == 3)(lambda: act(self.copy(c, s, 3, 0, 3, self.net.relay)))
        pl.when(z == 0)(lambda: act(self.copy(c, s, 1, 3, 3, self.net.relay)))

    def sends(self, c, s, act):
        if not self.relayed(c, s):
            for j in self.hops(c, s):
                act(self.copy(c, s, j))
            return
        z = self.net.at["z"]
        self.far(c, s, act)
        pl.when(jnp.logical_or(z == 0, z == 3))(lambda: act(self.copy(c, s, 2)))
        pl.when(z != 3)(lambda: act(self.copy(c, s, 1)))
        pl.when(z != 0)(lambda: act(self.copy(c, s, 3)))

    def over(self, names, fn, place):
        if not names:
            fn(place)
        elif names[0] == "z":
            @pl.loop(0, self.net.size["z"])
            def _(z):
                self.over(names[1:], fn, {**place, "z": z})
        else:
            for n in range(self.net.size[names[0]]):
                self.over(names[1:], fn, {**place, names[0]: n})

    def pass_on(self, c, s):
        order = self.flows[c]
        rest = [e for e in "zyx" if e not in order[: s + 1]]
        buf = self.bufs[c, s]
        rows = self.rows(c)
        z = self.net.at["z"]

        def middle(owner):
            def fn():
                self.copy(c, s, 1, None, 3, self.net.relay).wait_recv()

                def block(place):
                    place = {**place, "z": owner}
                    idx = (self.slot(c), *[place[e] if e in place else self.net.at[e] for e in "yzx"], rows)
                    got = buf[(3, *[place[e] for e in "yzx" if e in rest])]
                    self.ref[idx] = (self.ref[idx].astype(F32) + got.astype(F32)).astype(self.ref.dtype)

                self.over(rest, block, {})
                self.copy(c, s, 2).start()
            return fn

        def end(unused):
            def fn():
                def block(place):
                    buf[(unused, *[place[e] for e in "yzx" if e in rest])] = jnp.zeros(buf.shape[-2:], buf.dtype)

                self.over(rest, block, {})
            return fn

        pl.when(z == 0)(end(0))
        pl.when(z == 1)(middle(3))
        pl.when(z == 2)(middle(0))
        pl.when(z == 3)(end(2))

    def add(self, c, s, out):
        order = self.flows[c]
        z = self.net.at["z"]
        for j in self.hops(c, s):
            take = self.copy(c, s, j).wait_recv
            if self.relayed(c, s) and j != 2:
                pl.when(z != (0 if j == 1 else 3))(take)
            else:
                take()
        rest = [e for e in "zyx" if e not in order[: s + 1]]
        buf = self.bufs[c, s]
        rows = self.rows(c)

        def block(place):
            idx = (self.slot(c), *[place[e] if e in place else self.net.at[e] for e in "yzx"], rows)
            total = self.ref[idx].astype(F32)
            for j in self.hops(c, s):
                total = total + buf[(j - 1, *[place[e] for e in "yzx" if e in place])].astype(F32)
            if s < 2:
                self.ref[idx] = total.astype(self.ref.dtype)
            elif self.halves:
                out.put(c // 2, rows, total)
            else:
                out[c] = total

        self.over(rest, block, {})

    def event(self, c, k, out):
        if self.rows(c) is None:
            return
        if k == 4:
            s = self.flows[c].index("z")
            if self.relayed(c, s):
                self.pass_on(c, s)
            return
        if k:
            self.add(c, k - 1, out)
        if k < 3:
            self.sends(c, k, lambda cp: cp.start())

    def drain(self, c):
        if self.rows(c) is None:
            return
        z = self.net.at["z"]
        for s in range(3):
            self.sends(c, s, lambda cp: cp.wait_send())
            if self.relayed(c, s):
                pl.when(jnp.logical_or(z == 1, z == 2))(lambda: self.copy(c, s, 2).wait_send())


def landing(flows, sizes, rows, ch):
    size = dict(zip("zxy", sizes))
    shapes = {}
    for c, order in enumerate(flows):
        n = rows(c)
        for s in range(3):
            if n:
                rest = [size[e] for e in "yzx" if e not in order[: s + 1]]
                places = 4 if order[s] == "z" and size["z"] == 4 else size[order[s]] - 1
                shapes[c, s] = (places, *rest, n, ch)
    return shapes


SLOT = {DN0: 9, DN1: 10, GA0: DN0, GA1: DN1, UP0: GA0, UP1: GA1, OUT: UP0, GEL: UP1, RNN: OUT}


def big_landing(sizes, part, ch):
    def rows(c):
        cut = chunk_rows(c, part)
        return 0 if cut is None else len(range(part)[cut])

    return landing(BACK, sizes, rows, ch)


def small_landing(sizes, ch):
    return landing(SMALL_BACK, sizes, lambda c: SMALL, ch)


def params_landing(sizes):
    return landing(SMALL_BACK, sizes, lambda c: 8, 128)


class Finals:
    def __init__(self, ref, out, sem):
        self.ref, self.out, self.sem, self.copies = ref, out, sem, []

    def copy(self, n):
        u, rows = self.copies[n]
        return pltpu.make_async_copy(self.ref.at[n % 2], self.out.at[u, rows], self.sem.at[n % 2])

    def put(self, u, rows, total):
        n = len(self.copies)
        self.copies.append((u, rows))
        if n >= 2:
            self.copy(n - 2).wait()
        self.ref[n % 2] = total
        self.copy(n).start()

    def drain(self):
        for n in range(max(0, len(self.copies) - 2), len(self.copies)):
            self.copy(n).wait()


def block_kernel(sizes, group,
                 tok, cot, w_rnn, w_gel, out_h, w_gate, w_up, down_h, taps_in, cb_in, rb_in, ib_in, dp_in, mg_in, lg_in, rec_h, inp_h, prm_in, gains_in, hw_in,
                 o_block, o_gtok, o_gw, gs_h, gp_h, h_cf, h_a, h_ri, h_cv,
                 W, gs, C6, LRU, T1, SA, N1, TT, MIX, PS, PR, gtok, AS, RS, FB, acc, pgain, prm, gains, hw,
                 w_out, w_down, rec_in, inp_in, o_gs, o_gp, taps, gp,
                 ss, rs, bss, brs, sss, srs, bsss, bsrs, pss, prs, bpss, bprs, ps, pr, ls, ts, fs, *landed):
    net = Net(*sizes)
    z_size, x_size, y_size = sizes
    c = net.at["c"]
    half = SEQ // 2
    ch = W.shape[-1]
    part = W.shape[4]
    depth = T1.shape[1]
    own, other = pl.ds(pl.multiple_of(c * half, half), half), pl.ds(pl.multiple_of((1 - c) * half, half), half)
    base_own, base_other = c * half, (1 - c) * half
    mine = (net.at["y"], net.at["z"], net.at["x"])
    dp_index = lax.axis_index("dp")

    sources = {RNN: w_rnn, GEL: w_gel, GA0: w_gate.at[:, 0:ch], GA1: w_gate.at[:, ch : 2 * ch], UP0: w_up.at[:, 0:ch],
               UP1: w_up.at[:, ch : 2 * ch]}
    place = {u: pltpu.make_async_copy(src, W.at[(u, *mine)], ls.at[u]) for u, src in sources.items()}
    place["tok"] = pltpu.make_async_copy(tok, T1.at[own], ls.at[OUT])
    place["cot"] = pltpu.make_async_copy(cot, SA.at[own], ls.at[DN0])
    for n, (name, src, dst) in enumerate((("out", out_h, w_out), ("down", down_h, w_down), ("rec", rec_h, rec_in),
                                          ("inp", inp_h, inp_in))):
        place[name] = pltpu.make_async_copy(src, dst, ls.at[15 + n])
    for cp in place.values():
        cp.start()
    net.barrier()

    ag = Gather(net, W, FLOW, ss, rs, True)
    shapes = big_landing(sizes, part, ch)
    back = Scatter(net, W, BACK, dict(zip(shapes, landed)), bss, brs, True)
    small = back_small = params = back_params = None
    if group == 1:
        small = Gather(net, gs, SMALL_FLOW, sss, srs, False)
        tail = landed[len(shapes):]
        params = Gather(net, gp, SMALL_FLOW, pss, prs, False)
        back_params = Scatter(net, gp, SMALL_BACK, dict(zip(params_landing(sizes), tail[3:])), bpss, bprs, False)
        back_small = Scatter(net, gs, SMALL_BACK, dict(zip(small_landing(sizes, ch), tail)), bsss, bsrs, False)

    tok_copy = pair_copy(net, tok, T1.at[own], ps, pr, 0)
    cot_copy = pair_copy(net, cot, SA.at[own], ps, pr, 1)
    tok_in = pair_copy(net, tok, T1.at[other], ps, pr, 0)
    cot_in = pair_copy(net, cot, SA.at[other], ps, pr, 1)
    mix_copy = pair_copy(net, PS, PR.at[0], ps, pr, 2)
    n2_copy = pair_copy(net, T1.at[own], T1.at[own], ps, pr, 3)
    n2_in = pair_copy(net, T1.at[other], T1.at[other], ps, pr, 3)
    back_copy = pair_copy(net, PS, PR.at[0], ps, pr, 4)
    row_copy = pair_copy(net, SA.at[own], SA.at[own], ps, pr, 5)
    row_in = pair_copy(net, SA.at[other], SA.at[other], ps, pr, 5)
    out_copy = pair_copy(net, PS, PR.at[1], ps, pr, 6)
    rnn_copy = pair_copy(net, PS, PR.at[0], ps, pr, 7)
    gain_copy = pair_copy(net, pgain.at[0:8], pgain.at[8:16], ps, pr, 8)
    cf_out = pltpu.make_async_copy(C6, h_cf, ls.at[9])
    cf_in = pltpu.make_async_copy(h_cf, C6, ls.at[10])
    cv_in = pltpu.make_async_copy(h_cv, LRU, ls.at[11])
    tok_again = pltpu.make_async_copy(tok, PR.at[1], ls.at[12])
    block_copy = pltpu.make_async_copy(PR.at[1], o_block, ls.at[13])
    gtok_copy = pltpu.make_async_copy(gtok, o_gtok, ls.at[14])
    gs_copy = pltpu.make_async_copy(o_gs, gs_h, ls.at[8])
    gp_copy = pltpu.make_async_copy(o_gp, gp_h, ls.at[19])

    tok_copy.start()
    cot_copy.start()

    def full(u):
        return jnp.concatenate([W[u, yy].reshape(depth, ch) for yy in range(y_size)], axis=1)

    finals = Finals(FB, o_gw, fs)


    def pre0():
        for name in ("out", "down", "rec", "inp"):
            place[name].wait()
        if group == 1:
            width = taps_in.shape[1]
            taps[...] = jnp.zeros_like(taps)
            taps[0:4, 0:width] = taps_in[...].astype(F32)
            for n, ref in enumerate((cb_in, rb_in, ib_in, dp_in)):
                taps[4 + n : 5 + n, 0:width] = ref[...].astype(F32)
            for n, ref in enumerate((mg_in, lg_in)):
                put_gain(taps, n, ref[...].astype(F32))
            gp[(0, *mine)] = taps[...]
            for n, src in enumerate((rec_in, inp_in)):
                for h in range(ch // 128):
                    gs[(0, *mine, slice(16 * n, 16 * n + 16), slice(h * 128, (h + 1) * 128))] = src[h]
        if part % 128:
            W[(OUT, *mine)] = w_out[...]
            W[(DN0, *mine)] = w_down[:, :ch]
            W[(DN1, *mine)] = w_down[:, ch:]
        else:
            W[(OUT, *mine)] = w_out[...].T
            W[(DN0, *mine)] = w_down[:ch, :].T
            W[(DN1, *mine)] = w_down[ch:, :].T

    def pre1():
        place["tok"].wait()
        place["cot"].wait()
        cot_in.wait_recv()
        transpose_into(TT, SA, SEQ)
        tok_in.wait_recv()

    def pre3():
        if group == 1:
            join_params(gp, prm, gains, sizes)
            for yy in range(y_size):
                for n in range(2):
                    hw[n, :, yy * ch : (yy + 1) * ch] = head_weight(gs, yy, 16 * n)
        else:
            prm[...] = prm_in[...]
            gains[...] = gains_in[...]
            hw[...] = hw_in[...]
        RS[1, 128:136, :] = jnp.zeros((8, y_size * ch), F32)

        @pl.loop(0, SEQ // 128)
        def _(i):
            v = T1[rows_of(i, 128), :].astype(F32)
            s = lax.rsqrt(jnp.mean(v * v, axis=1, keepdims=True) + EPS)
            N1[rows_of(i, 128), :] = (v * s * gains[0:1, :]).astype(BF)

    T = 128
    tiles = SEQ // T

    def kept(i, slot):
        return (pltpu.make_async_copy(AS.at[slot], h_a.at[i], ts.at[0, slot]),
                pltpu.make_async_copy(RS.at[slot], h_ri.at[i], ts.at[1, slot]),
                pltpu.make_async_copy(PS.at[rows_of(slot, T), 0 : y_size * ch], h_cv.at[rows_of(i, T)], ts.at[2, slot]))

    def branch(hook):
        def branch_tile(i, carries):
            hook(i)
            slot = lax.rem(i, 2)

            @pl.when(i >= 2)
            def _():
                for cp in kept(i - 2, slot):
                    cp.wait()

            RS[slot, 0:8, :] = RS[1 - slot, 128:136, :]
            RS[slot, 8:136, :] = nn(N1[rows_of(i, T), :], full(RNN))
            rows = rows_of(i, T)
            br = nn(N1[rows, :], full(GEL))
            new = []
            for yy in range(y_size):
                cols = slice(yy * ch, (yy + 1) * ch)
                p = prm[yy]
                x = RS[slot, :, cols]
                cv = p[4:5] + p[0:1] * x[8:]
                for k in range(1, 4):
                    cv = cv + p[k : k + 1] * pltpu.roll(x, k, 0)[8:]
                cv_low = cv.astype(BF)
                PS[pl.ds(pl.multiple_of(slot * T, T), T), cols] = cv_low
                cv = cv_low.astype(F32)
                rec, inp = [], []
                for h in range(ch // 128):
                    hc = slice(yy * ch + h * 128, yy * ch + (h + 1) * 128)
                    both = nn(cv_low[:, h * 128 : (h + 1) * 128], jnp.concatenate([hw[0, :, hc], hw[1, :, hc]], axis=1))
                    rec.append(both[:, :128])
                    inp.append(both[:, 128:])
                r = jax.nn.sigmoid(jnp.concatenate(rec, axis=1) + p[5:6])
                w = jax.nn.sigmoid(jnp.concatenate(inp, axis=1) + p[6:7])
                soft = jnp.log1p(jnp.exp(-jnp.abs(p[7:8]))) + jnp.maximum(p[7:8], 0.0)
                a = jnp.exp((-DECAY_SCALE * soft) * r)
                u = 1.0 - a * a + GUARD
                inv = lax.rsqrt(u)
                root = u * inv
                wc = w * cv
                state, last = scan_forward(a, root * wc, carries[yy])
                first = lax.broadcasted_iota(jnp.int32, (T, ch), 0) == 0
                prev = jnp.where(first, carries[yy], pltpu.roll(state, 1, 0))
                new.append(last)
                g, gp = gelu_parts(br[:, cols])
                LRU[rows, cols] = (state * g).astype(BF)
                cp = (prev - a * wc * inv) * a * r * (-DECAY_SCALE)
                AS[slot, :, cols] = a
                C6[0, rows, cols] = g.astype(BF)
                C6[1, rows, cols] = (state * gp).astype(BF)
                C6[2, rows, cols] = cp.astype(BF)
                C6[3, rows, cols] = (cp * soft * (1.0 - r)).astype(BF)
                C6[4, rows, cols] = (root * wc * (1.0 - w)).astype(BF)
                C6[5, rows, cols] = (root * w).astype(BF)
            for cp in kept(i, slot):
                cp.start()
            return tuple(new)

        lax.fori_loop(0, tiles, branch_tile, tuple(jnp.zeros((1, ch), F32) for _ in range(y_size)))
        cf_out.start()
        for i in (tiles - 2, tiles - 1):
            for cp in kept(i, i % 2):
                cp.wait()

    def out_rows(rows):
        return nt(LRU[rows, :], full(OUT))

    def out():
        PS[...] = out_rows(other).astype(BF)
        mix_copy.start()
        MIX[...] = out_rows(own)

    def mix():
        mix_copy.wait_recv()

        @pl.loop(0, half // T)
        def _(i):
            rows = rows_of(i, T)
            at = pl.ds(pl.multiple_of(base_own + i * T, T), T)
            v = T1[at, :].astype(F32) + MIX[rows, :] + PR[0, rows, :].astype(F32)
            MIX[rows, :] = v
            s = lax.rsqrt(jnp.mean(v * v, axis=1, keepdims=True) + EPS)
            T1[at, :] = (v * s * gains[1:2, :]).astype(BF)

        n2_copy.start()

    def n2():
        n2_in.wait_recv()
        cf_out.wait()

    F = 256

    def ff(j):
        def loop(hook):
            @pl.loop(0, SEQ // F)
            def _(i):
                hook(i)
                rows = rows_of(i, F)
                up = nn(T1[rows, :], full(UP[j]))
                g, gp = gelu_parts(nn(T1[rows, :], full(GATE[j])))
                C6[j, rows, :] = (g * up).astype(BF)
                C6[2 + j, rows, :] = (gp * up).astype(BF)
                C6[4 + j, rows, :] = g.astype(BF)
        return loop


    zh = z_size // 2

    def weight_grad(u, left, right):
        if SLOT[u] < UNITS:
            for chunk in (2 * SLOT[u], 2 * SLOT[u] + 1):
                ag.drain(chunk)

        @pl.loop(0, 2)
        def _(i):
            val = nn(left[rows_of(i, depth // 2), :], right[...]).astype(BF)
            for yy in range(y_size):
                W[SLOT[u], yy, pl.ds(i * zh, zh)] = val[:, yy * ch : (yy + 1) * ch].reshape(
                    zh, x_size, depth // (z_size * x_size), ch)

    def d0():
        weight_grad(DN0, TT, C6.at[0])

    def d1():
        weight_grad(DN1, TT, C6.at[1])

    def gh(hook):
        @pl.loop(0, 2 * (SEQ // F))
        def _(n):
            hook(n)
            j, i = n // (SEQ // F), lax.rem(n, SEQ // F)
            rows = rows_of(i, F)
            g = nn(SA[rows, :], full(DN0 + j))
            C6[2 + j, rows, :] = (g * C6[2 + j, rows, :].astype(F32)).astype(BF)
            C6[4 + j, rows, :] = (g * C6[4 + j, rows, :].astype(F32)).astype(BF)

    def span(base, i):
        return pl.ds(pl.multiple_of(base + i * F, F), F)

    def mlp_back(rows):
        return (nt(C6[2, rows, :], full(GA0)) + nt(C6[3, rows, :], full(GA1))
                + nt(C6[4, rows, :], full(UP0)) + nt(C6[5, rows, :], full(UP1)))

    def mlp_out(rows):
        return nt(C6[0, rows, :], full(DN0)) + nt(C6[1, rows, :], full(DN1))

    def rnn_back(rows):
        return nt(C6[5, rows, :], full(RNN)) + nt(C6[1, rows, :], full(GEL))

    def partial_rows(fn, base, dst, hook=None):
        @pl.loop(0, half // F)
        def _(i):
            if hook is not None:
                hook(i)
            dst[rows_of(i, F), :] = fn(span(base, i)).astype(dst.dtype)

    def bo():
        mix_copy.wait_send()
        partial_rows(mlp_out, base_other, PS)
        out_copy.start()

    def bw():
        partial_rows(mlp_out, base_own, gtok)

    def gno(hook):
        out_copy.wait_recv()

        @pl.loop(0, half // F)
        def _(i):
            rows = rows_of(i, F)
            PR[1, rows, :] = (MIX[rows, :] + gtok[rows, :] + PR[1, rows, :].astype(F32)).astype(BF)

        block_copy.start()
        out_copy.wait_send()
        partial_rows(mlp_back, base_other, PS, hook)
        back_copy.start()

    def gnw(hook):
        partial_rows(mlp_back, base_own, gtok, hook)

    def norm():
        acc[...] = jnp.zeros_like(acc)
        pgain[...] = jnp.zeros_like(pgain)
        n2_copy.wait_send()
        back_copy.wait_recv()

        @pl.loop(0, half // T)
        def _(i):
            rows = rows_of(i, T)
            at = pl.ds(pl.multiple_of(base_own + i * T, T), T)
            v = MIX[rows, :]
            gn = gtok[rows, :] + PR[0, rows, :].astype(F32)
            s = lax.rsqrt(jnp.mean(v * v, axis=1, keepdims=True) + EPS)
            q = gn * gains[1:2, :]
            pgain[1:2, :] += jnp.sum(gn * v * s, axis=0, keepdims=True)
            gm = SA[at, :].astype(F32) + s * q - (s * s * s) * v * jnp.mean(q * v, axis=1, keepdims=True)
            gtok[rows, :] = gm
            SA[at, :] = gm.astype(BF)

        row_copy.start()

    def ga0():
        transpose_into(TT, T1, SEQ)
        weight_grad(GA0, TT, C6.at[2])

    def ga1():
        weight_grad(GA1, TT, C6.at[3])

    def up0():
        weight_grad(UP0, TT, C6.at[4])

    def up1():
        weight_grad(UP1, TT, C6.at[5])
        cf_in.start()
        block_copy.wait()
        tok_again.start()

    def fetch(n, slot):
        i = tiles - 1 - n
        return (pltpu.make_async_copy(h_a.at[i], AS.at[slot], ts.at[0, slot]),
                pltpu.make_async_copy(h_ri.at[i], RS.at[slot], ts.at[1, slot]))

    def outg():
        for cp in fetch(0, 0):
            cp.start()
        row_in.wait_recv()
        transpose_into(TT, SA, SEQ)
        weight_grad(OUT, TT, LRU)
        cv_in.start()
        cf_in.wait()

    def back_rows(hook):
        def back_tile(n, carries):
            hook(n)
            slot = lax.rem(n, 2)
            for cp in fetch(n, slot):
                cp.wait()

            @pl.when(n + 1 < tiles)
            def _():
                for cp in fetch(n + 1, 1 - slot):
                    cp.start()

            i = tiles - 1 - n
            rows = rows_of(i, T)
            gl_all = nn(SA[rows, :], full(OUT))
            new = []
            for yy in range(y_size):
                adj_next, a_next, gco_next = carries[yy]
                cols = slice(yy * ch, (yy + 1) * ch)
                p = prm[yy]
                gl = gl_all[:, cols]
                at = AS[slot, :, cols]
                last = lax.broadcasted_iota(jnp.int32, (T, ch), 0) == T - 1
                shifted = jnp.where(last, a_next, pltpu.roll(at, T - 1, 0))
                adj, adj_first = scan_backward(shifted, gl * C6[0, rows, cols].astype(F32), adj_next)
                C6[1, rows, cols] = (gl * C6[1, rows, cols].astype(F32)).astype(BF)
                grp = adj * C6[3, rows, cols].astype(F32)
                gip = adj * C6[4, rows, cols].astype(F32)
                gr_low, gi_low = grp.astype(BF), gip.astype(BF)
                gcd = adj * C6[5, rows, cols].astype(F32)
                acc[yy, 5:6] += jnp.sum(grp, axis=0, keepdims=True)
                acc[yy, 6:7] += jnp.sum(gip, axis=0, keepdims=True)
                acc[yy, 7:8] += jnp.sum(adj * C6[2, rows, cols].astype(F32), axis=0, keepdims=True)
                C6[3, rows, cols] = gr_low
                C6[4, rows, cols] = gi_low
                parts = []
                for h in range(ch // 128):
                    hs = slice(h * 128, (h + 1) * 128)
                    hc = slice(yy * ch + h * 128, yy * ch + (h + 1) * 128)
                    parts.append(nt(jnp.concatenate([gr_low[:, hs], gi_low[:, hs]], axis=1),
                                    jnp.concatenate([hw[0, :, hc], hw[1, :, hc]], axis=1)))
                gco = gcd + jnp.concatenate(parts, axis=1)
                ext = jnp.concatenate([gco, gco_next], axis=0)
                x = RS[slot, :, cols]
                grn = p[0:1] * gco
                acc[yy, 0:1] += jnp.sum(gco * x[8:], axis=0, keepdims=True)
                acc[yy, 4:5] += jnp.sum(gco, axis=0, keepdims=True)
                for k in range(1, 4):
                    grn = grn + p[k : k + 1] * pltpu.roll(ext, T + 8 - k, 0)[:T]
                    acc[yy, k : k + 1] += jnp.sum(gco * pltpu.roll(x, k, 0)[8:], axis=0, keepdims=True)
                C6[5, rows, cols] = grn.astype(BF)
                new.append((adj_first, at[0:1], gco[0:8]))
            return tuple(new)

        zero = (jnp.zeros((1, ch), F32), jnp.zeros((1, ch), F32), jnp.zeros((8, ch), F32))
        lax.fori_loop(0, tiles, back_tile, (zero,) * y_size)

    def gel():
        transpose_into(TT, N1, SEQ)
        weight_grad(GEL, TT, C6.at[1])

    def rnn():
        weight_grad(RNN, TT, C6.at[5])

    def gn1o():
        back_copy.wait_send()
        partial_rows(rnn_back, base_other, PS)
        rnn_copy.start()

    def gn1w():
        partial_rows(rnn_back, base_own, MIX)

    def heads():
        cv_in.wait()
        if group == 1:
            small.drain(0)
            params.drain(0)
        for yy in range(y_size):
            acc[yy, 7:8] = acc[yy, 7:8] * jax.nn.sigmoid(prm[yy, 7:8])
            for h in range(ch // 128):
                hs = slice(h * 128, (h + 1) * 128)
                hc = slice(yy * ch + h * 128, yy * ch + (h + 1) * 128)
                both = lax.dot_general(LRU[:, hc], jnp.concatenate([C6[3, :, hc], C6[4, :, hc]], axis=1),
                                       (((0,), (0,)), ((), ())), preferred_element_type=F32)
                for n in range(2):
                    val = both[:, n * 128 : (n + 1) * 128]
                    if group > 1:
                        o_gs[yy, 128 * n : 128 * n + 128, hs] = val
                    else:
                        gs[0, yy, :, :, 16 * n : 16 * n + 16, hs] = val.astype(BF).reshape(z_size, x_size, 16, 128)

    def fin():
        tok_again.wait()
        rnn_copy.wait_recv()

        @pl.loop(0, half // T)
        def _(i):
            rows = rows_of(i, T)
            v = PR[1, rows, :].astype(F32)
            gn = MIX[rows, :] + PR[0, rows, :].astype(F32)
            s = lax.rsqrt(jnp.mean(v * v, axis=1, keepdims=True) + EPS)
            q = gn * gains[0:1, :]
            pgain[0:1, :] += jnp.sum(gn * v * s, axis=0, keepdims=True)
            gtok[rows, :] += s * q - (s * s * s) * v * jnp.mean(q * v, axis=1, keepdims=True)

        gain_copy.start()
        gtok_copy.start()

    def s0():
        gain_copy.wait_recv()
        rows = [pgain[n : n + 1, :] + pgain[8 + n : 9 + n, :] for n in range(2)]
        if group > 1:
            for n in range(2):
                row = jnp.concatenate([rows[n], jnp.zeros((1, 3 * ch - depth), F32)], axis=1)
                for m in range(3):
                    for yy in range(y_size):
                        acc[yy, 8 + 3 * n + m : 9 + 3 * n + m, :] = row[:, m * ch : (m + 1) * ch]
            for yy in range(y_size):
                o_gs[yy, 256:272, :] = acc[yy]
            return
        own_lanes = ch // (z_size * x_size)
        lane = lax.broadcasted_iota(jnp.int32, (8, 128), 1)
        for i in range(z_size * x_size):
            for yy in range(y_size):
                turned = pltpu.roll(acc[yy, 0:8, :], (ch - i * own_lanes) % ch, 1)[:, 0:128] if i else acc[yy, 0:8, 0:128]
                taps[...] = jnp.where(lane < own_lanes, turned, 0.0)
                for n in range(2):
                    put_gain(taps, n, rows[n][:, i * 128 : (i + 1) * 128])
                gp[0, yy, i // x_size, i % x_size] = taps[...]

    blocks = dict(pre0=pre0, pre1=pre1, pre3=pre3, out=out, mix=mix, n2=n2, d0=d0, d1=d1, bo=bo, bw=bw, ga0=ga0,
                  ga1=ga1, norm=norm, up0=up0, up1=up1, outg=outg, gel=gel, rnn=rnn, gn1o=gn1o, gn1w=gn1w, heads=heads,
                  fin=fin, s0=s0)
    blocks = {name: (1, fn) for name, fn in blocks.items()}
    blocks.update(br=(tiles, branch), ffa=(SEQ // F, ff(0)), ffb=(SEQ // F, ff(1)), gh=(2 * SEQ // F, gh),
                  gno=(half // F, gno), gnw=(half // F, gnw), t=(tiles, back_rows))

    placed = set()

    def event(chunk, k):
        if chunk < CHUNKS:
            u = chunk // 2
            if k == 0 and u in sources and u not in placed:
                placed.add(u)
                place[u].wait()
            ag.event(chunk, k)
        elif chunk < 2 * CHUNKS:
            back.event(chunk - CHUNKS, k, finals)
        elif group == 1:
            if chunk == 2 * CHUNKS:
                small.event(0, k)
                params.event(0, k)
            else:
                back_small.event(0, k, o_gs)
                back_params.event(0, k, o_gp)
                if k == 3:
                    gs_copy.start()
                    gp_copy.start()

    run_plan(PLAN, blocks, event)
    for u in (RNN, GEL):
        for chunk in (2 * u, 2 * u + 1):
            ag.drain(chunk)
    for chunk in range(CHUNKS):
        back.drain(chunk)
    if group == 1:
        back_small.drain(0)
        back_params.drain(0)
        gp_copy.wait()
    else:
        gs_copy.start()
    finals.drain()
    gtok_copy.wait()
    gs_copy.wait()
    for cp in (tok_copy, cot_copy, row_copy, rnn_copy, gain_copy):
        cp.wait_send()


def finish_kernel(block_in, gtok_in, gw, gs, gp,
                  o_block, o_gtok, o_mg, o_rnn, o_gel, o_cw, o_cb, o_rw, o_iw, o_rb, o_ib, o_dp, o_out, o_lg, o_gate, o_up,
                  o_down):
    ch = gw.shape[2]
    part, own = o_mg.shape[1], o_cb.shape[1]
    o_block[...] = block_in[...]
    o_gtok[...] = gtok_in[...]
    o_rnn[...] = gw[RNN]
    o_gel[...] = gw[GEL]
    o_out[...] = gw[OUT].T
    for j in range(2):
        cols = slice(j * ch, (j + 1) * ch)
        o_gate[:, cols] = gw[GATE[j]]
        o_up[:, cols] = gw[UP[j]]
        o_down[cols, :] = gw[DOWN[j]].T
    for h in range(ch // 128):
        o_rw[h] = gs[0, 0:16, h * 128 : (h + 1) * 128]
        o_iw[h] = gs[0, 16:32, h * 128 : (h + 1) * 128]
    block = gp[0]
    o_cw[...] = block[0:4, 0:own]
    for k, ref in ((4, o_cb), (5, o_rb), (6, o_ib), (7, o_dp)):
        ref[...] = block[k : k + 1, 0:own]
    turned = pltpu.roll(block, 64, 1)
    lane = lax.broadcasted_iota(jnp.int32, (1, 128), 1)
    for n, ref in ((0, o_mg), (1, o_lg)):
        ref[...] = jnp.where(lane < 64, turned[2 * n : 2 * n + 1], block[2 * n + 1 : 2 * n + 2])[:, 0:part]


def any_spec():
    return pl.BlockSpec(memory_space=pl.ANY)


def vmem_spec():
    return pl.BlockSpec(memory_space=pltpu.VMEM)


def body(sizes, tokens, mix_gain, rnn_weight, gelu_weight, conv_weight, conv_bias, recur_weight, input_weight,
         recur_bias, input_bias, decay_param, out_weight, mlp_gain, gate_weight, up_weight, down_weight, cotangent):
    z_size, x_size, y_size = sizes
    dp = z_size * x_size
    dp_index = lax.axis_index("dp")
    rows, depth = tokens.shape
    part, ch = rnn_weight.shape
    head_rows = recur_weight.shape[1]
    group = max(1, 16 // head_rows)
    wide = y_size * ch
    own = ch // dp
    vectors = [v[None] for v in (conv_bias, recur_bias, input_bias, decay_param, mix_gain, mlp_gain)]
    heads = [recur_weight, input_weight]
    out_w, down_w = out_weight, down_weight
    if part % 128:
        out_w, down_w = out_weight.T, down_weight.T
    shape = jax.ShapeDtypeStruct
    grid = (y_size, z_size, x_size)
    hops = z_size + x_size + y_size - 2
    t = lax.axis_index("tensor")
    joined = [conv_weight] * 3
    if group > 1:
        lanes = jnp.concatenate([conv_weight, *vectors[0:4]], axis=0).astype(F32)
        lanes = jnp.pad(lanes, ((0, 8), (0, ch - own)))
        lanes = jnp.roll(lanes, dp_index * own, axis=1)
        gain = jnp.pad(jnp.concatenate(vectors[4:6], axis=0).astype(F32), ((0, 6), (0, depth - part)))
        gain = lax.psum(jnp.roll(gain, dp_index * part, axis=1), "dp")
        every = jnp.zeros((2 * y_size, 272, ch), F32)
        for n, w in enumerate(heads):
            w = jnp.transpose(w, (1, 0, 2)).reshape(1, head_rows, ch).astype(F32)
            every = lax.dynamic_update_slice(every, w, (t, 128 * n + dp_index * head_rows, 0))
        every = lax.psum(lax.dynamic_update_slice(every, lanes[None], (t, 256, 0)), ("dp", "tensor"))
        mine = [every[2 * yy] * (1 - lax.rem(t, 2)) + every[2 * yy + 1] * lax.rem(t, 2) for yy in range(y_size)]
        joined = [jnp.stack([m[256:] for m in mine]), gain,
                  jnp.concatenate([m[0:256].reshape(2, 128, ch) for m in mine], axis=2).astype(BF)]
        heads = [jnp.zeros((ch // 128, 16, 128), BF)] * 2
    dma = pltpu.SemaphoreType.DMA
    landed = list(big_landing(sizes, part, ch).values())
    landed_params = []
    gs_out, small_grid = (y_size, 272, ch), (1, 1, 1)
    if group == 1:
        landed += list(small_landing(sizes, ch).values())
        landed_params = list(params_landing(sizes).values())
        gs_out, small_grid = (1, SMALL, ch), grid
    block_out, grad_tokens, gw, gs, gp = pl.pallas_call(
        functools.partial(block_kernel, sizes, group),
        out_shape=[shape((rows, depth), BF), shape((rows, depth), F32), shape((UNITS, part, ch), F32), shape(gs_out, F32),
                   shape((1, 8, 128), F32),
                   shape((6, SEQ, wide), BF), shape((SEQ // 128, 128, wide), F32), shape((SEQ // 128, 136, wide), F32),
                   shape((SEQ, wide), BF)],
        in_specs=[*[any_spec()] * 8, *[vmem_spec()] * 7, any_spec(), any_spec(), *([vmem_spec()] * 3 if group > 1 else [any_spec()] * 3)],
        out_specs=[any_spec()] * 9,
        scratch_shapes=[
            pltpu.VMEM((UNITS + 2, *grid, part, ch), BF), pltpu.VMEM((1, *small_grid, SMALL, ch), BF),
            pltpu.VMEM((6, SEQ, wide), BF), pltpu.VMEM((SEQ, wide), BF),
            *[pltpu.VMEM((SEQ, depth), BF)] * 4, pltpu.VMEM((rows, depth), F32),
            pltpu.VMEM((rows, depth), BF), pltpu.VMEM((2, rows, depth), BF),
            pltpu.VMEM((rows, depth), F32), pltpu.VMEM((2, 128, wide), F32), pltpu.VMEM((2, 136, wide), F32),
            pltpu.VMEM((2, max(part // 2, 16), ch), F32),
            pltpu.VMEM((y_size, 16, ch), F32), pltpu.VMEM((16, depth), F32),
            pltpu.VMEM((y_size, 16, ch), F32), pltpu.VMEM((8, depth), F32), pltpu.VMEM((2, 128, wide), BF),
            pltpu.VMEM(out_w.shape, BF), pltpu.VMEM(down_w.shape, BF), pltpu.VMEM(heads[0].shape, BF),
            pltpu.VMEM(heads[1].shape, BF), pltpu.VMEM(gs_out, F32), pltpu.VMEM((1, 8, 128), F32),
            pltpu.VMEM((8, 128), F32), pltpu.VMEM((1, *small_grid, 8, 128), F32),
            dma((CHUNKS, hops)), dma((CHUNKS, hops)), dma((CHUNKS, hops)), dma((CHUNKS, hops)),
            *[dma((1, hops))] * 8, dma((9,)), dma((9,)), dma((20,)), dma((3, 2)), dma((2,)),
            *[pltpu.VMEM(s, BF) for s in landed], *[pltpu.VMEM(s, F32) for s in landed_params],
        ],
        compiler_params=pltpu.CompilerParams(collective_id=0, has_side_effects=True, vmem_limit_bytes=VMEM_LIMIT),
        name="residual_block",
    )(tokens, cotangent, rnn_weight, gelu_weight, out_w, gate_weight, up_weight, down_w, conv_weight, *vectors, *heads,
      *joined)[:5]
    if group > 1:
        every = jnp.zeros((2 * y_size, 272, ch), F32)
        for yy in range(y_size):
            every = lax.dynamic_update_slice(every, gs[yy : yy + 1], (2 * yy + lax.rem(t, 2), 0, 0))
        gs = lax.dynamic_slice(lax.psum(every, ("dp", "tensor")), (t, 0, 0), (1, 272, ch))
        first = dp_index * head_rows
        rec = lax.dynamic_slice(gs[0], (first, 0), (head_rows, ch))
        inp = lax.dynamic_slice(gs[0], (128 + first, 0), (head_rows, ch))
        fill = jnp.zeros((16 - head_rows, ch), F32)
        par = lax.dynamic_slice(gs[0, 256:264], (0, dp_index * own), (8, own))
        gain = lax.dynamic_slice(gs[0, 264:270].reshape(2, 3 * ch), (0, dp_index * part), (2, part))
        gp = jnp.zeros((1, 8, 128), F32).at[0, :, :own].set(par).at[0, 0:4:2, 64 : 64 + part].set(gain)
        gs = jnp.concatenate([rec, fill, inp, fill], axis=0)[None]
    f_shapes = [
        shape((rows, depth), BF), shape((rows, depth), F32), shape((1, part), F32), shape((part, ch), F32),
        shape((part, ch), F32), shape((4, own), F32), shape((1, own), F32), shape((ch // 128, 16, 128), F32),
        shape((ch // 128, 16, 128), F32), shape((1, own), F32), shape((1, own), F32), shape((1, own), F32),
        shape((ch, part), F32), shape((1, part), F32), shape((part, 2 * ch), F32), shape((part, 2 * ch), F32),
        shape((2 * ch, part), F32),
    ]
    res = list(pl.pallas_call(
        finish_kernel,
        out_shape=f_shapes,
        in_specs=[vmem_spec()] * 5,
        out_specs=[vmem_spec()] * 17,
        compiler_params=pltpu.CompilerParams(vmem_limit_bytes=VMEM_LIMIT),
        name="unpack",
    )(block_out, grad_tokens, gw, gs, gp))
    for k in (2, 6, 9, 10, 11, 13):
        res[k] = res[k][0]
    for k in (7, 8):
        res[k] = res[k][:, :head_rows]
    return tuple(res)


def solution(mesh):
    dp, tensor = mesh.shape["dp"], mesh.shape["tensor"]
    x_size = 2
    sizes = (dp // x_size, x_size, tensor // 2)
    rows, split, vec = P(("dp", "tensor"), None), P("dp", "tensor"), P(("tensor", "dp"))
    head, flip, taps = P("tensor", "dp", None), P("tensor", "dp"), P(None, ("tensor", "dp"))
    return jax.shard_map(
        functools.partial(body, sizes),
        mesh=mesh,
        in_specs=(rows, P("dp"), split, split, taps, vec, head, head, vec, vec, vec, flip, P("dp"), split, split, flip,
                  rows),
        out_specs=(rows, rows, P("dp"), split, split, taps, vec, head, head, vec, vec, vec, flip, P("dp"), split, split,
                   flip),
        check_vma=False,
    )
```

```python
import functools

import jax
import jax.numpy as jnp
from jax import lax
from jax.experimental import pallas as pl
from jax.experimental.pallas import tpu as pltpu
from jax.sharding import PartitionSpec as P

SEQ = 1024
EPS = 1e-06
GUARD = 0.01
DECAY_SCALE = 8.0
GELU_K = 0.7978845608028654
GELU_C = 0.044715
BF = jnp.bfloat16
F32 = jnp.float32
MESH = pl.DeviceIdType.MESH
VMEM_LIMIT = 63 * 1024 * 1024

RNN, GEL, OUT, GA0, UP0, GA1, UP1, DN0, DN1 = range(9)
UNITS = 9
GATE, UP, DOWN = (GA0, GA1), (UP0, UP1), (DN0, DN1)
CHUNKS = 2 * UNITS
SMALL = 32
FLOW = (
    "zxy", "zxy", "zyx", "zxy", "yzx", "zyx", "zxy", "zyx", "xyz", "xzy", "yxz", "zyx", "zxy", "yzx", "zxy", "xyz",
    "zyx", "zxy",
)
BACK = (
    "yxz", "yxz", "yxz", "xzy", "xzy", "xzy", "xzy", "yzx", "xyz", "yxz", "zyx", "xzy", "yxz", "yxz", "yxz", "zyx",
    "xyz", "zxy",
)
SMALL_FLOW, SMALL_BACK = ("zyx",), ("yxz",)
PLAN = (
    10, 50, 15, 40, "pre0", 51, 41, 14, 20, "pre1", 180, 75, 45, 11, 19, 16, 55, 184, 5, 76, 12, 35, 181, 65, 9, 6,
    17, 0, 39, 30, 36, 21, 182, 59, 4, 25, 7, 1, 37, 34, 29, 80, 24, 60, 26, 13, 46, 2, 56, 64, 31, 84, 183, 18, 85,
    38, 70, 27, "pre3", 66, 3, 74, 81, 8, 22, "br", 89, 49, 32, 42, "br", 47, 71, "br", 61, 57, 86, "br", 69, "br",
    52, 28, "br", "br", "br", 62, 44, 23, 67, "out", 48, 77, "mix", 72, 82, "n2", 43, 33, "ffa", "ffa", "ffa", 54,
    58, 63, 87, "ffa", "d0", 165, 160, 73, 53, 68, "ffb", "ffb", 79, "ffb", "ffb", "d1", 170, 88, 175, 169, 78, 83,
    "gh", "gh", "gh", "gh", "gh", "gh", "gh", "gh", "bo", 161, "bw", "ga0", 120, 125, 179, "ga1", 140, "gno", "gno",
    145, "gnw", 171, "gnw", "norm", "up0", 135, 130, 162, 144, "up1", "outg", 110, 126, "t", 150, "t", 164, "t", 121,
    "t", 115, "t", 155, 129, 131, 136, 124, 146, 172, "t", "t", 149, 111, "t", "gel", "rnn", 90, 116, 114, 156, 105,
    "gn1o", "gn1w", "heads", 100, 132, 119, 95, 174, "fin", "s0", 137, 157, 151, 101, 106, 134, 185, 133, 159, 147,
    141, 139, 91, 109, 152, 112, 117, 102, 96, 154, 166, 92, 186, 148, 176, 97, 122, 142, 94, 163, 104, 113, 158,
    173, 138, 127, 187, 107, 167, 93, 177, 99, 118, 103, 153, 123, 143, 189, 128, 108, 98, 178, 168, 188,
)


def run_plan(plan, blocks, event):
    i = 0
    while i < len(plan):
        name = plan[i]
        i += 1
        if isinstance(name, int):
            event(name // 5, name % 5)
            continue
        turns, fn = blocks[name]
        if turns == 1:
            fn()
            continue
        hooks = {}
        for turn in range(1, turns):
            hooks[turn] = []
            while isinstance(plan[i], int):
                hooks[turn].append(plan[i])
                i += 1
            i += 1

        def hook(n, hooks=hooks):
            for turn, steps in hooks.items():
                if steps:
                    @pl.when(n == turn)
                    def _(steps=steps):
                        for step in steps:
                            event(step // 5, step % 5)

        fn(hook)


def nn(a, b):
    return jnp.dot(a, b, preferred_element_type=F32)


def nt(a, b):
    return lax.dot_general(a, b, (((1,), (1,)), ((), ())), preferred_element_type=F32)


def gelu_parts(v):
    v2 = v * v
    th = jnp.tanh(GELU_K * v * (1.0 + GELU_C * v2))
    half = 0.5 * (1.0 + th)
    return v * half, half + (0.5 * GELU_K) * v * (1.0 - th * th) * (1.0 + (3.0 * GELU_C) * v2)


class Net:
    def __init__(self, z_size, x_size, y_size):
        self.size = {"z": z_size, "x": x_size, "y": y_size, "c": 2}
        dp, t = lax.axis_index("dp"), lax.axis_index("tensor")
        self.at = {"z": dp // x_size, "x": lax.rem(dp, x_size), "y": t // 2, "c": lax.rem(t, 2)}
        self.off = {"z": 0, "x": z_size - 1, "y": z_size + x_size - 2}
        self.relay = z_size + x_size + y_size - 3 if z_size == 4 else None

    def shifted(self, d, j):
        n = self.size[d]
        return lax.rem(self.at[d] + (j % n), n)

    def device(self, d, j):
        at = dict(self.at)
        at[d] = self.shifted(d, j)
        return (at["z"] * self.size["x"] + at["x"], at["y"] * 2 + at["c"])

    def barrier(self):
        sem = pltpu.get_barrier_semaphore()
        count = 0
        for d in "zxyc":
            for j in range(1, self.size[d]):
                pl.semaphore_signal(sem, inc=1, device_id=self.device(d, j), device_id_type=MESH)
                count += 1
        pl.semaphore_wait(sem, count)


def chunk_rows(c, part):
    if part % 32:
        return slice(None) if c % 2 == 0 else None
    return slice(c % 2 * (part // 2), (c % 2 + 1) * (part // 2))


class Gather:
    def __init__(self, net, ref, flows, ss, rs, halves):
        self.net, self.ref, self.flows, self.ss, self.rs, self.halves = net, ref, flows, ss, rs, halves

    def region(self, c, s, at):
        order = self.flows[c]
        idx = [slice(None) if d in order[:s] else at[d] for d in "yzx"]
        if not self.halves:
            return self.ref.at[(c, *idx)]
        return self.ref.at[(c // 2, *idx, chunk_rows(c, self.ref.shape[4]))]

    def copy(self, c, s, j, sender, origin=None, send=None, recv=None):
        d = self.flows[c][s]
        at = dict(self.net.at)
        if sender:
            at[d] = self.net.shifted(d, -j)
        if origin is not None:
            at[d] = origin
        region = self.region(c, s, at)
        k = self.net.off[d] + j - 1
        return pltpu.make_async_remote_copy(
            src_ref=region, dst_ref=region, send_sem=self.ss.at[c, k if send is None else send],
            recv_sem=self.rs.at[c, k if recv is None else recv], device_id=self.net.device(d, j), device_id_type=MESH)

    def relayed(self, c, s):
        return self.net.relay is not None and self.flows[c][s] == "z"

    def sends(self, c, s, act):
        if not self.relayed(c, s):
            for j in range(1, self.net.size[self.flows[c][s]]):
                act(self.copy(c, s, j, False))
            return
        z = self.net.at["z"]
        act(self.copy(c, s, 2, False))
        pl.when(z != 3)(lambda: act(self.copy(c, s, 1, False)))
        pl.when(z != 0)(lambda: act(self.copy(c, s, 3, False)))

    def passes_on(self, c, s, act):
        z = self.net.at["z"]
        k = self.net.relay
        pl.when(z == 2)(lambda: act(self.copy(c, s, 1, False, 0, k, 2)))
        pl.when(z == 1)(lambda: act(self.copy(c, s, 3, False, 3, k, 0)))

    def event(self, c, k):
        if self.halves and chunk_rows(c, self.ref.shape[4]) is None:
            return
        if k == 4:
            s = self.flows[c].index("z")
            if self.relayed(c, s):
                self.copy(c, s, 2, True).wait_recv()
                self.passes_on(c, s, lambda cp: cp.start())
            return
        if k:
            for j in range(1, self.net.size[self.flows[c][k - 1]]):
                if not (self.relayed(c, k - 1) and j == 2):
                    self.copy(c, k - 1, j, True).wait_recv()
        if k < 3:
            self.sends(c, k, lambda cp: cp.start())

    def drain(self, c):
        if self.halves and chunk_rows(c, self.ref.shape[4]) is None:
            return
        for s in range(3):
            self.sends(c, s, lambda cp: cp.wait_send())
            if self.relayed(c, s):
                self.passes_on(c, s, lambda cp: cp.wait_send())


def pair_copy(net, src, dst, ss, rs, k):
    return pltpu.make_async_remote_copy(
        src_ref=src, dst_ref=dst, send_sem=ss.at[k], recv_sem=rs.at[k],
        device_id=net.device("c", 1), device_id_type=MESH)


def scan_forward(a, b, carry):
    rows, cols = a.shape
    a = a.reshape(rows // 8, 8, cols)
    b = b.reshape(rows // 8, 8, cols)
    place = lax.broadcasted_iota(jnp.int32, (rows // 8, 8, cols), 1)
    for k in (1, 2, 4):
        keep = place >= k
        b = b + a * jnp.where(keep, pltpu.roll(b, k, 1), 0.0)
        a = a * jnp.where(keep, pltpu.roll(a, k, 1), 1.0)
    out = []
    for g in range(rows // 8):
        s = b[g] + a[g] * carry
        out.append(s)
        carry = s[7:8]
    return jnp.concatenate(out, axis=0), carry


def scan_backward(a, b, carry):
    rows, cols = a.shape
    a = a.reshape(rows // 8, 8, cols)
    b = b.reshape(rows // 8, 8, cols)
    place = lax.broadcasted_iota(jnp.int32, (rows // 8, 8, cols), 1)
    for k in (1, 2, 4):
        keep = place < 8 - k
        b = b + a * jnp.where(keep, pltpu.roll(b, 8 - k, 1), 0.0)
        a = a * jnp.where(keep, pltpu.roll(a, 8 - k, 1), 1.0)
    out = []
    for g in reversed(range(rows // 8)):
        s = b[g] + a[g] * carry
        out.append(s)
        carry = s[0:1]
    return jnp.concatenate(out[::-1], axis=0), carry


def rows_of(i, n):
    return pl.ds(pl.multiple_of(i * n, n), n)


def join_params(gp, prm, gains, sizes):
    z_size, x_size, y_size = sizes
    ch = prm.shape[2]
    own = ch // (z_size * x_size)
    lane = lax.broadcasted_iota(jnp.int32, (8, 128), 1)
    for yy in range(y_size):
        total = jnp.zeros((8, ch), F32)
        for i in range(z_size * x_size):
            block = gp[0, yy, i // x_size, i % x_size]
            row = jnp.concatenate([jnp.where(lane < own, block, 0.0), jnp.zeros((8, ch - 128), F32)], axis=1)
            total = total + (pltpu.roll(row, i * own, 1) if i else row)
        prm[yy] = jnp.concatenate([total, jnp.zeros((8, ch), F32)], axis=0)
    for i in range(z_size * x_size):
        block = gp[0, 0, i // x_size, i % x_size]
        turned = pltpu.roll(block, 64, 1)
        for n in range(2):
            gains[n : n + 1, i * 128 : (i + 1) * 128] = jnp.where(
                lane[0:1] < 64, turned[2 * n : 2 * n + 1], block[2 * n + 1 : 2 * n + 2])


def put_gain(block, n, row):
    turned = pltpu.roll(jnp.broadcast_to(row, (8, 128)), 64, 1)
    block[2 * n : 2 * n + 1, 64:128] = turned[0:1, 64:128]
    block[2 * n + 1 : 2 * n + 2, 64:128] = row[:, 64:128]


def head_weight(gs, yy, first):
    blocks = gs[0, yy, :, :, first : first + 16, :]
    return blocks.reshape(-1, blocks.shape[-1])


def transpose_into(dst, src, n, step=256):
    @pl.loop(0, n // step)
    def _(i):
        dst[:, rows_of(i, step)] = src[rows_of(i, step), :].T


class Scatter:
    def __init__(self, net, ref, flows, bufs, ss, rs, halves):
        self.net, self.ref, self.flows, self.bufs, self.ss, self.rs, self.halves = net, ref, flows, bufs, ss, rs, halves

    def rows(self, c):
        return chunk_rows(c, self.ref.shape[4]) if self.halves else slice(None)

    def slot(self, c):
        return SLOT[c // 2] if self.halves else c

    def copy(self, c, s, j, owner=None, slot=None, k=None):
        order = self.flows[c]
        d = order[s]
        at = dict(self.net.at)
        at[d] = self.net.shifted(d, j) if owner is None else owner
        idx = [at[e] if e in order[: s + 1] else slice(None) for e in "yzx"]
        k = self.net.off[d] + j - 1 if k is None else k
        return pltpu.make_async_remote_copy(
            src_ref=self.ref.at[(self.slot(c), *idx, self.rows(c))], dst_ref=self.bufs[c, s].at[j - 1 if slot is None else slot],
            send_sem=self.ss.at[c, k], recv_sem=self.rs.at[c, k],
            device_id=self.net.device(d, j), device_id_type=MESH)

    def relayed(self, c, s):
        return self.net.relay is not None and self.flows[c][s] == "z"

    def hops(self, c, s):
        return range(1, self.net.size[self.flows[c][s]])

    def far(self, c, s, act):
        z = self.net.at["z"]
        pl.when(z == 3)(lambda: act(self.copy(c, s, 3, 0, 3, self.net.relay)))
        pl.when(z == 0)(lambda: act(self.copy(c, s, 1, 3, 3, self.net.relay)))

    def sends(self, c, s, act):
        if not self.relayed(c, s):
            for j in self.hops(c, s):
                act(self.copy(c, s, j))
            return
        z = self.net.at["z"]
        self.far(c, s, act)
        pl.when(jnp.logical_or(z == 0, z == 3))(lambda: act(self.copy(c, s, 2)))
        pl.when(z != 3)(lambda: act(self.copy(c, s, 1)))
        pl.when(z != 0)(lambda: act(self.copy(c, s, 3)))

    def over(self, names, fn, place):
        if not names:
            fn(place)
        elif names[0] == "z":
            @pl.loop(0, self.net.size["z"])
            def _(z):
                self.over(names[1:], fn, {**place, "z": z})
        else:
            for n in range(self.net.size[names[0]]):
                self.over(names[1:], fn, {**place, names[0]: n})

    def pass_on(self, c, s):
        order = self.flows[c]
        rest = [e for e in "zyx" if e not in order[: s + 1]]
        buf = self.bufs[c, s]
        rows = self.rows(c)
        z = self.net.at["z"]

        def middle(owner):
            def fn():
                self.copy(c, s, 1, None, 3, self.net.relay).wait_recv()

                def block(place):
                    place = {**place, "z": owner}
                    idx = (self.slot(c), *[place[e] if e in place else self.net.at[e] for e in "yzx"], rows)
                    got = buf[(3, *[place[e] for e in "yzx" if e in rest])]
                    self.ref[idx] = (self.ref[idx].astype(F32) + got.astype(F32)).astype(self.ref.dtype)

                self.over(rest, block, {})
                self.copy(c, s, 2).start()
            return fn

        def end(unused):
            def fn():
                def block(place):
                    buf[(unused, *[place[e] for e in "yzx" if e in rest])] = jnp.zeros(buf.shape[-2:], buf.dtype)

                self.over(rest, block, {})
            return fn

        pl.when(z == 0)(end(0))
        pl.when(z == 1)(middle(3))
        pl.when(z == 2)(middle(0))
        pl.when(z == 3)(end(2))

    def add(self, c, s, out):
        order = self.flows[c]
        z = self.net.at["z"]
        for j in self.hops(c, s):
            take = self.copy(c, s, j).wait_recv
            if self.relayed(c, s) and j != 2:
                pl.when(z != (0 if j == 1 else 3))(take)
            else:
                take()
        rest = [e for e in "zyx" if e not in order[: s + 1]]
        buf = self.bufs[c, s]
        rows = self.rows(c)

        def block(place):
            idx = (self.slot(c), *[place[e] if e in place else self.net.at[e] for e in "yzx"], rows)
            total = self.ref[idx].astype(F32)
            for j in self.hops(c, s):
                total = total + buf[(j - 1, *[place[e] for e in "yzx" if e in place])].astype(F32)
            if s < 2:
                self.ref[idx] = total.astype(self.ref.dtype)
            elif self.halves:
                out.put(c // 2, rows, total)
            else:
                out[c] = total

        self.over(rest, block, {})

    def event(self, c, k, out):
        if self.rows(c) is None:
            return
        if k == 4:
            s = self.flows[c].index("z")
            if self.relayed(c, s):
                self.pass_on(c, s)
            return
        if k:
            self.add(c, k - 1, out)
        if k < 3:
            self.sends(c, k, lambda cp: cp.start())
        else:
            self.drain(c)

    def drain(self, c):
        if self.rows(c) is None:
            return
        z = self.net.at["z"]
        for s in range(3):
            self.sends(c, s, lambda cp: cp.wait_send())
            if self.relayed(c, s):
                pl.when(jnp.logical_or(z == 1, z == 2))(lambda: self.copy(c, s, 2).wait_send())


def landing(flows, sizes, rows, ch):
    size = dict(zip("zxy", sizes))
    shapes = {}
    for c, order in enumerate(flows):
        n = rows(c)
        for s in range(3):
            if n:
                rest = [size[e] for e in "yzx" if e not in order[: s + 1]]
                places = 4 if order[s] == "z" and size["z"] == 4 else size[order[s]] - 1
                shapes[c, s] = (places, *rest, n, ch)
    return shapes


SLOT = {DN0: 9, DN1: 10, GA0: DN0, GA1: DN1, UP0: GA0, UP1: GA1, OUT: UP0, GEL: UP1, RNN: OUT}


def big_landing(sizes, part, ch):
    def rows(c):
        cut = chunk_rows(c, part)
        return 0 if cut is None else len(range(part)[cut])

    return landing(BACK, sizes, rows, ch)


def small_landing(sizes, ch):
    return landing(SMALL_BACK, sizes, lambda c: SMALL, ch)


def params_landing(sizes):
    return landing(SMALL_BACK, sizes, lambda c: 8, 128)


class Finals:
    def __init__(self, ref, out, sem):
        self.ref, self.out, self.sem, self.copies = ref, out, sem, []

    def copy(self, n):
        u, rows = self.copies[n]
        return pltpu.make_async_copy(self.ref.at[n % 2], self.out.at[u, rows], self.sem.at[n % 2])

    def put(self, u, rows, total):
        n = len(self.copies)
        self.copies.append((u, rows))
        if n >= 2:
            self.copy(n - 2).wait()
        self.ref[n % 2] = total
        self.copy(n).start()

    def drain(self):
        for n in range(max(0, len(self.copies) - 2), len(self.copies)):
            self.copy(n).wait()


def block_kernel(sizes, group,
                 tok, cot, w_rnn, w_gel, out_h, w_gate, w_up, down_h, taps_in, cb_in, rb_in, ib_in, dp_in, mg_in, lg_in, rec_h, inp_h, prm_in, gains_in, hw_in,
                 o_block, o_gtok, o_gw, gs_h, gp_h, h_cf, h_a, h_ri, h_cv,
                 W, gs, C6, LRU, T1, SA, N1, TT, MIX, PS, PR, gtok, AS, RS, FB, acc, pgain, prm, gains, hw,
                 w_out, w_down, rec_in, inp_in, o_gs, o_gp, taps, gp,
                 ss, rs, bss, brs, sss, srs, bsss, bsrs, pss, prs, bpss, bprs, ps, pr, ls, ts, fs, *landed):
    net = Net(*sizes)
    z_size, x_size, y_size = sizes
    c = net.at["c"]
    half = SEQ // 2
    ch = W.shape[-1]
    part = W.shape[4]
    depth = T1.shape[1]
    own, other = pl.ds(pl.multiple_of(c * half, half), half), pl.ds(pl.multiple_of((1 - c) * half, half), half)
    base_own, base_other = c * half, (1 - c) * half
    mine = (net.at["y"], net.at["z"], net.at["x"])
    dp_index = lax.axis_index("dp")

    sources = {RNN: w_rnn, GEL: w_gel, GA0: w_gate.at[:, 0:ch], GA1: w_gate.at[:, ch : 2 * ch], UP0: w_up.at[:, 0:ch],
               UP1: w_up.at[:, ch : 2 * ch]}
    place = {u: pltpu.make_async_copy(src, W.at[(u, *mine)], ls.at[u]) for u, src in sources.items()}
    place["tok"] = pltpu.make_async_copy(tok, T1.at[own], ls.at[OUT])
    place["cot"] = pltpu.make_async_copy(cot, SA.at[own], ls.at[DN0])
    for n, (name, src, dst) in enumerate((("out", out_h, w_out), ("down", down_h, w_down), ("rec", rec_h, rec_in),
                                          ("inp", inp_h, inp_in))):
        place[name] = pltpu.make_async_copy(src, dst, ls.at[15 + n])
    for cp in place.values():
        cp.start()
    net.barrier()

    ag = Gather(net, W, FLOW, ss, rs, True)
    shapes = big_landing(sizes, part, ch)
    back = Scatter(net, W, BACK, dict(zip(shapes, landed)), bss, brs, True)
    small = back_small = params = back_params = None
    if group == 1:
        small = Gather(net, gs, SMALL_FLOW, sss, srs, False)
        tail = landed[len(shapes):]
        params = Gather(net, gp, SMALL_FLOW, pss, prs, False)
        back_params = Scatter(net, gp, SMALL_BACK, dict(zip(params_landing(sizes), tail[3:])), bpss, bprs, False)
        back_small = Scatter(net, gs, SMALL_BACK, dict(zip(small_landing(sizes, ch), tail)), bsss, bsrs, False)

    tok_copy = pair_copy(net, tok, T1.at[own], ps, pr, 0)
    cot_copy = pair_copy(net, cot, SA.at[own], ps, pr, 1)
    tok_in = pair_copy(net, tok, T1.at[other], ps, pr, 0)
    cot_in = pair_copy(net, cot, SA.at[other], ps, pr, 1)
    mix_copy = pair_copy(net, PS, PR.at[0], ps, pr, 2)
    n2_copy = pair_copy(net, T1.at[own], T1.at[own], ps, pr, 3)
    n2_in = pair_copy(net, T1.at[other], T1.at[other], ps, pr, 3)
    back_copy = pair_copy(net, PS, PR.at[0], ps, pr, 4)
    row_copy = pair_copy(net, SA.at[own], SA.at[own], ps, pr, 5)
    row_in = pair_copy(net, SA.at[other], SA.at[other], ps, pr, 5)
    out_copy = pair_copy(net, PS, PR.at[1], ps, pr, 6)
    rnn_copy = pair_copy(net, PS, PR.at[0], ps, pr, 7)
    gain_copy = pair_copy(net, pgain.at[0:8], pgain.at[8:16], ps, pr, 8)
    cf_out = pltpu.make_async_copy(C6, h_cf, ls.at[9])
    cf_in = pltpu.make_async_copy(h_cf, C6, ls.at[10])
    cv_in = pltpu.make_async_copy(h_cv, LRU, ls.at[11])
    tok_again = pltpu.make_async_copy(tok, PR.at[1], ls.at[12])
    block_copy = pltpu.make_async_copy(PR.at[1], o_block, ls.at[13])
    gtok_copy = pltpu.make_async_copy(gtok, o_gtok, ls.at[14])
    gs_copy = pltpu.make_async_copy(o_gs, gs_h, ls.at[8])
    gp_copy = pltpu.make_async_copy(o_gp, gp_h, ls.at[19])

    tok_copy.start()
    cot_copy.start()

    def full(u):
        return jnp.concatenate([W[u, yy].reshape(depth, ch) for yy in range(y_size)], axis=1)

    finals = Finals(FB, o_gw, fs)


    def pre0():
        for name in ("out", "down", "rec", "inp"):
            place[name].wait()
        if group == 1:
            width = taps_in.shape[1]
            taps[...] = jnp.zeros_like(taps)
            taps[0:4, 0:width] = taps_in[...].astype(F32)
            for n, ref in enumerate((cb_in, rb_in, ib_in, dp_in)):
                taps[4 + n : 5 + n, 0:width] = ref[...].astype(F32)
            for n, ref in enumerate((mg_in, lg_in)):
                put_gain(taps, n, ref[...].astype(F32))
            gp[(0, *mine)] = taps[...]
            for n, src in enumerate((rec_in, inp_in)):
                for h in range(ch // 128):
                    gs[(0, *mine, slice(16 * n, 16 * n + 16), slice(h * 128, (h + 1) * 128))] = src[h]
        if part % 128:
            W[(OUT, *mine)] = w_out[...]
            W[(DN0, *mine)] = w_down[:, :ch]
            W[(DN1, *mine)] = w_down[:, ch:]
        else:
            W[(OUT, *mine)] = w_out[...].T
            W[(DN0, *mine)] = w_down[:ch, :].T
            W[(DN1, *mine)] = w_down[ch:, :].T

    def pre1():
        place["tok"].wait()
        place["cot"].wait()
        cot_in.wait_recv()
        transpose_into(TT, SA, SEQ)
        tok_in.wait_recv()

    def pre3():
        if group == 1:
            join_params(gp, prm, gains, sizes)
            for yy in range(y_size):
                for n in range(2):
                    hw[n, :, yy * ch : (yy + 1) * ch] = head_weight(gs, yy, 16 * n)
        else:
            prm[...] = prm_in[...]
            gains[...] = gains_in[...]
            hw[...] = hw_in[...]
        RS[1, 128:136, :] = jnp.zeros((8, y_size * ch), F32)

        @pl.loop(0, SEQ // 128)
        def _(i):
            v = T1[rows_of(i, 128), :].astype(F32)
            s = lax.rsqrt(jnp.mean(v * v, axis=1, keepdims=True) + EPS)
            N1[rows_of(i, 128), :] = (v * s * gains[0:1, :]).astype(BF)

    T = 128
    tiles = SEQ // T

    def kept(i, slot):
        return (pltpu.make_async_copy(AS.at[slot], h_a.at[i], ts.at[0, slot]),
                pltpu.make_async_copy(RS.at[slot], h_ri.at[i], ts.at[1, slot]),
                pltpu.make_async_copy(PS.at[rows_of(slot, T), 0 : y_size * ch], h_cv.at[rows_of(i, T)], ts.at[2, slot]))

    def branch(hook):
        def branch_tile(i, carries):
            hook(i)
            slot = lax.rem(i, 2)

            @pl.when(i >= 2)
            def _():
                for cp in kept(i - 2, slot):
                    cp.wait()

            RS[slot, 0:8, :] = RS[1 - slot, 128:136, :]
            RS[slot, 8:136, :] = nn(N1[rows_of(i, T), :], full(RNN))
            rows = rows_of(i, T)
            br = nn(N1[rows, :], full(GEL))
            new = []
            for yy in range(y_size):
                cols = slice(yy * ch, (yy + 1) * ch)
                p = prm[yy]
                x = RS[slot, :, cols]
                cv = p[4:5] + p[0:1] * x[8:]
                for k in range(1, 4):
                    cv = cv + p[k : k + 1] * pltpu.roll(x, k, 0)[8:]
                cv_low = cv.astype(BF)
                PS[pl.ds(pl.multiple_of(slot * T, T), T), cols] = cv_low
                cv = cv_low.astype(F32)
                rec, inp = [], []
                for h in range(ch // 128):
                    hc = slice(yy * ch + h * 128, yy * ch + (h + 1) * 128)
                    both = nn(cv_low[:, h * 128 : (h + 1) * 128], jnp.concatenate([hw[0, :, hc], hw[1, :, hc]], axis=1))
                    rec.append(both[:, :128])
                    inp.append(both[:, 128:])
                r = jax.nn.sigmoid(jnp.concatenate(rec, axis=1) + p[5:6])
                w = jax.nn.sigmoid(jnp.concatenate(inp, axis=1) + p[6:7])
                soft = jnp.log1p(jnp.exp(-jnp.abs(p[7:8]))) + jnp.maximum(p[7:8], 0.0)
                a = jnp.exp((-DECAY_SCALE * soft) * r)
                u = 1.0 - a * a + GUARD
                inv = lax.rsqrt(u)
                root = u * inv
                wc = w * cv
                state, last = scan_forward(a, root * wc, carries[yy])
                first = lax.broadcasted_iota(jnp.int32, (T, ch), 0) == 0
                prev = jnp.where(first, carries[yy], pltpu.roll(state, 1, 0))
                new.append(last)
                g, gp = gelu_parts(br[:, cols])
                LRU[rows, cols] = (state * g).astype(BF)
                cp = (prev - a * wc * inv) * a * r * (-DECAY_SCALE)
                AS[slot, :, cols] = a
                C6[0, rows, cols] = g.astype(BF)
                C6[1, rows, cols] = (state * gp).astype(BF)
                C6[2, rows, cols] = cp.astype(BF)
                C6[3, rows, cols] = (cp * soft * (1.0 - r)).astype(BF)
                C6[4, rows, cols] = (root * wc * (1.0 - w)).astype(BF)
                C6[5, rows, cols] = (root * w).astype(BF)
            for cp in kept(i, slot):
                cp.start()
            return tuple(new)

        lax.fori_loop(0, tiles, branch_tile, tuple(jnp.zeros((1, ch), F32) for _ in range(y_size)))
        cf_out.start()
        for i in (tiles - 2, tiles - 1):
            for cp in kept(i, i % 2):
                cp.wait()

    def out_rows(rows):
        return nt(LRU[rows, :], full(OUT))

    def out():
        PS[...] = out_rows(other).astype(BF)
        mix_copy.start()
        MIX[...] = out_rows(own)

    def mix():
        mix_copy.wait_recv()

        @pl.loop(0, half // T)
        def _(i):
            rows = rows_of(i, T)
            at = pl.ds(pl.multiple_of(base_own + i * T, T), T)
            v = T1[at, :].astype(F32) + MIX[rows, :] + PR[0, rows, :].astype(F32)
            MIX[rows, :] = v
            s = lax.rsqrt(jnp.mean(v * v, axis=1, keepdims=True) + EPS)
            T1[at, :] = (v * s * gains[1:2, :]).astype(BF)

        n2_copy.start()

    def n2():
        n2_in.wait_recv()
        cf_out.wait()

    F = 256

    def ff(j):
        def loop(hook):
            @pl.loop(0, SEQ // F)
            def _(i):
                hook(i)
                rows = rows_of(i, F)
                up = nn(T1[rows, :], full(UP[j]))
                g, gp = gelu_parts(nn(T1[rows, :], full(GATE[j])))
                C6[j, rows, :] = (g * up).astype(BF)
                C6[2 + j, rows, :] = (gp * up).astype(BF)
                C6[4 + j, rows, :] = g.astype(BF)
        return loop


    zh = z_size // 2

    def weight_grad(u, left, right):
        if SLOT[u] < UNITS:
            for chunk in (2 * SLOT[u], 2 * SLOT[u] + 1):
                ag.drain(chunk)

        @pl.loop(0, 2)
        def _(i):
            val = nn(left[rows_of(i, depth // 2), :], right[...]).astype(BF)
            for yy in range(y_size):
                W[SLOT[u], yy, pl.ds(i * zh, zh)] = val[:, yy * ch : (yy + 1) * ch].reshape(
                    zh, x_size, depth // (z_size * x_size), ch)

    def d0():
        weight_grad(DN0, TT, C6.at[0])

    def d1():
        weight_grad(DN1, TT, C6.at[1])

    def gh(hook):
        @pl.loop(0, 2 * (SEQ // F))
        def _(n):
            hook(n)
            j, i = n // (SEQ // F), lax.rem(n, SEQ // F)
            rows = rows_of(i, F)
            g = nn(SA[rows, :], full(DN0 + j))
            C6[2 + j, rows, :] = (g * C6[2 + j, rows, :].astype(F32)).astype(BF)
            C6[4 + j, rows, :] = (g * C6[4 + j, rows, :].astype(F32)).astype(BF)

    def span(base, i):
        return pl.ds(pl.multiple_of(base + i * F, F), F)

    def mlp_back(rows):
        return (nt(C6[2, rows, :], full(GA0)) + nt(C6[3, rows, :], full(GA1))
                + nt(C6[4, rows, :], full(UP0)) + nt(C6[5, rows, :], full(UP1)))

    def mlp_out(rows):
        return nt(C6[0, rows, :], full(DN0)) + nt(C6[1, rows, :], full(DN1))

    def rnn_back(rows):
        return nt(C6[5, rows, :], full(RNN)) + nt(C6[1, rows, :], full(GEL))

    def partial_rows(fn, base, dst, hook=None):
        @pl.loop(0, half // F)
        def _(i):
            if hook is not None:
                hook(i)
            dst[rows_of(i, F), :] = fn(span(base, i)).astype(dst.dtype)

    def bo():
        mix_copy.wait_send()
        partial_rows(mlp_out, base_other, PS)
        out_copy.start()

    def bw():
        partial_rows(mlp_out, base_own, gtok)

    def gno(hook):
        out_copy.wait_recv()

        @pl.loop(0, half // F)
        def _(i):
            rows = rows_of(i, F)
            PR[1, rows, :] = (MIX[rows, :] + gtok[rows, :] + PR[1, rows, :].astype(F32)).astype(BF)

        block_copy.start()
        out_copy.wait_send()
        partial_rows(mlp_back, base_other, PS, hook)
        back_copy.start()

    def gnw(hook):
        partial_rows(mlp_back, base_own, gtok, hook)

    def norm():
        acc[...] = jnp.zeros_like(acc)
        pgain[...] = jnp.zeros_like(pgain)
        n2_copy.wait_send()
        back_copy.wait_recv()

        @pl.loop(0, half // T)
        def _(i):
            rows = rows_of(i, T)
            at = pl.ds(pl.multiple_of(base_own + i * T, T), T)
            v = MIX[rows, :]
            gn = gtok[rows, :] + PR[0, rows, :].astype(F32)
            s = lax.rsqrt(jnp.mean(v * v, axis=1, keepdims=True) + EPS)
            q = gn * gains[1:2, :]
            pgain[1:2, :] += jnp.sum(gn * v * s, axis=0, keepdims=True)
            gm = SA[at, :].astype(F32) + s * q - (s * s * s) * v * jnp.mean(q * v, axis=1, keepdims=True)
            gtok[rows, :] = gm
            SA[at, :] = gm.astype(BF)

        row_copy.start()

    def ga0():
        transpose_into(TT, T1, SEQ)
        weight_grad(GA0, TT, C6.at[2])

    def ga1():
        weight_grad(GA1, TT, C6.at[3])

    def up0():
        weight_grad(UP0, TT, C6.at[4])

    def up1():
        weight_grad(UP1, TT, C6.at[5])
        cf_in.start()
        block_copy.wait()
        tok_again.start()

    def fetch(n, slot):
        i = tiles - 1 - n
        return (pltpu.make_async_copy(h_a.at[i], AS.at[slot], ts.at[0, slot]),
                pltpu.make_async_copy(h_ri.at[i], RS.at[slot], ts.at[1, slot]))

    def outg():
        for cp in fetch(0, 0):
            cp.start()
        row_in.wait_recv()
        transpose_into(TT, SA, SEQ)
        weight_grad(OUT, TT, LRU)
        cv_in.start()
        cf_in.wait()

    def back_rows(hook):
        def back_tile(n, carries):
            hook(n)
            slot = lax.rem(n, 2)
            for cp in fetch(n, slot):
                cp.wait()

            @pl.when(n + 1 < tiles)
            def _():
                for cp in fetch(n + 1, 1 - slot):
                    cp.start()

            i = tiles - 1 - n
            rows = rows_of(i, T)
            gl_all = nn(SA[rows, :], full(OUT))
            new = []
            for yy in range(y_size):
                adj_next, a_next, gco_next = carries[yy]
                cols = slice(yy * ch, (yy + 1) * ch)
                p = prm[yy]
                gl = gl_all[:, cols]
                at = AS[slot, :, cols]
                last = lax.broadcasted_iota(jnp.int32, (T, ch), 0) == T - 1
                shifted = jnp.where(last, a_next, pltpu.roll(at, T - 1, 0))
                adj, adj_first = scan_backward(shifted, gl * C6[0, rows, cols].astype(F32), adj_next)
                C6[1, rows, cols] = (gl * C6[1, rows, cols].astype(F32)).astype(BF)
                grp = adj * C6[3, rows, cols].astype(F32)
                gip = adj * C6[4, rows, cols].astype(F32)
                gr_low, gi_low = grp.astype(BF), gip.astype(BF)
                gcd = adj * C6[5, rows, cols].astype(F32)
                acc[yy, 5:6] += jnp.sum(grp, axis=0, keepdims=True)
                acc[yy, 6:7] += jnp.sum(gip, axis=0, keepdims=True)
                acc[yy, 7:8] += jnp.sum(adj * C6[2, rows, cols].astype(F32), axis=0, keepdims=True)
                C6[3, rows, cols] = gr_low
                C6[4, rows, cols] = gi_low
                parts = []
                for h in range(ch // 128):
                    hs = slice(h * 128, (h + 1) * 128)
                    hc = slice(yy * ch + h * 128, yy * ch + (h + 1) * 128)
                    parts.append(nt(jnp.concatenate([gr_low[:, hs], gi_low[:, hs]], axis=1),
                                    jnp.concatenate([hw[0, :, hc], hw[1, :, hc]], axis=1)))
                gco = gcd + jnp.concatenate(parts, axis=1)
                ext = jnp.concatenate([gco, gco_next], axis=0)
                x = RS[slot, :, cols]
                grn = p[0:1] * gco
                acc[yy, 0:1] += jnp.sum(gco * x[8:], axis=0, keepdims=True)
                acc[yy, 4:5] += jnp.sum(gco, axis=0, keepdims=True)
                for k in range(1, 4):
                    grn = grn + p[k : k + 1] * pltpu.roll(ext, T + 8 - k, 0)[:T]
                    acc[yy, k : k + 1] += jnp.sum(gco * pltpu.roll(x, k, 0)[8:], axis=0, keepdims=True)
                C6[5, rows, cols] = grn.astype(BF)
                new.append((adj_first, at[0:1], gco[0:8]))
            return tuple(new)

        zero = (jnp.zeros((1, ch), F32), jnp.zeros((1, ch), F32), jnp.zeros((8, ch), F32))
        lax.fori_loop(0, tiles, back_tile, (zero,) * y_size)

    def gel():
        transpose_into(TT, N1, SEQ)
        weight_grad(GEL, TT, C6.at[1])

    def rnn():
        weight_grad(RNN, TT, C6.at[5])

    def gn1o():
        back_copy.wait_send()
        partial_rows(rnn_back, base_other, PS)
        rnn_copy.start()

    def gn1w():
        partial_rows(rnn_back, base_own, MIX)

    def heads():
        cv_in.wait()
        if group == 1:
            small.drain(0)
            params.drain(0)
        for yy in range(y_size):
            acc[yy, 7:8] = acc[yy, 7:8] * jax.nn.sigmoid(prm[yy, 7:8])
            for h in range(ch // 128):
                hs = slice(h * 128, (h + 1) * 128)
                hc = slice(yy * ch + h * 128, yy * ch + (h + 1) * 128)
                both = lax.dot_general(LRU[:, hc], jnp.concatenate([C6[3, :, hc], C6[4, :, hc]], axis=1),
                                       (((0,), (0,)), ((), ())), preferred_element_type=F32)
                for n in range(2):
                    val = both[:, n * 128 : (n + 1) * 128]
                    if group > 1:
                        o_gs[yy, 128 * n : 128 * n + 128, hs] = val
                    else:
                        gs[0, yy, :, :, 16 * n : 16 * n + 16, hs] = val.astype(BF).reshape(z_size, x_size, 16, 128)

    def fin():
        tok_again.wait()
        rnn_copy.wait_recv()

        @pl.loop(0, half // T)
        def _(i):
            rows = rows_of(i, T)
            v = PR[1, rows, :].astype(F32)
            gn = MIX[rows, :] + PR[0, rows, :].astype(F32)
            s = lax.rsqrt(jnp.mean(v * v, axis=1, keepdims=True) + EPS)
            q = gn * gains[0:1, :]
            pgain[0:1, :] += jnp.sum(gn * v * s, axis=0, keepdims=True)
            gtok[rows, :] += s * q - (s * s * s) * v * jnp.mean(q * v, axis=1, keepdims=True)

        gain_copy.start()
        gtok_copy.start()

    def s0():
        gain_copy.wait_recv()
        rows = [pgain[n : n + 1, :] + pgain[8 + n : 9 + n, :] for n in range(2)]
        if group > 1:
            for n in range(2):
                row = jnp.concatenate([rows[n], jnp.zeros((1, 3 * ch - depth), F32)], axis=1)
                for m in range(3):
                    for yy in range(y_size):
                        acc[yy, 8 + 3 * n + m : 9 + 3 * n + m, :] = row[:, m * ch : (m + 1) * ch]
            for yy in range(y_size):
                o_gs[yy, 256:272, :] = acc[yy]
            return
        own_lanes = ch // (z_size * x_size)
        lane = lax.broadcasted_iota(jnp.int32, (8, 128), 1)
        for i in range(z_size * x_size):
            for yy in range(y_size):
                turned = pltpu.roll(acc[yy, 0:8, :], (ch - i * own_lanes) % ch, 1)[:, 0:128] if i else acc[yy, 0:8, 0:128]
                taps[...] = jnp.where(lane < own_lanes, turned, 0.0)
                for n in range(2):
                    put_gain(taps, n, rows[n][:, i * 128 : (i + 1) * 128])
                gp[0, yy, i // x_size, i % x_size] = taps[...]

    blocks = dict(pre0=pre0, pre1=pre1, pre3=pre3, out=out, mix=mix, n2=n2, d0=d0, d1=d1, bo=bo, bw=bw, ga0=ga0,
                  ga1=ga1, norm=norm, up0=up0, up1=up1, outg=outg, gel=gel, rnn=rnn, gn1o=gn1o, gn1w=gn1w, heads=heads,
                  fin=fin, s0=s0)
    blocks = {name: (1, fn) for name, fn in blocks.items()}
    blocks.update(br=(tiles, branch), ffa=(SEQ // F, ff(0)), ffb=(SEQ // F, ff(1)), gh=(2 * SEQ // F, gh),
                  gno=(half // F, gno), gnw=(half // F, gnw), t=(tiles, back_rows))

    placed = set()

    def event(chunk, k):
        if chunk < CHUNKS:
            u = chunk // 2
            if k == 0 and u in sources and u not in placed:
                placed.add(u)
                place[u].wait()
            ag.event(chunk, k)
        elif chunk < 2 * CHUNKS:
            back.event(chunk - CHUNKS, k, finals)
        elif group == 1:
            if chunk == 2 * CHUNKS:
                small.event(0, k)
                params.event(0, k)
            else:
                back_small.event(0, k, o_gs)
                back_params.event(0, k, o_gp)
                if k == 3:
                    gs_copy.start()
                    gp_copy.start()

    run_plan(PLAN, blocks, event)
    for u in (RNN, GEL):
        for chunk in (2 * u, 2 * u + 1):
            ag.drain(chunk)
    if group == 1:
        gp_copy.wait()
    else:
        gs_copy.start()
    finals.drain()
    gtok_copy.wait()
    gs_copy.wait()
    for cp in (tok_copy, cot_copy, row_copy, rnn_copy, gain_copy):
        cp.wait_send()


def finish_kernel(block_in, gtok_in, gw, gs, gp,
                  o_block, o_gtok, o_mg, o_rnn, o_gel, o_cw, o_cb, o_rw, o_iw, o_rb, o_ib, o_dp, o_out, o_lg, o_gate, o_up,
                  o_down):
    ch = gw.shape[2]
    part, own = o_mg.shape[1], o_cb.shape[1]
    o_block[...] = block_in[...]
    o_gtok[...] = gtok_in[...]
    o_rnn[...] = gw[RNN]
    o_gel[...] = gw[GEL]
    o_out[...] = gw[OUT].T
    for j in range(2):
        cols = slice(j * ch, (j + 1) * ch)
        o_gate[:, cols] = gw[GATE[j]]
        o_up[:, cols] = gw[UP[j]]
        o_down[cols, :] = gw[DOWN[j]].T
    for h in range(ch // 128):
        o_rw[h] = gs[0, 0:16, h * 128 : (h + 1) * 128]
        o_iw[h] = gs[0, 16:32, h * 128 : (h + 1) * 128]
    block = gp[0]
    o_cw[...] = block[0:4, 0:own]
    for k, ref in ((4, o_cb), (5, o_rb), (6, o_ib), (7, o_dp)):
        ref[...] = block[k : k + 1, 0:own]
    turned = pltpu.roll(block, 64, 1)
    lane = lax.broadcasted_iota(jnp.int32, (1, 128), 1)
    for n, ref in ((0, o_mg), (1, o_lg)):
        ref[...] = jnp.where(lane < 64, turned[2 * n : 2 * n + 1], block[2 * n + 1 : 2 * n + 2])[:, 0:part]


def any_spec():
    return pl.BlockSpec(memory_space=pl.ANY)


def vmem_spec():
    return pl.BlockSpec(memory_space=pltpu.VMEM)


def body(sizes, tokens, mix_gain, rnn_weight, gelu_weight, conv_weight, conv_bias, recur_weight, input_weight,
         recur_bias, input_bias, decay_param, out_weight, mlp_gain, gate_weight, up_weight, down_weight, cotangent):
    z_size, x_size, y_size = sizes
    dp = z_size * x_size
    dp_index = lax.axis_index("dp")
    rows, depth = tokens.shape
    part, ch = rnn_weight.shape
    head_rows = recur_weight.shape[1]
    group = max(1, 16 // head_rows)
    wide = y_size * ch
    own = ch // dp
    vectors = [v[None] for v in (conv_bias, recur_bias, input_bias, decay_param, mix_gain, mlp_gain)]
    heads = [recur_weight, input_weight]
    out_w, down_w = out_weight, down_weight
    if part % 128:
        out_w, down_w = out_weight.T, down_weight.T
    shape = jax.ShapeDtypeStruct
    grid = (y_size, z_size, x_size)
    hops = z_size + x_size + y_size - 2
    t = lax.axis_index("tensor")
    joined = [conv_weight] * 3
    if group > 1:
        lanes = jnp.concatenate([conv_weight, *vectors[0:4]], axis=0).astype(F32)
        lanes = jnp.pad(lanes, ((0, 8), (0, ch - own)))
        lanes = jnp.roll(lanes, dp_index * own, axis=1)
        gain = jnp.pad(jnp.concatenate(vectors[4:6], axis=0).astype(F32), ((0, 6), (0, depth - part)))
        gain = lax.psum(jnp.roll(gain, dp_index * part, axis=1), "dp")
        every = jnp.zeros((2 * y_size, 272, ch), F32)
        for n, w in enumerate(heads):
            w = jnp.transpose(w, (1, 0, 2)).reshape(1, head_rows, ch).astype(F32)
            every = lax.dynamic_update_slice(every, w, (t, 128 * n + dp_index * head_rows, 0))
        every = lax.psum(lax.dynamic_update_slice(every, lanes[None], (t, 256, 0)), ("dp", "tensor"))
        mine = [every[2 * yy] * (1 - lax.rem(t, 2)) + every[2 * yy + 1] * lax.rem(t, 2) for yy in range(y_size)]
        joined = [jnp.stack([m[256:] for m in mine]), gain,
                  jnp.concatenate([m[0:256].reshape(2, 128, ch) for m in mine], axis=2).astype(BF)]
        heads = [jnp.zeros((ch // 128, 16, 128), BF)] * 2
    dma = pltpu.SemaphoreType.DMA
    landed = list(big_landing(sizes, part, ch).values())
    landed_params = []
    gs_out, small_grid = (y_size, 272, ch), (1, 1, 1)
    if group == 1:
        landed += list(small_landing(sizes, ch).values())
        landed_params = list(params_landing(sizes).values())
        gs_out, small_grid = (1, SMALL, ch), grid
    block_out, grad_tokens, gw, gs, gp = pl.pallas_call(
        functools.partial(block_kernel, sizes, group),
        out_shape=[shape((rows, depth), BF), shape((rows, depth), F32), shape((UNITS, part, ch), F32), shape(gs_out, F32),
                   shape((1, 8, 128), F32),
                   shape((6, SEQ, wide), BF), shape((SEQ // 128, 128, wide), F32), shape((SEQ // 128, 136, wide), F32),
                   shape((SEQ, wide), BF)],
        in_specs=[*[any_spec()] * 8, *[vmem_spec()] * 7, any_spec(), any_spec(), *([vmem_spec()] * 3 if group > 1 else [any_spec()] * 3)],
        out_specs=[any_spec()] * 9,
        scratch_shapes=[
            pltpu.VMEM((UNITS + 2, *grid, part, ch), BF), pltpu.VMEM((1, *small_grid, SMALL, ch), BF),
            pltpu.VMEM((6, SEQ, wide), BF), pltpu.VMEM((SEQ, wide), BF),
            *[pltpu.VMEM((SEQ, depth), BF)] * 4, pltpu.VMEM((rows, depth), F32),
            pltpu.VMEM((rows, depth), BF), pltpu.VMEM((2, rows, depth), BF),
            pltpu.VMEM((rows, depth), F32), pltpu.VMEM((2, 128, wide), F32), pltpu.VMEM((2, 136, wide), F32),
            pltpu.VMEM((2, max(part // 2, 16), ch), F32),
            pltpu.VMEM((y_size, 16, ch), F32), pltpu.VMEM((16, depth), F32),
            pltpu.VMEM((y_size, 16, ch), F32), pltpu.VMEM((8, depth), F32), pltpu.VMEM((2, 128, wide), BF),
            pltpu.VMEM(out_w.shape, BF), pltpu.VMEM(down_w.shape, BF), pltpu.VMEM(heads[0].shape, BF),
            pltpu.VMEM(heads[1].shape, BF), pltpu.VMEM(gs_out, F32), pltpu.VMEM((1, 8, 128), F32),
            pltpu.VMEM((8, 128), F32), pltpu.VMEM((1, *small_grid, 8, 128), F32),
            dma((CHUNKS, hops)), dma((CHUNKS, hops)), dma((CHUNKS, hops)), dma((CHUNKS, hops)),
            *[dma((1, hops))] * 8, dma((9,)), dma((9,)), dma((20,)), dma((3, 2)), dma((2,)),
            *[pltpu.VMEM(s, BF) for s in landed], *[pltpu.VMEM(s, F32) for s in landed_params],
        ],
        compiler_params=pltpu.CompilerParams(collective_id=0, has_side_effects=True, vmem_limit_bytes=VMEM_LIMIT),
        name="residual_block",
    )(tokens, cotangent, rnn_weight, gelu_weight, out_w, gate_weight, up_weight, down_w, conv_weight, *vectors, *heads,
      *joined)[:5]
    if group > 1:
        every = jnp.zeros((2 * y_size, 272, ch), F32)
        for yy in range(y_size):
            every = lax.dynamic_update_slice(every, gs[yy : yy + 1], (2 * yy + lax.rem(t, 2), 0, 0))
        gs = lax.dynamic_slice(lax.psum(every, ("dp", "tensor")), (t, 0, 0), (1, 272, ch))
        first = dp_index * head_rows
        rec = lax.dynamic_slice(gs[0], (first, 0), (head_rows, ch))
        inp = lax.dynamic_slice(gs[0], (128 + first, 0), (head_rows, ch))
        fill = jnp.zeros((16 - head_rows, ch), F32)
        par = lax.dynamic_slice(gs[0, 256:264], (0, dp_index * own), (8, own))
        gain = lax.dynamic_slice(gs[0, 264:270].reshape(2, 3 * ch), (0, dp_index * part), (2, part))
        gp = jnp.zeros((1, 8, 128), F32).at[0, :, :own].set(par).at[0, 0:4:2, 64 : 64 + part].set(gain)
        gs = jnp.concatenate([rec, fill, inp, fill], axis=0)[None]
    f_shapes = [
        shape((rows, depth), BF), shape((rows, depth), F32), shape((1, part), F32), shape((part, ch), F32),
        shape((part, ch), F32), shape((4, own), F32), shape((1, own), F32), shape((ch // 128, 16, 128), F32),
        shape((ch // 128, 16, 128), F32), shape((1, own), F32), shape((1, own), F32), shape((1, own), F32),
        shape((ch, part), F32), shape((1, part), F32), shape((part, 2 * ch), F32), shape((part, 2 * ch), F32),
        shape((2 * ch, part), F32),
    ]
    res = list(pl.pallas_call(
        finish_kernel,
        out_shape=f_shapes,
        in_specs=[vmem_spec()] * 5,
        out_specs=[vmem_spec()] * 17,
        compiler_params=pltpu.CompilerParams(vmem_limit_bytes=VMEM_LIMIT),
        name="unpack",
    )(block_out, grad_tokens, gw, gs, gp))
    for k in (2, 6, 9, 10, 11, 13):
        res[k] = res[k][0]
    for k in (7, 8):
        res[k] = res[k][:, :head_rows]
    return tuple(res)


def solution(mesh):
    dp, tensor = mesh.shape["dp"], mesh.shape["tensor"]
    x_size = 2
    sizes = (dp // x_size, x_size, tensor // 2)
    rows, split, vec = P(("dp", "tensor"), None), P("dp", "tensor"), P(("tensor", "dp"))
    head, flip, taps = P("tensor", "dp", None), P("tensor", "dp"), P(None, ("tensor", "dp"))
    return jax.shard_map(
        functools.partial(body, sizes),
        mesh=mesh,
        in_specs=(rows, P("dp"), split, split, taps, vec, head, head, vec, vec, vec, flip, P("dp"), split, split, flip,
                  rows),
        out_specs=(rows, rows, P("dp"), split, split, taps, vec, head, head, vec, vec, vec, flip, P("dp"), split, split,
                   flip),
        check_vma=False,
    )
```
